512 devices in a mesh: leaf: 64 (over y, z), cols: 8 (over x, core).
Axes of the slice: x: 4, y: 4, z: 16, core: 2. Of those that a mesh axis runs over, the one named last changes fastest.
Arguments:
- points: float32 [3, 131072], P(None, 'leaf'), may hold values from 0 to 1
- samples: float32 [256, 131072], P('cols', 'leaf'), may hold values from -6 to 6
- sketch: float32 [32, 256], P(None, 'cols'), may hold values from -0.375 to 0.375
- far_requests: int32 [64, 64, 8], P('leaf'), may hold values from 0 to 31, as said below
- far_slots: int32 [2048, 16], P('leaf'), may hold values from 0 to 511, as said below
- far_count: int32 [2048], P('leaf'), may hold values from 1 to 16, as said below
- near_mask: int32 [2048, 3], P('leaf'), may hold values 0 or 1
Outputs:
- far_sample: float32 [256, 131072], P('cols', 'leaf')
- near_sample: float32 [256, 131072], P('cols', 'leaf')
- leaf_basis: float32 [32, 131072], P(None, 'leaf')
- branch_samples: float32 [2048, 256], P('leaf', 'cols')
- top_transfer: float32 [63, 64, 32], replicated
- root_sample: float32 [32, 256], P(None, 'cols')
The draws below stay inside these ranges and needn't reach their ends.
Inputs may be any that keep to these rules, and one draw needn't show every extreme that they name: far_requests[e, d, c] is a leaf counted on device d of leaf (0 for its first); the 8 entries of each [e, d] are distinct. far_slots[i, f] names slot far_slots[i, f] mod 8 of the clusters fetched from device far_slots[i, f] // 8; only entries f < far_count[i] are used; among the 512 entries (used or not) of the leaves of one device, no device is named by more than 8 entries, and some device by exactly 8. `far_count`: used entries of each leaf's far-field list.
All inputs are finite; a program needn't handle non-finite values. No bound on the sum of `near_mask` on one device may be relied on, other than what follows from the above.
Results may differ from the reference program's by a relative error of at most 0.0003.
Values sent between devices are 32-bit elements; how exact they have to be, the bound alone decides.
A program may use at most 64 MiB of HBM per device.

```python
import math
import jax
import jax.numpy as jnp
from jax import lax

LEAF = 64
SAMPLES = 256
RANK = 32
FAR = 16
NS = 1
CAP = 8
LEAVES_DEV = 32
LEAVES = 2048
NPTS = 131072
N_LEAF = 64


def draw_far_requests(key, part):
    key = jax.random.fold_in(key, 11)
    scores = jax.random.randint(key, (N_LEAF, N_LEAF, LEAVES_DEV), 0, 1 << 18)
    scores = scores * LEAVES_DEV + jnp.arange(LEAVES_DEV, dtype=jnp.int32)
    unused, chosen = jax.lax.top_k(scores, CAP)
    return chosen.astype(jnp.int32)


def draw_far_slots(key, part):
    key = jax.random.fold_in(key, 37)
    order_key, slot_key = jax.random.split(key, 2)
    scores = jax.random.randint(order_key, (N_LEAF, N_LEAF), 0, 1 << 18)
    scores = scores * N_LEAF + jnp.arange(N_LEAF, dtype=jnp.int32)[None, :]
    orders = jnp.argsort(scores, axis=1, stable=True).astype(jnp.int32)
    entry_ids = jnp.arange(LEAVES_DEV * FAR, dtype=jnp.int32) % N_LEAF
    owners = jnp.take(orders, entry_ids, axis=1)
    slot_ids = jax.random.randint(slot_key, (N_LEAF, LEAVES_DEV * FAR), 0, CAP)
    return (owners * CAP + slot_ids).reshape(LEAVES, FAR).astype(jnp.int32)


def draw_far_count(key, part):
    key = jax.random.fold_in(key, 23)
    first_key, second_key, third_key, fourth_key = jax.random.split(key, 4)
    levels = jax.random.randint(first_key, (N_LEAF,), 1, 5)
    busiest = jax.random.randint(second_key, (), 0, N_LEAF)
    levels = jnp.where(jnp.arange(N_LEAF, dtype=jnp.int32) == busiest, 4, levels)
    highest_count = jnp.maximum(1, FAR * levels // 4)
    leaf_highest = jnp.repeat(highest_count, LEAVES_DEV)
    chosen_leaf = jnp.repeat(jax.random.randint(third_key, (N_LEAF,), 0, LEAVES_DEV), LEAVES_DEV)
    local_ids = jnp.arange(LEAVES, dtype=jnp.int32) % LEAVES_DEV
    counts = 1 + jax.random.randint(fourth_key, (LEAVES,), 0, 1 << 20) % leaf_highest
    return jnp.where(local_ids == chosen_leaf, leaf_highest, counts).astype(jnp.int32)


def plant(array, key, low, high):
    longest = array.shape.index(max(array.shape))
    spots = []
    for shift in (0, 1):
        where = [jax.random.randint(jax.random.fold_in(key, axis), (), 0, length) for axis, length in enumerate(array.shape)]
        where[longest] = (where[longest] + shift) % array.shape[longest]
        spots.append(tuple(where))
    return array.at[spots[0]].set(low).at[spots[1]].set(high)


def steps_of(rng, dims, pieces, least, top_value):
    def one(axis_at, parts):
        steps = jax.random.uniform(jax.random.fold_in(jax.random.fold_in(rng, 6), axis_at), (parts,), jnp.float32, least / len(pieces), top_value / len(pieces))
        return jnp.repeat(jnp.exp(steps), dims[axis_at] // parts).reshape((-1,) + (1,) * (len(dims) - axis_at - 1))

    factor_of = one(*pieces[0])
    for cut in pieces[1:]:
        factor_of = factor_of * one(*cut)
    return factor_of


def noise(key, dims, spread, bound, shards=(), kind=jnp.bfloat16):
    loudness = steps_of(key, dims, shards, -0.22, 0.18) if shards else 1.0
    result = jax.random.normal(key, dims, jnp.float32) * spread * loudness
    return jnp.minimum(jnp.maximum(result, -bound), bound).astype(kind)


def setup_inputs(seed: int = 0) -> dict:
    splits = jax.random.split(jax.random.key(seed), 8)
    return {
        "points": jnp.clip(1.0 * jax.random.uniform(splits[0], (3, NPTS), jnp.float32) ** steps_of(splits[0], (3, NPTS), ((1, 64),), -0.2, 0.2), 0.0, 1.0),
        "samples": noise(splits[1], (SAMPLES, NPTS), 1.0, 6.0, ((0, 8), (1, 64)), jnp.float32),
        "sketch": noise(splits[2], (RANK, SAMPLES), SAMPLES ** -0.5, 0.375, ((1, 8),), jnp.float32),
        "far_requests": draw_far_requests(jax.random.fold_in(splits[7], 71), 0),
        "far_slots": draw_far_slots(jax.random.fold_in(splits[7], 71), 0),
        "far_count": draw_far_count(jax.random.fold_in(splits[7], 71), 0),
        "near_mask": plant((jax.random.randint(splits[6], (LEAVES, 2 * NS + 1), 0, 4) < 3).astype(jnp.int32), jax.random.fold_in(splits[6], 1), 0, 1),
    }


length_scale = 0.3
shift_share = 0.05
highest = lax.Precision.HIGHEST

def kernel_block(source_coords, target_coords):
    differences = source_coords[:, :, :, None] - target_coords[:, :, None, :]
    return jnp.exp(-jnp.sqrt(lax.optimization_barrier(jnp.sum(differences * differences, axis=1))) / length_scale)

def compress(sample_block, sketch):
    sketched = jnp.einsum('nms,rs->nmr', sample_block, sketch, precision=highest)
    gram_matrix = jnp.einsum('nmr,nmq->nrq', sketched, sketched, precision=highest)
    order_size = gram_matrix.shape[-1]
    trace_sum = jnp.trace(gram_matrix, axis1=1, axis2=2)
    shifted = gram_matrix + (shift_share * trace_sum / order_size + 1e-06)[:, None, None] * jnp.eye(order_size, dtype=jnp.float32)
    lower_factor = jnp.linalg.cholesky(shifted)
    basis_t = jax.scipy.linalg.solve_triangular(lower_factor, jnp.swapaxes(sketched, 1, 2), lower=True)
    projected = jnp.einsum('nrm,nms->nrs', basis_t, sample_block, precision=highest)
    return (basis_t, projected)

def reference(points, samples, sketch, far_requests, far_slots, far_count, near_mask):
    coords = jnp.transpose(points.reshape(3, LEAVES, LEAF), (1, 0, 2))
    sample_blocks = jnp.transpose(samples.reshape(SAMPLES, LEAVES, LEAF), (1, 0, 2))
    leaf_ids = jnp.arange(LEAVES, dtype=jnp.int32)
    device_ids = leaf_ids // LEAVES_DEV
    owners = far_slots // CAP
    positions = far_slots % CAP
    sources = (owners * LEAVES_DEV + far_requests[device_ids[:, None], owners, positions]).astype(jnp.int32)
    valid_mask = (jnp.arange(FAR, dtype=jnp.int32)[None, :] < far_count[:, None]).astype(jnp.float32)
    near_weights = near_mask.astype(jnp.float32)
    pad_coords = jnp.pad(coords, ((NS, NS), (0, 0), (0, 0)))
    pad_samples = jnp.pad(sample_blocks, ((NS, NS), (0, 0), (0, 0)))
    block_size = math.gcd(LEAVES, 256)
    block_count = LEAVES // block_size

    def one_block(inputs):
        target, source_ids, weights, first_ids, near_block = inputs
        start = jnp.zeros((block_size, SAMPLES, LEAF), jnp.float32)

        def far_step(accumulated, step_inputs):
            picked, scale = step_inputs
            kernel_vals = kernel_block(coords[picked], target) * scale[:, None, None]
            term = jnp.einsum('bsp,bpq->bsq', sample_blocks[picked], kernel_vals, precision=highest)
            return (accumulated + term, None)
        far_part, _ = lax.scan(far_step, start, (source_ids.T, weights.T))
        near_part = start
        for offset in range(2 * NS + 1):
            picked = first_ids + offset
            kernel_vals = kernel_block(pad_coords[picked], target) * near_block[:, offset][:, None, None]
            near_part = near_part + jnp.einsum('bsp,bpq->bsq', pad_samples[picked], kernel_vals, precision=highest)
        return (far_part, near_part)
    far_all, near_all = lax.map(one_block, (coords.reshape(block_count, block_size, 3, LEAF), sources.reshape(block_count, block_size, FAR), valid_mask.reshape(block_count, block_size, FAR), leaf_ids.reshape(block_count, block_size), near_weights.reshape(block_count, block_size, 2 * NS + 1)))
    far_all = far_all.reshape(LEAVES, SAMPLES, LEAF)
    near_all = near_all.reshape(LEAVES, SAMPLES, LEAF)
    far_sample = jnp.transpose(far_all, (1, 0, 2)).reshape(SAMPLES, NPTS)
    near_sample = jnp.transpose(near_all, (1, 0, 2)).reshape(SAMPLES, NPTS)
    sample_rows = jnp.transpose(far_all, (0, 2, 1))
    basis_t, current = compress(sample_rows, sketch)
    leaf_basis = jnp.transpose(basis_t, (1, 0, 2)).reshape(RANK, NPTS)
    while current.shape[0] > N_LEAF:
        unused, current = compress(current.reshape(current.shape[0] // 2, 2 * RANK, SAMPLES), sketch)
    branch_samples = current.reshape(N_LEAF * RANK, SAMPLES)
    transfers = []
    while current.shape[0] > 1:
        transfer_t, current = compress(current.reshape(current.shape[0] // 2, 2 * RANK, SAMPLES), sketch)
        transfers.append(jnp.swapaxes(transfer_t, 1, 2))
    top_transfer = jnp.concatenate(transfers, axis=0)
    root_sample = current[0]
    return (far_sample, near_sample, leaf_basis, branch_samples, top_transfer, root_sample)
```

```python
import functools

import jax
import jax.numpy as jnp
from jax import lax
from jax.experimental import pallas as pl
from jax.experimental.pallas import tpu as pltpu
from jax.sharding import PartitionSpec as P

LEAF = 64
FAR = 16
CAP = 8
RANK = 32
NEAR = 3
ROWS_Y = 4
CELL = 16
HALF = 16
SUB = HALF * CELL + HALF * 2
MSG = CAP * CELL + CAP * 2
NODE = 24

length_scale = 0.3
shift_share = 0.05
highest = lax.Precision.HIGHEST
MESH = pl.DeviceIdType.MESH
VMEM = pltpu.VMEM
whole = pl.BlockSpec(memory_space=pltpu.VMEM)
scalars = pl.BlockSpec(memory_space=pltpu.SMEM)
MIB = 1 << 20


def lanes(shape):
    return lax.broadcasted_iota(jnp.int32, shape, len(shape) - 1)


def swap_halves(tile):
    return pltpu.roll(tile, 64, 1)


def dot_nt(a, b, precision=highest):
    return lax.dot_general(
        a, b, (((1,), (1,)), ((), ())), precision=precision, preferred_element_type=jnp.float32
    )


def dot_nn(a, b, precision=highest):
    return lax.dot_general(
        a, b, (((1,), (0,)), ((), ())), precision=precision, preferred_element_type=jnp.float32
    )


def greet(axis, peers):
    barrier = pltpu.get_barrier_semaphore()
    for peer in peers:
        pl.semaphore_signal(barrier, inc=1, device_id={axis: peer}, device_id_type=MESH)
    pl.semaphore_wait(barrier, len(peers))


def fetch_body(
    n_leaf, samples, coords, own_requests, sent_requests, recv, local, halo, *scratch
):
    n_y = ROWS_Y
    n_z = n_leaf // n_y
    chunks = (local,) + scratch[: n_z - 1]
    stage, edge, asked_v, asked, ring_send, ring_recv, y_send, y_recv, q_send, q_recv, q_local, e_send, e_recv = scratch[n_z - 1 :]
    me = lax.axis_index("leaf")
    y, z = me // n_z, me % n_z
    up = y * n_z + (z + 1) % n_z
    down = y * n_z + (z + n_z - 1) % n_z
    above, below = (me + 1) % n_leaf, (me + n_leaf - 1) % n_leaf
    across = [None] + [((y + k) % n_y) * n_z + z for k in range(1, n_y)]
    greet("leaf", [up, down, above, below] + across[1:])

    def remote(src, dst, send, recv_sem, peer):
        return pltpu.make_async_remote_copy(
            src_ref=src, dst_ref=dst, send_sem=send, recv_sem=recv_sem,
            device_id={"leaf": peer}, device_id_type=MESH,
        )

    sent = []
    asks = []
    for k in range(1, n_y):
        copy = remote(
            sent_requests.at[(y + k) % n_y], asked_v.at[n_y - k - 1], q_send.at[k - 1], q_recv.at[n_y - k - 1], across[k]
        )
        copy.start()
        asks.append(copy)
    sent += asks

    low = lanes((CELL, 2 * LEAF)) < LEAF
    for j in range(HALF):
        top = samples[0:CELL, 2 * LEAF * j : 2 * LEAF * (j + 1)]
        bottom = samples[CELL : 2 * CELL, 2 * LEAF * j : 2 * LEAF * (j + 1)]
        base = (2 * j // HALF) * SUB + (2 * j % HALF) * CELL
        local[base : base + CELL, :] = jnp.where(low, top, swap_halves(bottom))
        local[base + CELL : base + 2 * CELL, :] = jnp.where(low, swap_halves(top), bottom)
    for h in range(2):
        local[h * SUB + HALF * CELL : (h + 1) * SUB, :] = coords[2 * HALF * h : 2 * HALF * (h + 1), :]

    hops = {(0, 0): n_z // 2, (0, 1): n_z // 2 - 1, (1, 0): n_z // 2 - 1, (1, 1): n_z // 2}

    def ring(way, part, step):
        here, there = (step, step + 1) if way == 0 else ((n_z - step) % n_z, n_z - step - 1)
        rows = pl.ds(part * SUB, SUB)
        return remote(
            chunks[here].at[rows], chunks[there].at[rows], ring_send.at[way, part, step],
            ring_recv.at[way, part, step], up if way == 0 else down,
        )

    def forward(way, part, step):
        if step < hops[way, part]:
            copy = ring(way, part, step)
            copy.start()
            sent.append(copy)

    order = ((0, 0), (1, 1), (0, 1), (1, 0))
    for way, part in order:
        forward(way, part, 0)

    for side, cluster in ((0, 0), (1, 2 * HALF - 1)):
        base = (cluster // HALF) * SUB + (cluster % HALF) * CELL
        cbase = (cluster // HALF) * SUB + HALF * CELL + (cluster % HALF) * 2
        edge[side, 0:CELL, :] = local[base : base + CELL, :]
        edge[side, CELL : CELL + 2, :] = local[cbase : cbase + 2, :]
        edge[side, CELL + 2 : NODE, :] = jnp.zeros((NODE - CELL - 2, 2 * LEAF), jnp.float32)
    edges = [
        remote(edge.at[0], halo.at[1], e_send.at[0], e_recv.at[1], below),
        remote(edge.at[1], halo.at[0], e_send.at[1], e_recv.at[0], above),
    ]
    for copy in edges:
        copy.start()
    sent += edges

    for copy in asks:
        copy.wait_recv()
    move = pltpu.make_async_copy(asked_v, asked, q_local)
    move.start()
    move.wait()

    def pick(chunk, target, request):
        def one(c, carry):
            cell, row = request(c)
            target[pl.ds(pl.multiple_of(c * CELL, CELL), CELL), :] = chunk[pl.ds(cell * CELL, CELL), :]
            for part in range(2):
                target[pl.ds(CAP * CELL + c * 2 + part, 1), :] = chunk[pl.ds(row + part, 1), :]
            return carry

        lax.fori_loop(0, CAP, one, 0)

    arriving = []

    def select(slot):
        chunk = chunks[slot]
        source_z = (z + n_z - slot) % n_z
        for k in range(1, n_y):
            pick(chunk, stage.at[k - 1, slot], lambda c: (asked[k - 1, 0, source_z * CAP + c], asked[k - 1, 1, source_z * CAP + c]))
            copy = remote(
                stage.at[k - 1, slot], recv.at[k * n_z + slot], y_send.at[k - 1, slot], y_recv.at[k - 1, slot], across[k]
            )
            copy.start()
            sent.append(copy)
            arriving.append(copy)
        pick(chunk, recv.at[slot], lambda c: (own_requests[0, y * n_z + source_z, c], own_requests[1, y * n_z + source_z, c]))

    select(0)
    for step in range(1, n_z // 2 + 1):
        for way, part in order:
            if step - 1 < hops[way, part]:
                ring(way, part, step - 1).wait_recv()
                forward(way, part, step)
        select(step)
        if step < n_z // 2:
            select(n_z - step)
    for copy in arriving + edges:
        copy.wait_recv()
    for copy in sent:
        copy.wait_send()


def fetch(samples, coords, requests, n_leaf):
    n_z = n_leaf // ROWS_Y
    rows = samples.shape[0]
    half, cell = requests // HALF, requests % HALF
    places = jnp.stack([half * (SUB // CELL) + cell, half * SUB + HALF * CELL + cell * 2])
    sent_requests = jnp.swapaxes(places.reshape(2, ROWS_Y, n_z * CAP), 0, 1)
    sent_requests = jnp.pad(sent_requests, ((0, 0), (0, 6), (0, 0)))
    dma = pltpu.SemaphoreType.DMA
    f32 = jnp.float32
    return pl.pallas_call(
        functools.partial(fetch_body, n_leaf),
        out_shape=(
            jax.ShapeDtypeStruct((n_leaf, MSG, 2 * LEAF), f32),
            jax.ShapeDtypeStruct((2 * SUB, 2 * LEAF), f32),
            jax.ShapeDtypeStruct((2, NODE, 2 * LEAF), f32),
        ),
        in_specs=[whole, whole, scalars, whole],
        out_specs=(whole, whole, whole),
        scratch_shapes=[VMEM((2 * SUB, 2 * LEAF), f32)] * (n_z - 1)
        + [
            VMEM((ROWS_Y - 1, n_z, MSG, 2 * LEAF), f32),
            VMEM((2, NODE, 2 * LEAF), f32),
            VMEM((ROWS_Y - 1, 8, n_z * CAP), jnp.int32),
            pltpu.SMEM((ROWS_Y - 1, 8, n_z * CAP), jnp.int32),
            dma((2, 2, n_z // 2)),
            dma((2, 2, n_z // 2)),
            dma((ROWS_Y - 1, n_z)),
            dma((ROWS_Y - 1, n_z)),
            dma((ROWS_Y - 1,)),
            dma((ROWS_Y - 1,)),
            dma,
            dma((2,)),
            dma((2,)),
        ],
        compiler_params=pltpu.CompilerParams(
            collective_id=1, has_side_effects=True, vmem_limit_bytes=40 * MIB
        ),
        name="fetch",
    )(samples, coords, places, sent_requests)


def sample_body(
    leaves, recv, local, halo, target, slots, counts, near, sketch, far_out, near_out, partial_out, cells
):
    low16 = lanes((CELL, 2 * LEAF)) < LEAF
    low1 = lanes((1, 2 * LEAF)) < LEAF
    low32 = lanes((2 * CELL, 2 * LEAF)) < LEAF
    for c in range(leaves):
        base = (c // HALF) * SUB + (c % HALF) * CELL
        cbase = (c // HALF) * SUB + HALF * CELL + (c % HALF) * 2
        cells[c + 1, 0:CELL, :] = local[base : base + CELL, :]
        cells[c + 1, CELL : CELL + 2, :] = local[cbase : cbase + 2, :]
    cells[0] = halo[0]
    cells[leaves + 1] = halo[1]

    def halves(value):
        high = value.astype(jnp.bfloat16)
        return high, (value - high.astype(jnp.float32)).astype(jnp.bfloat16)

    def pair(coordinates, first, second):
        (block_a, row_a, last_a, scale_a), (block_b, row_b, last_b, scale_b) = first, second
        x = jnp.where(low1, row_a, swap_halves(row_b))
        yy = jnp.where(low1, swap_halves(row_a), row_b)
        zz = jnp.where(low1, last_a, last_b)
        dx = coordinates[0] - x
        dy = coordinates[1] - yy
        dz = coordinates[2] - zz
        values = jnp.exp(jnp.sqrt(dx * dx + dy * dy + dz * dz) * (-1.0 / length_scale))
        block_a = block_a * scale_a
        block_b = block_b * scale_b
        rows = jnp.concatenate(
            [jnp.where(low16, block_a, swap_halves(block_b)), jnp.where(low16, swap_halves(block_a), block_b)], axis=0
        )
        return halves(values), halves(rows)

    def four(coordinates, entries):
        (k0h, k0l), (s0h, s0l) = pair(coordinates, entries[0], entries[1])
        (k1h, k1l), (s1h, s1l) = pair(coordinates, entries[2], entries[3])
        left = jnp.concatenate(
            [jnp.concatenate([s0h, s1h], axis=1), jnp.concatenate([s0l, s1l], axis=1)], axis=0
        )
        right = jnp.concatenate(
            [jnp.concatenate([k0h, k1h], axis=1), jnp.concatenate([k0l, k1l], axis=1)], axis=0
        )
        return dot_nt(left, right, None)

    def far_entry(leaf, f, count):
        slot = slots[leaf, f]
        message = slot // CAP
        c = slot - message * CAP
        scale = jnp.where(f < count, 1.0, 0.0).astype(jnp.float32)
        return (
            recv[message, pl.ds(pl.multiple_of(c * CELL, CELL), CELL), :],
            recv[message, pl.ds(CAP * CELL + 2 * c, 1), :],
            recv[message, pl.ds(CAP * CELL + 2 * c + 1, 1), :],
            scale,
        )

    def near_entry(leaf, offset):
        at = leaf + offset
        scale = near[leaf * NEAR + offset].astype(jnp.float32) if offset < NEAR else jnp.float32(0)
        at = at if offset < NEAR else leaf
        return cells[at, 0:CELL, :], cells[at, CELL : CELL + 1, :], cells[at, CELL + 1 : CELL + 2, :], scale

    def fold(total):
        total = total[: 2 * CELL] + total[2 * CELL :]
        return total + swap_halves(total)

    def one_leaf(leaf):
        block = target[pl.ds(pl.multiple_of(leaf * LEAF, LEAF), LEAF), :]
        coordinates = [jnp.broadcast_to(block[:, a : a + 1], (LEAF, 2 * LEAF)) for a in range(3)]
        count = counts[leaf]

        def step(g, total):
            return total + four(coordinates, [far_entry(leaf, 4 * g + b, count) for b in range(4)])

        far = lax.fori_loop(0, (count + 3) // 4, step, jnp.zeros((2 * LEAF // 2, 2 * LEAF), jnp.float32))
        close = four(coordinates, [near_entry(leaf, o) for o in range(4)])
        return fold(far), fold(close)

    def two_leaves(j, carry):
        far_a, near_a = one_leaf(2 * j)
        far_b, near_b = one_leaf(2 * j + 1)
        far = jnp.where(low32, far_a, far_b)
        at = pl.ds(pl.multiple_of(j * 2 * LEAF, 2 * LEAF), 2 * LEAF)
        far_out[:, at] = far
        near_out[:, at] = jnp.where(low32, near_a, near_b)
        partial_out[:, at] = dot_nn(sketch[...], far)
        return carry

    lax.fori_loop(0, leaves // 2, two_leaves, 0)


def sample(recv, local, halo, target, slots, counts, near, sketch):
    leaves = counts.shape[0]
    shape = jax.ShapeDtypeStruct((RANK, leaves * LEAF), jnp.float32)
    return pl.pallas_call(
        functools.partial(sample_body, leaves),
        out_shape=(shape, shape, shape),
        in_specs=[whole, whole, whole, whole, scalars, scalars, scalars, whole],
        out_specs=(whole, whole, whole),
        scratch_shapes=[VMEM((leaves + 2, NODE, 2 * LEAF), jnp.float32)],
        compiler_params=pltpu.CompilerParams(vmem_limit_bytes=40 * MIB),
        name="sample",
    )(recv, local, halo, target, slots, counts, near, sketch)


def total_body(n, partial, out, parts, send_a, recv_a, send_b, recv_b):
    me = lax.axis_index("cols")
    width = partial.shape[1] // n
    peers = [(me + k) % n for k in range(1, n)]
    greet("cols", peers)

    def piece(owner):
        return pl.ds(pl.multiple_of(owner * width, width), width)

    first = []
    for k in range(1, n):
        copy = pltpu.make_async_remote_copy(
            src_ref=partial.at[:, piece(peers[k - 1])], dst_ref=parts.at[k - 1], send_sem=send_a.at[k - 1],
            recv_sem=recv_a.at[k - 1], device_id={"cols": peers[k - 1]}, device_id_type=MESH,
        )
        copy.start()
        first.append(copy)
    value = partial[:, piece(me)]
    for k in range(1, n):
        first[k - 1].wait_recv()
        value = value + parts[k - 1]
    out[:, piece(me)] = value
    second = []
    for k in range(1, n):
        copy = pltpu.make_async_remote_copy(
            src_ref=out.at[:, piece(me)], dst_ref=out.at[:, piece(me)], send_sem=send_b.at[k - 1],
            recv_sem=recv_b.at[k - 1], device_id={"cols": peers[k - 1]}, device_id_type=MESH,
        )
        copy.start()
        second.append(copy)
    for k in range(1, n):
        owner = (me + n - k) % n
        pltpu.make_async_remote_copy(
            src_ref=out.at[:, piece(owner)], dst_ref=out.at[:, piece(owner)], send_sem=send_b.at[k - 1],
            recv_sem=recv_b.at[k - 1], device_id={"cols": peers[k - 1]}, device_id_type=MESH,
        ).wait_recv()
    for copy in first + second:
        copy.wait_send()


def total(partial, n):
    rows, columns = partial.shape
    dma = pltpu.SemaphoreType.DMA
    return pl.pallas_call(
        functools.partial(total_body, n),
        out_shape=jax.ShapeDtypeStruct(partial.shape, jnp.float32),
        in_specs=[whole],
        out_specs=whole,
        scratch_shapes=[VMEM((n - 1, rows, columns // n), jnp.float32)] + [dma((n - 1,))] * 4,
        compiler_params=pltpu.CompilerParams(collective_id=2, has_side_effects=True),
        name="total",
    )(partial)


def eye(shape, first=0):
    rows = lax.broadcasted_iota(jnp.int32, shape, 0)
    return jnp.where(lanes(shape) == rows + first, 1.0, 0.0).astype(jnp.float32)


def compress(sketched_t):
    unit = eye((2 * RANK, 2 * RANK))
    shape = (RANK, 4 * RANK)
    on_diagonal = lanes(shape) == lax.broadcasted_iota(jnp.int32, shape, 0)
    tiles = []
    for b in sketched_t:
        tile = dot_nt(b, jnp.concatenate([b, b, unit], axis=0))
        diagonal = jnp.where(on_diagonal, tile, 0.0)
        trace = jnp.sum(jnp.sum(diagonal, axis=1, keepdims=True), axis=0, keepdims=True)
        tile = tile + jnp.where(on_diagonal, shift_share * trace / RANK + 1e-06, 0.0)
        tiles.append([tile[8 * g : 8 * g + 8] for g in range(4)])
    sub = lax.broadcasted_iota(jnp.int32, (8, 4 * RANK), 0)
    for k in range(RANK):
        g, s = k // 8, k % 8
        for tile in tiles:
            row = tile[g][s : s + 1, :]
            scaled = row * (1.0 / row[:, k : k + 1])
            for h in range(g, 4):
                column = tile[h][:, k : k + 1]
                if h == g:
                    if s == 7:
                        continue
                    tile[h] = tile[h] - jnp.where(sub > s, column, 0.0) * scaled
                else:
                    tile[h] = tile[h] - column * scaled
    done = []
    for tile in tiles:
        tile = jnp.concatenate(tile, axis=0)
        diagonal = jnp.sum(jnp.where(on_diagonal, tile, 0.0), axis=1, keepdims=True)
        done.append(tile * lax.rsqrt(diagonal))
    return done


def level(read, write, count, group):
    def some(start):
        inputs = [read(start + b) for b in range(min(group, count))]
        tiles = compress([b for b, _ in inputs])
        for b, (tile, (_, stacked)) in enumerate(zip(tiles, inputs)):
            padded = jnp.concatenate([jnp.zeros((2 * RANK, stacked.shape[1]), jnp.float32), stacked], axis=0)
            write(start + b, tile, dot_nn(tile, padded))

    if count <= group:
        some(0)
    else:
        lax.fori_loop(0, count // group, lambda g, carry: (some(g * group), carry)[1], 0)


def branch_body(leaves, sketched, far, basis, branch, packed, nodes, projected):
    low = lanes((RANK, 2 * LEAF)) < LEAF
    group = 8

    def some(g, carry):
        bs, rows = [], []
        for j in range(group // 2):
            at = pl.ds(pl.multiple_of((g * (group // 2) + j) * 2 * LEAF, 2 * LEAF), 2 * LEAF)
            b, row = sketched[:, at], far[:, at]
            bs += [b[:, :LEAF], swap_halves(b)[:, :LEAF]]
            rows += [jnp.where(low, 0.0, swap_halves(row)), jnp.where(low, 0.0, row)]
        tiles = compress(bs)
        for b, (tile, row) in enumerate(zip(tiles, rows)):
            nodes[g * group + b] = tile
            projected[g * group + b] = dot_nt(tile, row)
        for j in range(group // 2):
            at = pl.ds(pl.multiple_of((g * (group // 2) + j) * 2 * LEAF, 2 * LEAF), 2 * LEAF)
            basis[:, at] = jnp.where(low, swap_halves(tiles[2 * j]), tiles[2 * j + 1])
        return carry

    lax.fori_loop(0, leaves // group, some, 0)

    middle = eye((RANK, 4 * RANK), RANK)

    def read(node):
        pair = nodes[pl.ds(2 * node, 2)].reshape(2 * RANK, 4 * RANK)
        return dot_nt(middle, pair), projected[pl.ds(2 * node, 2)].reshape(2 * RANK, RANK)

    def write(node, tile, value):
        nodes[node] = tile
        projected[node] = value

    count = leaves // 2
    while count >= 1:
        level(read, write, count, 8)
        count //= 2
    branch[...] = projected[0]
    quarter = lanes((8, 4 * RANK)) // RANK
    wide = dot_nn(projected[0], eye((RANK, 4 * RANK)))
    tile = nodes[0]
    for i, (source, shift) in enumerate(((tile, RANK), (wide, 0))):
        row = jnp.zeros((8, 4 * RANK), jnp.float32)
        for g in range(4):
            turned = pltpu.roll(source[8 * g : 8 * g + 8], (RANK * g - shift) % (4 * RANK), 1)
            row = jnp.where(quarter == g, turned, row)
        packed[8 * i : 8 * i + 8] = row


def branch(sketched, far):
    leaves = sketched.shape[1] // LEAF
    f32 = jnp.float32
    return pl.pallas_call(
        functools.partial(branch_body, leaves),
        out_shape=(
            jax.ShapeDtypeStruct(sketched.shape, f32),
            jax.ShapeDtypeStruct((RANK, RANK), f32),
            jax.ShapeDtypeStruct((CELL, 4 * RANK), f32),
        ),
        in_specs=[whole, whole],
        out_specs=(whole, whole, whole),
        scratch_shapes=[VMEM((leaves, RANK, 4 * RANK), f32), VMEM((leaves, RANK, RANK), f32)],
        compiler_params=pltpu.CompilerParams(vmem_limit_bytes=40 * MIB),
        name="branch",
    )(sketched, far)


def gather_body(n_leaf, packed, out, y_send, y_recv, ring_send, ring_recv, own_sem):
    n_y = ROWS_Y
    n_z = n_leaf // n_y
    me = lax.axis_index("leaf")
    y, z = me // n_z, me % n_z
    up = y * n_z + (z + 1) % n_z
    down = y * n_z + (z + n_z - 1) % n_z
    across = [((y + k) % n_y) * n_z + z for k in range(1, n_y)]
    greet("leaf", [up, down] + across)
    sent = []
    for k in range(1, n_y):
        copy = pltpu.make_async_remote_copy(
            src_ref=packed, dst_ref=out.at[z, y], send_sem=y_send.at[k - 1], recv_sem=y_recv.at[k - 1],
            device_id={"leaf": across[k - 1]}, device_id_type=MESH,
        )
        copy.start()
        sent.append(copy)
    own = pltpu.make_async_copy(packed, out.at[z, y], own_sem)
    own.start()
    own.wait()
    for k in range(1, n_y):
        other = (y + n_y - k) % n_y
        pltpu.make_async_remote_copy(
            src_ref=packed, dst_ref=out.at[z, other], send_sem=y_send.at[k - 1], recv_sem=y_recv.at[k - 1],
            device_id={"leaf": across[k - 1]}, device_id_type=MESH,
        ).wait_recv()

    def hop(way, step, slot):
        return pltpu.make_async_remote_copy(
            src_ref=out.at[slot], dst_ref=out.at[slot], send_sem=ring_send.at[way, step],
            recv_sem=ring_recv.at[way, step], device_id={"leaf": up if way == 0 else down}, device_id_type=MESH,
        )

    hops = (n_z // 2, n_z // 2 - 1)
    for step in range(n_z // 2 + 1):
        for way in range(2):
            slot = (z + n_z - step) % n_z if way == 0 else (z + step) % n_z
            if 1 <= step <= hops[way]:
                hop(way, step - 1, slot).wait_recv()
            if step < hops[way]:
                copy = hop(way, step, slot)
                copy.start()
                sent.append(copy)
    for copy in sent:
        copy.wait_send()


def gather(packed, n_leaf):
    n_z = n_leaf // ROWS_Y
    dma = pltpu.SemaphoreType.DMA
    return pl.pallas_call(
        functools.partial(gather_body, n_leaf),
        out_shape=jax.ShapeDtypeStruct((n_z, ROWS_Y) + packed.shape, jnp.float32),
        in_specs=[whole],
        out_specs=whole,
        scratch_shapes=[
            dma((ROWS_Y - 1,)), dma((ROWS_Y - 1,)), dma((2, n_z // 2)), dma((2, n_z // 2)), dma,
        ],
        compiler_params=pltpu.CompilerParams(collective_id=3, has_side_effects=True),
        name="gather",
    )(packed)


def top_body(n_leaf, gathered, transfers, root, nodes, projected):
    n_z = n_leaf // ROWS_Y
    quarters = [eye((RANK, 4 * RANK), 0)]
    right = eye((2 * RANK, 4 * RANK), 2 * RANK)
    count = n_leaf // 2

    def unpack(block):
        return jnp.concatenate([pltpu.roll(block, (4 * RANK - RANK * g) % (4 * RANK), 1) for g in range(4)], axis=0)

    def read_first(node):
        pairs = []
        for part in range(2):
            a = gathered[(2 * node) % n_z, (2 * node) // n_z, 8 * part : 8 * part + 8, :]
            b = gathered[(2 * node + 1) % n_z, (2 * node + 1) // n_z, 8 * part : 8 * part + 8, :]
            pairs.append(jnp.concatenate([unpack(a), unpack(b)], axis=0))
        return dot_nt(quarters[0], pairs[0]), pairs[1]

    middle = eye((RANK, 4 * RANK), RANK)

    def read(node):
        pair = nodes[pl.ds(2 * node, 2)].reshape(2 * RANK, 4 * RANK)
        return dot_nt(middle, pair), projected[pl.ds(2 * node, 2)].reshape(2 * RANK, 4 * RANK)

    first = 0
    reader = read_first
    while count >= 1:

        def write(node, tile, value, first=first):
            nodes[node] = tile
            projected[node] = value
            transfers[first + node] = dot_nt(right, tile)

        level(reader, write, count, 8)
        reader = read
        first += count
        count //= 2
    root[...] = projected[0][:, :RANK]


def top(gathered, n_leaf):
    f32 = jnp.float32
    return pl.pallas_call(
        functools.partial(top_body, n_leaf),
        out_shape=(
            jax.ShapeDtypeStruct((n_leaf - 1, 2 * RANK, RANK), f32),
            jax.ShapeDtypeStruct((RANK, RANK), f32),
        ),
        in_specs=[whole],
        out_specs=(whole, whole),
        scratch_shapes=[VMEM((n_leaf // 2, RANK, 4 * RANK), f32), VMEM((n_leaf // 2, RANK, 4 * RANK), f32)],
        compiler_params=pltpu.CompilerParams(vmem_limit_bytes=40 * MIB),
        name="top",
    )(gathered)


def on_device(n_leaf, n_cols, points, samples, sketch, far_requests, far_slots, far_count, near_mask):
    n_z = n_leaf // ROWS_Y
    leaves = far_count.shape[0]
    me = lax.axis_index("leaf")
    y, z = me // n_z, me % n_z
    coords = points.reshape(3, leaves, LEAF)
    packed_coords = jnp.stack(
        [jnp.concatenate([coords[0], coords[1]], axis=1), jnp.concatenate([coords[2], coords[2]], axis=1)], axis=1
    ).reshape(2 * leaves, 2 * LEAF)
    target = jnp.pad(points.T, ((0, 0), (0, 5)))
    owner = far_slots // CAP
    slots = (((y - owner // n_z) % ROWS_Y) * n_z + (z - owner % n_z) % n_z) * CAP + far_slots % CAP
    places = me * leaves + jnp.arange(leaves)[:, None] + jnp.arange(NEAR)[None, :] - NEAR // 2
    inside = (places >= 0) & (places < n_leaf * leaves)
    near = jnp.where(inside, near_mask, 0).reshape(-1)

    recv, local, halo = fetch(samples, packed_coords, far_requests[0], n_leaf)
    far_sample, near_sample, partial = sample(recv, local, halo, target, slots, far_count, near, sketch)
    sketched = total(partial, n_cols)
    leaf_basis, branch_samples, packed = branch(sketched, far_sample)
    gathered = gather(packed, n_leaf)
    top_transfer, root_sample = top(gathered, n_leaf)
    return far_sample, near_sample, leaf_basis, branch_samples, top_transfer, root_sample


def solution(mesh):
    return jax.shard_map(
        functools.partial(on_device, mesh.shape["leaf"], mesh.shape["cols"]),
        mesh=mesh,
        in_specs=(
            P(None, "leaf"),
            P("cols", "leaf"),
            P(None, "cols"),
            P("leaf", None, None),
            P("leaf", None),
            P("leaf"),
            P("leaf", None),
        ),
        out_specs=(
            P("cols", "leaf"),
            P("cols", "leaf"),
            P(None, "leaf"),
            P("leaf", "cols"),
            P(),
            P(None, "cols"),
        ),
        check_vma=False,
    )
```

```python
import functools

import jax
import jax.numpy as jnp
from jax import lax
from jax.experimental import pallas as pl
from jax.experimental.pallas import tpu as pltpu
from jax.sharding import PartitionSpec as P

LEAF = 64
FAR = 16
CAP = 8
RANK = 32
NEAR = 3
ROWS_Y = 4
CELL = 16
HALF = 16
SUB = HALF * CELL + HALF * 2
MSG = CAP * CELL + CAP * 2
NODE = 24

length_scale = 0.3
shift_share = 0.05
highest = lax.Precision.HIGHEST
MESH = pl.DeviceIdType.MESH
VMEM = pltpu.VMEM
whole = pl.BlockSpec(memory_space=pltpu.VMEM)
scalars = pl.BlockSpec(memory_space=pltpu.SMEM)
MIB = 1 << 20


def lanes(shape):
    return lax.broadcasted_iota(jnp.int32, shape, len(shape) - 1)


def swap_halves(tile):
    return pltpu.roll(tile, 64, 1)


def dot_nt(a, b, precision=highest):
    return lax.dot_general(
        a, b, (((1,), (1,)), ((), ())), precision=precision, preferred_element_type=jnp.float32
    )


def dot_nn(a, b, precision=highest):
    return lax.dot_general(
        a, b, (((1,), (0,)), ((), ())), precision=precision, preferred_element_type=jnp.float32
    )


def greet(axis, peers):
    barrier = pltpu.get_barrier_semaphore()
    for peer in peers:
        pl.semaphore_signal(barrier, inc=1, device_id={axis: peer}, device_id_type=MESH)
    pl.semaphore_wait(barrier, len(peers))


def fetch_body(
    n_leaf, samples, coords, own_requests, sent_requests, recv, local, halo, *scratch
):
    n_y = ROWS_Y
    n_z = n_leaf // n_y
    chunks = (local,) + scratch[: n_z - 1]
    stage, edge, asked_v, asked, ring_send, ring_recv, y_send, y_recv, q_send, q_recv, q_local, e_send, e_recv = scratch[n_z - 1 :]
    me = lax.axis_index("leaf")
    y, z = me // n_z, me % n_z
    up = y * n_z + (z + 1) % n_z
    down = y * n_z + (z + n_z - 1) % n_z
    above, below = (me + 1) % n_leaf, (me + n_leaf - 1) % n_leaf
    across = [None] + [((y + k) % n_y) * n_z + z for k in range(1, n_y)]
    greet("leaf", [up, down, above, below] + across[1:])

    def remote(src, dst, send, recv_sem, peer):
        return pltpu.make_async_remote_copy(
            src_ref=src, dst_ref=dst, send_sem=send, recv_sem=recv_sem,
            device_id={"leaf": peer}, device_id_type=MESH,
        )

    sent = []
    asks = []
    for k in range(1, n_y):
        copy = remote(
            sent_requests.at[(y + k) % n_y], asked_v.at[n_y - k - 1], q_send.at[k - 1], q_recv.at[n_y - k - 1], across[k]
        )
        copy.start()
        asks.append(copy)
    sent += asks

    low = lanes((CELL, 2 * LEAF)) < LEAF
    for j in range(HALF):
        top = samples[0:CELL, 2 * LEAF * j : 2 * LEAF * (j + 1)]
        bottom = samples[CELL : 2 * CELL, 2 * LEAF * j : 2 * LEAF * (j + 1)]
        base = (2 * j // HALF) * SUB + (2 * j % HALF) * CELL
        local[base : base + CELL, :] = jnp.where(low, top, swap_halves(bottom))
        local[base + CELL : base + 2 * CELL, :] = jnp.where(low, swap_halves(top), bottom)
    for h in range(2):
        local[h * SUB + HALF * CELL : (h + 1) * SUB, :] = coords[2 * HALF * h : 2 * HALF * (h + 1), :]

    hops = {(0, 0): n_z // 2, (0, 1): n_z // 2 - 1, (1, 0): n_z // 2 - 1, (1, 1): n_z // 2}

    def ring(way, part, step):
        here, there = (step, step + 1) if way == 0 else ((n_z - step) % n_z, n_z - step - 1)
        rows = pl.ds(part * SUB, SUB)
        return remote(
            chunks[here].at[rows], chunks[there].at[rows], ring_send.at[way, part, step],
            ring_recv.at[way, part, step], up if way == 0 else down,
        )

    def forward(way, part, step):
        if step < hops[way, part]:
            copy = ring(way, part, step)
            copy.start()
            sent.append(copy)

    order = ((0, 0), (1, 1), (0, 1), (1, 0))
    for way, part in order:
        forward(way, part, 0)

    for side, cluster in ((0, 0), (1, 2 * HALF - 1)):
        base = (cluster // HALF) * SUB + (cluster % HALF) * CELL
        cbase = (cluster // HALF) * SUB + HALF * CELL + (cluster % HALF) * 2
        edge[side, 0:CELL, :] = local[base : base + CELL, :]
        edge[side, CELL : CELL + 2, :] = local[cbase : cbase + 2, :]
        edge[side, CELL + 2 : NODE, :] = jnp.zeros((NODE - CELL - 2, 2 * LEAF), jnp.float32)
    edges = [
        remote(edge.at[0], halo.at[1], e_send.at[0], e_recv.at[1], below),
        remote(edge.at[1], halo.at[0], e_send.at[1], e_recv.at[0], above),
    ]
    for copy in edges:
        copy.start()
    sent += edges

    for copy in asks:
        copy.wait_recv()
    move = pltpu.make_async_copy(asked_v, asked, q_local)
    move.start()
    move.wait()

    def pick(chunk, target, request):
        def one(c, carry):
            cell, row = request(c)
            target[pl.ds(pl.multiple_of(c * CELL, CELL), CELL), :] = chunk[pl.ds(cell * CELL, CELL), :]
            for part in range(2):
                target[pl.ds(CAP * CELL + c * 2 + part, 1), :] = chunk[pl.ds(row + part, 1), :]
            return carry

        lax.fori_loop(0, CAP, one, 0)

    arriving = []

    def select(slot):
        chunk = chunks[slot]
        source_z = (z + n_z - slot) % n_z
        for k in range(1, n_y):
            pick(chunk, stage.at[k - 1, slot], lambda c: (asked[k - 1, 0, source_z * CAP + c], asked[k - 1, 1, source_z * CAP + c]))
            copy = remote(
                stage.at[k - 1, slot], recv.at[k * n_z + slot], y_send.at[k - 1, slot], y_recv.at[k - 1, slot], across[k]
            )
            copy.start()
            sent.append(copy)
            arriving.append(copy)
        pick(chunk, recv.at[slot], lambda c: (own_requests[0, y * n_z + source_z, c], own_requests[1, y * n_z + source_z, c]))

    select(0)
    for step in range(1, n_z // 2 + 1):
        for way, part in order:
            if step - 1 < hops[way, part]:
                ring(way, part, step - 1).wait_recv()
                forward(way, part, step)
        select(step)
        if step < n_z // 2:
            select(n_z - step)
    for copy in arriving + edges:
        copy.wait_recv()
    for copy in sent:
        copy.wait_send()


def fetch(samples, coords, requests, n_leaf):
    n_z = n_leaf // ROWS_Y
    rows = samples.shape[0]
    half, cell = requests // HALF, requests % HALF
    places = jnp.stack([half * (SUB // CELL) + cell, half * SUB + HALF * CELL + cell * 2])
    sent_requests = jnp.swapaxes(places.reshape(2, ROWS_Y, n_z * CAP), 0, 1)
    sent_requests = jnp.pad(sent_requests, ((0, 0), (0, 6), (0, 0)))
    dma = pltpu.SemaphoreType.DMA
    f32 = jnp.float32
    return pl.pallas_call(
        functools.partial(fetch_body, n_leaf),
        out_shape=(
            jax.ShapeDtypeStruct((n_leaf, MSG, 2 * LEAF), f32),
            jax.ShapeDtypeStruct((2 * SUB, 2 * LEAF), f32),
            jax.ShapeDtypeStruct((2, NODE, 2 * LEAF), f32),
        ),
        in_specs=[whole, whole, scalars, whole],
        out_specs=(whole, whole, whole),
        scratch_shapes=[VMEM((2 * SUB, 2 * LEAF), f32)] * (n_z - 1)
        + [
            VMEM((ROWS_Y - 1, n_z, MSG, 2 * LEAF), f32),
            VMEM((2, NODE, 2 * LEAF), f32),
            VMEM((ROWS_Y - 1, 8, n_z * CAP), jnp.int32),
            pltpu.SMEM((ROWS_Y - 1, 8, n_z * CAP), jnp.int32),
            dma((2, 2, n_z // 2)),
            dma((2, 2, n_z // 2)),
            dma((ROWS_Y - 1, n_z)),
            dma((ROWS_Y - 1, n_z)),
            dma((ROWS_Y - 1,)),
            dma((ROWS_Y - 1,)),
            dma,
            dma((2,)),
            dma((2,)),
        ],
        compiler_params=pltpu.CompilerParams(
            collective_id=1, has_side_effects=True, vmem_limit_bytes=40 * MIB
        ),
        name="fetch",
    )(samples, coords, places, sent_requests)


def sample_body(
    leaves, recv, local, halo, target, slots, counts, near, sketch, far_out, near_out, partial_out, cells
):
    low16 = lanes((CELL, 2 * LEAF)) < LEAF
    low1 = lanes((1, 2 * LEAF)) < LEAF
    low32 = lanes((2 * CELL, 2 * LEAF)) < LEAF
    for c in range(leaves):
        base = (c // HALF) * SUB + (c % HALF) * CELL
        cbase = (c // HALF) * SUB + HALF * CELL + (c % HALF) * 2
        cells[c + 1, 0:CELL, :] = local[base : base + CELL, :]
        cells[c + 1, CELL : CELL + 2, :] = local[cbase : cbase + 2, :]
    cells[0] = halo[0]
    cells[leaves + 1] = halo[1]

    def halves(value):
        high = value.astype(jnp.bfloat16)
        return high, (value - high.astype(jnp.float32)).astype(jnp.bfloat16)

    def pair(coordinates, first, second):
        (block_a, row_a, last_a, scale_a), (block_b, row_b, last_b, scale_b) = first, second
        x = jnp.where(low1, row_a, swap_halves(row_b))
        yy = jnp.where(low1, swap_halves(row_a), row_b)
        zz = jnp.where(low1, last_a, last_b)
        dx = coordinates[0] - x
        dy = coordinates[1] - yy
        dz = coordinates[2] - zz
        square = dx * dx + dy * dy + dz * dz
        values = jnp.exp2(square * lax.rsqrt(jnp.maximum(square, 1e-30)) * (-1.4426950408889634 / length_scale))
        block_a = block_a * scale_a
        block_b = block_b * scale_b
        rows = jnp.concatenate(
            [jnp.where(low16, block_a, swap_halves(block_b)), jnp.where(low16, swap_halves(block_a), block_b)], axis=0
        )
        return halves(values), halves(rows)

    def four(coordinates, entries):
        (k0h, k0l), (s0h, s0l) = pair(coordinates, entries[0], entries[1])
        (k1h, k1l), (s1h, s1l) = pair(coordinates, entries[2], entries[3])
        left = jnp.concatenate(
            [jnp.concatenate([s0h, s1h], axis=1), jnp.concatenate([s0l, s1l], axis=1)], axis=0
        )
        right = jnp.concatenate(
            [jnp.concatenate([k0h, k1h], axis=1), jnp.concatenate([k0l, k1l], axis=1)], axis=0
        )
        return left, right

    def far_entry(leaf, f, count):
        slot = slots[leaf, f]
        message = slot // CAP
        c = slot - message * CAP
        scale = jnp.where(f < count, 1.0, 0.0).astype(jnp.float32)
        return (
            recv[message, pl.ds(pl.multiple_of(c * CELL, CELL), CELL), :],
            recv[message, pl.ds(CAP * CELL + 2 * c, 1), :],
            recv[message, pl.ds(CAP * CELL + 2 * c + 1, 1), :],
            scale,
        )

    def near_entry(leaf, offset):
        at = leaf + offset
        scale = near[leaf * NEAR + offset].astype(jnp.float32) if offset < NEAR else jnp.float32(0)
        at = at if offset < NEAR else leaf
        return cells[at, 0:CELL, :], cells[at, CELL : CELL + 1, :], cells[at, CELL + 1 : CELL + 2, :], scale

    def fold(total):
        total = total[: 2 * CELL] + total[2 * CELL :]
        return total + swap_halves(total)

    def two_leaves(j, carry):
        pair_of = (2 * j, 2 * j + 1)
        coordinates = []
        for leaf in pair_of:
            block = target[pl.ds(pl.multiple_of(leaf * LEAF, LEAF), LEAF), :]
            coordinates.append([jnp.broadcast_to(block[:, a : a + 1], (LEAF, 2 * LEAF)) for a in range(3)])
        count = [counts[leaf] for leaf in pair_of]

        def operands(g):
            return [
                four(coordinates[i], [far_entry(pair_of[i], 4 * g + b, count[i]) for b in range(4)]) for i in range(2)
            ]

        def step(g, carried):
            totals, waiting = carried
            totals = [total + dot_nt(left, right, None) for total, (left, right) in zip(totals, waiting)]
            return totals, operands(g)

        zero = jnp.zeros((LEAF, 2 * LEAF), jnp.float32)
        steps = (jnp.maximum(count[0], count[1]) + 3) // 4
        totals, waiting = lax.fori_loop(1, steps, step, ([zero, zero], operands(0)))
        far = [total + dot_nt(left, right, None) for total, (left, right) in zip(totals, waiting)]
        close = [four(coordinates[i], [near_entry(pair_of[i], o) for o in range(4)]) for i in range(2)]
        close = [dot_nt(left, right, None) for left, right in close]
        far = jnp.where(low32, fold(far[0]), fold(far[1]))
        at = pl.ds(pl.multiple_of(j * 2 * LEAF, 2 * LEAF), 2 * LEAF)
        far_out[:, at] = far
        near_out[:, at] = jnp.where(low32, fold(close[0]), fold(close[1]))
        partial_out[:, at] = dot_nn(sketch[...], far)
        return carry

    lax.fori_loop(0, leaves // 2, two_leaves, 0)


def sample(recv, local, halo, target, slots, counts, near, sketch):
    leaves = counts.shape[0]
    shape = jax.ShapeDtypeStruct((RANK, leaves * LEAF), jnp.float32)
    return pl.pallas_call(
        functools.partial(sample_body, leaves),
        out_shape=(shape, shape, shape),
        in_specs=[whole, whole, whole, whole, scalars, scalars, scalars, whole],
        out_specs=(whole, whole, whole),
        scratch_shapes=[VMEM((leaves + 2, NODE, 2 * LEAF), jnp.float32)],
        compiler_params=pltpu.CompilerParams(vmem_limit_bytes=40 * MIB),
        name="sample",
    )(recv, local, halo, target, slots, counts, near, sketch)


def total_body(n, partial, out, parts, send_a, recv_a, send_b, recv_b):
    me = lax.axis_index("cols")
    width = partial.shape[1] // n
    peers = [(me + k) % n for k in range(1, n)]
    greet("cols", peers)

    def piece(owner):
        return pl.ds(pl.multiple_of(owner * width, width), width)

    first = []
    for k in range(1, n):
        copy = pltpu.make_async_remote_copy(
            src_ref=partial.at[:, piece(peers[k - 1])], dst_ref=parts.at[k - 1], send_sem=send_a.at[k - 1],
            recv_sem=recv_a.at[k - 1], device_id={"cols": peers[k - 1]}, device_id_type=MESH,
        )
        copy.start()
        first.append(copy)
    value = partial[:, piece(me)]
    for k in range(1, n):
        first[k - 1].wait_recv()
        value = value + parts[k - 1]
    out[:, piece(me)] = value
    second = []
    for k in range(1, n):
        copy = pltpu.make_async_remote_copy(
            src_ref=out.at[:, piece(me)], dst_ref=out.at[:, piece(me)], send_sem=send_b.at[k - 1],
            recv_sem=recv_b.at[k - 1], device_id={"cols": peers[k - 1]}, device_id_type=MESH,
        )
        copy.start()
        second.append(copy)
    for k in range(1, n):
        owner = (me + n - k) % n
        pltpu.make_async_remote_copy(
            src_ref=out.at[:, piece(owner)], dst_ref=out.at[:, piece(owner)], send_sem=send_b.at[k - 1],
            recv_sem=recv_b.at[k - 1], device_id={"cols": peers[k - 1]}, device_id_type=MESH,
        ).wait_recv()
    for copy in first + second:
        copy.wait_send()


def total(partial, n):
    rows, columns = partial.shape
    dma = pltpu.SemaphoreType.DMA
    return pl.pallas_call(
        functools.partial(total_body, n),
        out_shape=jax.ShapeDtypeStruct(partial.shape, jnp.float32),
        in_specs=[whole],
        out_specs=whole,
        scratch_shapes=[VMEM((n - 1, rows, columns // n), jnp.float32)] + [dma((n - 1,))] * 4,
        compiler_params=pltpu.CompilerParams(collective_id=2, has_side_effects=True),
        name="total",
    )(partial)


def eye(shape, first=0):
    rows = lax.broadcasted_iota(jnp.int32, shape, 0)
    return jnp.where(lanes(shape) == rows + first, 1.0, 0.0).astype(jnp.float32)


def inverse(value):
    guess = pl.reciprocal(value, approx=True)
    guess = guess * (2.0 - value * guess)
    return guess * (2.0 - value * guess)


def compress(tiles, traces):
    block = 4 if len(tiles) > 8 else 8
    shape = (RANK, 4 * RANK)
    on_diagonal = lanes(shape) == lax.broadcasted_iota(jnp.int32, shape, 0)
    tiles = [
        tile + jnp.where(on_diagonal, shift_share * trace / RANK + 1e-06, 0.0) for tile, trace in zip(tiles, traces)
    ]
    tiles = [[tile[8 * g : 8 * g + 8] for g in range(4)] for tile in tiles]
    full = (8, 4 * RANK)
    sub = lax.broadcasted_iota(jnp.int32, full, 0)
    scales = [[jnp.zeros(full, jnp.float32) for g in range(4)] for tile in tiles]
    for first in range(0, RANK, block):
        g = first // 8
        columns = [
            [[jnp.broadcast_to(part[:, first + t : first + t + 1], full) for t in range(block)] for part in tile[g:]]
            for tile in tiles
        ]
        for t in range(block):
            s = (first + t) % 8
            for tile, column, scale in zip(tiles, columns, scales):
                pivot = jnp.broadcast_to(column[0][t][s : s + 1], full)
                inv = inverse(pivot)
                scale[g] = jnp.where(sub == s, lax.rsqrt(pivot), scale[g])
                row = jnp.broadcast_to(tile[g][s : s + 1], full) * inv
                right = [None] * block
                for u in range(t + 1, block):
                    right[u] = jnp.broadcast_to(column[0][u][s : s + 1], full) * inv
                for h in range(g, 4):
                    c = column[h - g][t]
                    if h == g:
                        if s == 7:
                            continue
                        c = jnp.where(sub > s, c, 0.0)
                    tile[h] = tile[h] - c * row
                    for u in range(t + 1, block):
                        column[h - g][u] = column[h - g][u] - c * right[u]
    return [
        jnp.concatenate([part * factor for part, factor in zip(tile, scale)], axis=0)
        for tile, scale in zip(tiles, scales)
    ]


def halves(value):
    high = value.astype(jnp.bfloat16)
    return high, (value - high.astype(jnp.float32)).astype(jnp.bfloat16)


def total_of(value):
    return jnp.sum(jnp.sum(value, axis=0, keepdims=True), axis=1, keepdims=True)


def parent_tile(stacked):
    lane = lanes(stacked.shape)
    c = jnp.where(lane < RANK, stacked, 0.0)
    right = jnp.where(lane < 2 * RANK, c + pltpu.roll(c, RANK, 1), eye(stacked.shape, 2 * RANK))
    tile = lax.dot_general(
        c[:, :RANK], right, (((0,), (0,)), ((), ())), precision=highest, preferred_element_type=jnp.float32
    )
    return tile, total_of(c * c)


def project(tile, stacked):
    low = lanes(tile.shape) < 2 * RANK
    high, rest = halves(tile)
    s_high, s_rest = halves(stacked)
    high = high.astype(jnp.float32)
    first = jnp.where(low, swap_halves(rest.astype(jnp.float32)), high)
    left = jnp.concatenate([first, swap_halves(high)], axis=1)[:, : 6 * RANK].astype(jnp.bfloat16)
    return dot_nn(left, jnp.concatenate([s_high, s_high, s_rest], axis=0), None)


def level(read, write, count, group):
    def some(start):
        inputs = [read(start + b) for b in range(min(group, count))]
        pairs = [parent_tile(c) for c, _ in inputs]
        tiles = compress([tile for tile, _ in pairs], [trace for _, trace in pairs])
        for b, (tile, (_, stacked)) in enumerate(zip(tiles, inputs)):
            write(start + b, tile, project(tile, stacked))

    if count <= group:
        some(0)
    else:
        lax.fori_loop(0, count // group, lambda g, carry: (some(g * group), carry)[1], 0)


def branch_body(leaves, sketched, far, basis, branch, packed_c, packed_p, nodes, projected):
    low = lanes((RANK, 2 * LEAF)) < LEAF
    unit = eye((2 * RANK, 2 * RANK))
    group = 16

    def project_t(tile, row):
        high, rest = [part.astype(jnp.float32) for part in halves(tile)]
        r_high, r_rest = [part.astype(jnp.float32) for part in halves(row)]
        left = [jnp.where(low, swap_halves(rest), high), jnp.where(low, 0.0, high)]
        right = [jnp.where(low, swap_halves(r_high), r_high), r_rest]
        return dot_nt(
            jnp.concatenate(left, axis=1).astype(jnp.bfloat16), jnp.concatenate(right, axis=1).astype(jnp.bfloat16), None
        )

    def some(g, carry):
        bs, rows = [], []
        for j in range(group // 2):
            at = pl.ds(pl.multiple_of((g * (group // 2) + j) * 2 * LEAF, 2 * LEAF), 2 * LEAF)
            b, row = sketched[:, at], far[:, at]
            bs += [b[:, :LEAF], swap_halves(b)[:, :LEAF]]
            rows += [swap_halves(row), row]
        tiles = compress([dot_nt(b, jnp.concatenate([b, b, unit], axis=0)) for b in bs], [total_of(b * b) for b in bs])
        for b, (tile, row) in enumerate(zip(tiles, rows)):
            nodes[g * group + b] = tile
            projected[g * group + b] = project_t(tile, row)
        for j in range(group // 2):
            at = pl.ds(pl.multiple_of((g * (group // 2) + j) * 2 * LEAF, 2 * LEAF), 2 * LEAF)
            basis[:, at] = jnp.where(low, swap_halves(tiles[2 * j]), tiles[2 * j + 1])
        return carry

    lax.fori_loop(0, leaves // group, some, 0)

    def read(node):
        pair = nodes[pl.ds(2 * node, 2)].reshape(2 * RANK, 4 * RANK)
        return pltpu.roll(pair, 3 * RANK, 1), projected[pl.ds(2 * node, 2)].reshape(2 * RANK, RANK)

    def write(node, tile, value):
        nodes[node] = tile
        projected[node] = value

    count = leaves // 2
    while count >= 1:
        level(read, write, count, 16)
        count //= 2
    branch[...] = projected[0]
    quarter = lanes((8, 4 * RANK)) // RANK
    wide = dot_nn(projected[0], eye((RANK, 4 * RANK)))
    tile = nodes[0]
    for i, (source, shift) in enumerate(((tile, RANK), (wide, 0))):
        row = jnp.zeros((8, 4 * RANK), jnp.float32)
        for g in range(4):
            turned = pltpu.roll(source[8 * g : 8 * g + 8], (RANK * g - shift) % (4 * RANK), 1)
            row = jnp.where(quarter == g, turned, row)
        if i == 0:
            for g in range(8):
                packed_c[g] = row[g : g + 1]
        else:
            packed_p[...] = row


def branch(sketched, far):
    leaves = sketched.shape[1] // LEAF
    f32 = jnp.float32
    return pl.pallas_call(
        functools.partial(branch_body, leaves),
        out_shape=(
            jax.ShapeDtypeStruct(sketched.shape, f32),
            jax.ShapeDtypeStruct((RANK, RANK), f32),
            jax.ShapeDtypeStruct((8, 1, 4 * RANK), f32),
            jax.ShapeDtypeStruct((8, 4 * RANK), f32),
        ),
        in_specs=[whole, whole],
        out_specs=(whole, whole, whole, whole),
        scratch_shapes=[VMEM((leaves, RANK, 4 * RANK), f32), VMEM((leaves, RANK, RANK), f32)],
        compiler_params=pltpu.CompilerParams(vmem_limit_bytes=40 * MIB),
        name="branch",
    )(sketched, far)


def gather_body(n_leaf, n_cols, packed_c, packed_p, out_c, out_p, *sems):
    yc_send, yc_recv, yp_send, yp_recv, zc_send, zc_recv, zp_send, zp_recv, x_send, x_recv, own = sems
    n_y = ROWS_Y
    n_z = n_leaf // n_y
    me, col = lax.axis_index("leaf"), lax.axis_index("cols")
    y, z = me // n_z, me % n_z
    across = [((y + k) % n_y) * n_z + z for k in range(1, n_y)]
    along = [y * n_z + (z + k) % n_z for k in range(1, n_z)]
    others = [(col + k) % n_cols for k in range(1, n_cols)]
    barrier = pltpu.get_barrier_semaphore()
    for peer in across + along:
        pl.semaphore_signal(barrier, inc=1, device_id={"leaf": peer}, device_id_type=MESH)
    for peer in others:
        pl.semaphore_signal(barrier, inc=1, device_id={"cols": peer}, device_id_type=MESH)
    pl.semaphore_wait(barrier, len(across) + len(along) + len(others))
    sent = []

    def push(src, dst, send, recv, axis, peer):
        copy = pltpu.make_async_remote_copy(
            src_ref=src, dst_ref=dst, send_sem=send, recv_sem=recv, device_id={axis: peer}, device_id_type=MESH
        )
        copy.start()
        sent.append(copy)

    def arrived(ref, send, recv, axis, peer):
        pltpu.make_async_remote_copy(
            src_ref=ref, dst_ref=ref, send_sem=send, recv_sem=recv, device_id={axis: peer}, device_id_type=MESH
        ).wait_recv()

    for k in range(n_y - 1):
        push(packed_c.at[col], out_c.at[col, z, y], yc_send.at[k], yc_recv.at[k], "leaf", across[k])
    for k in range(n_y - 1):
        push(packed_p, out_p.at[z, y], yp_send.at[k], yp_recv.at[k], "leaf", across[k])
    mine = [
        pltpu.make_async_copy(packed_c.at[col], out_c.at[col, z, y], own.at[0]),
        pltpu.make_async_copy(packed_p, out_p.at[z, y], own.at[1]),
    ]
    for copy in mine:
        copy.start()
    for copy in mine:
        copy.wait()
    far_first = sorted(range(n_z - 1), key=lambda k: -min(k + 1, n_z - 1 - k))
    for k in range(n_y - 1):
        arrived(out_c.at[col, z, (y + n_y - k - 1) % n_y], yc_send.at[k], yc_recv.at[k], "leaf", across[k])
    for k in far_first:
        push(out_c.at[col, z], out_c.at[col, z], zc_send.at[k], zc_recv.at[k], "leaf", along[k])
    for k in range(n_y - 1):
        arrived(out_p.at[z, (y + n_y - k - 1) % n_y], yp_send.at[k], yp_recv.at[k], "leaf", across[k])
    for k in far_first:
        push(out_p.at[z], out_p.at[z], zp_send.at[k], zp_recv.at[k], "leaf", along[k])
    for k in range(n_z - 1):
        arrived(out_c.at[col, (z + n_z - k - 1) % n_z], zc_send.at[k], zc_recv.at[k], "leaf", along[k])
    for k in range(n_cols - 1):
        push(out_c.at[col], out_c.at[col], x_send.at[k], x_recv.at[k], "cols", others[k])
    for k in range(n_cols - 1):
        arrived(out_c.at[(col + n_cols - k - 1) % n_cols], x_send.at[k], x_recv.at[k], "cols", others[k])
    for k in range(n_z - 1):
        arrived(out_p.at[(z + n_z - k - 1) % n_z], zp_send.at[k], zp_recv.at[k], "leaf", along[k])
    for copy in sent:
        copy.wait_send()


def gather(packed_c, packed_p, n_leaf, n_cols):
    n_z = n_leaf // ROWS_Y
    dma = pltpu.SemaphoreType.DMA
    f32 = jnp.float32
    return pl.pallas_call(
        functools.partial(gather_body, n_leaf, n_cols),
        out_shape=(
            jax.ShapeDtypeStruct((8, n_z, ROWS_Y, 1, 4 * RANK), f32),
            jax.ShapeDtypeStruct((n_z, ROWS_Y, 8, 4 * RANK), f32),
        ),
        in_specs=[whole, whole],
        out_specs=(whole, whole),
        scratch_shapes=[dma((ROWS_Y - 1,))] * 4
        + [dma((n_z - 1,))] * 4
        + [dma((n_cols - 1,))] * 2
        + [dma((2,))],
        compiler_params=pltpu.CompilerParams(collective_id=3, has_side_effects=True),
        name="gather",
    )(packed_c, packed_p)


def top_body(n_leaf, gathered_c, gathered_p, transfers, root, nodes, projected):
    n_z = n_leaf // ROWS_Y
    count = n_leaf // 2

    def unpack(block):
        return jnp.concatenate([pltpu.roll(block, (4 * RANK - RANK * g) % (4 * RANK), 1) for g in range(4)], axis=0)

    def read_first(node):
        parts = []
        for child in (2 * node, 2 * node + 1):
            z, y = child % n_z, child // n_z
            rows = jnp.concatenate([gathered_c[i, z, y] for i in range(8)], axis=0)
            parts.append((unpack(rows), unpack(gathered_p[z, y])))
        return [jnp.concatenate(pair, axis=0) for pair in zip(*parts)]

    def read(node):
        pair = nodes[pl.ds(2 * node, 2)].reshape(2 * RANK, 4 * RANK)
        return pltpu.roll(pair, 3 * RANK, 1), projected[pl.ds(2 * node, 2)].reshape(2 * RANK, 4 * RANK)

    first = 0
    reader = read_first
    while count >= 1:

        def write(node, tile, value, first=first):
            nodes[node] = tile
            projected[node] = value
            transfers[first + node] = tile.T[2 * RANK :, :]

        level(reader, write, count, 16)
        reader = read
        first += count
        count //= 2
    root[...] = projected[0][:, :RANK]


def top(gathered_c, gathered_p, n_leaf):
    f32 = jnp.float32
    return pl.pallas_call(
        functools.partial(top_body, n_leaf),
        out_shape=(
            jax.ShapeDtypeStruct((n_leaf - 1, 2 * RANK, RANK), f32),
            jax.ShapeDtypeStruct((RANK, RANK), f32),
        ),
        in_specs=[whole, whole],
        out_specs=(whole, whole),
        scratch_shapes=[VMEM((n_leaf // 2, RANK, 4 * RANK), f32), VMEM((n_leaf // 2, RANK, 4 * RANK), f32)],
        compiler_params=pltpu.CompilerParams(vmem_limit_bytes=40 * MIB),
        name="top",
    )(gathered_c, gathered_p)


def on_device(n_leaf, n_cols, points, samples, sketch, far_requests, far_slots, far_count, near_mask):
    n_z = n_leaf // ROWS_Y
    leaves = far_count.shape[0]
    me = lax.axis_index("leaf")
    y, z = me // n_z, me % n_z
    coords = points.reshape(3, leaves, LEAF)
    packed_coords = jnp.stack(
        [jnp.concatenate([coords[0], coords[1]], axis=1), jnp.concatenate([coords[2], coords[2]], axis=1)], axis=1
    ).reshape(2 * leaves, 2 * LEAF)
    target = jnp.pad(points.T, ((0, 0), (0, 5)))
    owner = far_slots // CAP
    slots = (((y - owner // n_z) % ROWS_Y) * n_z + (z - owner % n_z) % n_z) * CAP + far_slots % CAP
    places = me * leaves + jnp.arange(leaves)[:, None] + jnp.arange(NEAR)[None, :] - NEAR // 2
    inside = (places >= 0) & (places < n_leaf * leaves)
    near = jnp.where(inside, near_mask, 0).reshape(-1)

    recv, local, halo = fetch(samples, packed_coords, far_requests[0], n_leaf)
    far_sample, near_sample, partial = sample(recv, local, halo, target, slots, far_count, near, sketch)
    sketched = total(partial, n_cols)
    leaf_basis, branch_samples, packed_c, packed_p = branch(sketched, far_sample)
    gathered_c, gathered_p = gather(packed_c, packed_p, n_leaf, n_cols)
    top_transfer, root_sample = top(gathered_c, gathered_p, n_leaf)
    return far_sample, near_sample, leaf_basis, branch_samples, top_transfer, root_sample


def solution(mesh):
    return jax.shard_map(
        functools.partial(on_device, mesh.shape["leaf"], mesh.shape["cols"]),
        mesh=mesh,
        in_specs=(
            P(None, "leaf"),
            P("cols", "leaf"),
            P(None, "cols"),
            P("leaf", None, None),
            P("leaf", None),
            P("leaf"),
            P("leaf", None),
        ),
        out_specs=(
            P("cols", "leaf"),
            P("cols", "leaf"),
            P(None, "leaf"),
            P("leaf", "cols"),
            P(),
            P(None, "cols"),
        ),
        check_vma=False,
    )
```

```python
import functools

import jax
import jax.numpy as jnp
from jax import lax
from jax.experimental import pallas as pl
from jax.experimental.pallas import tpu as pltpu
from jax.sharding import PartitionSpec as P

LEAF = 64
FAR = 16
CAP = 8
RANK = 32
NEAR = 3
ROWS_Y = 4
CELL = 16
HALF = 16
SUB = HALF * CELL + HALF * 2
MSG = CAP * CELL + CAP * 2
NODE = 24

length_scale = 0.3
shift_share = 0.05
highest = lax.Precision.HIGHEST
MESH = pl.DeviceIdType.MESH
VMEM = pltpu.VMEM
whole = pl.BlockSpec(memory_space=pltpu.VMEM)
scalars = pl.BlockSpec(memory_space=pltpu.SMEM)
MIB = 1 << 20


def lanes(shape):
    return lax.broadcasted_iota(jnp.int32, shape, len(shape) - 1)


def swap_halves(tile):
    return pltpu.roll(tile, 64, 1)


def dot_nt(a, b, precision=highest):
    return lax.dot_general(
        a, b, (((1,), (1,)), ((), ())), precision=precision, preferred_element_type=jnp.float32
    )


def dot_nn(a, b, precision=highest):
    return lax.dot_general(
        a, b, (((1,), (0,)), ((), ())), precision=precision, preferred_element_type=jnp.float32
    )


def greet(axis, peers):
    barrier = pltpu.get_barrier_semaphore()
    for peer in peers:
        pl.semaphore_signal(barrier, inc=1, device_id={axis: peer}, device_id_type=MESH)
    pl.semaphore_wait(barrier, len(peers))


def fetch_body(
    n_leaf, samples, points, sent_requests, recv, local, halo, *scratch
):
    n_y = ROWS_Y
    n_z = n_leaf // n_y
    chunks = (local,) + scratch[: n_z - 1]
    stage, edge, asked_v, asked, ring_send, ring_recv, y_send, y_recv, q_send, q_recv, q_local, e_send, e_recv = scratch[n_z - 1 :]
    me = lax.axis_index("leaf")
    y, z = me // n_z, me % n_z
    up = y * n_z + (z + 1) % n_z
    down = y * n_z + (z + n_z - 1) % n_z
    above, below = (me + 1) % n_leaf, (me + n_leaf - 1) % n_leaf
    across = [None] + [((y + k) % n_y) * n_z + z for k in range(1, n_y)]
    greet("leaf", [up, down, above, below] + across[1:])

    def remote(src, dst, send, recv_sem, peer):
        return pltpu.make_async_remote_copy(
            src_ref=src, dst_ref=dst, send_sem=send, recv_sem=recv_sem,
            device_id={"leaf": peer}, device_id_type=MESH,
        )

    sent = []
    asks = []
    for k in range(1, n_y):
        copy = remote(
            sent_requests.at[(y + k) % n_y], asked_v.at[n_y - k - 1], q_send.at[k - 1], q_recv.at[n_y - k - 1], across[k]
        )
        copy.start()
        asks.append(copy)
    sent += asks

    low = lanes((CELL, 2 * LEAF)) < LEAF
    for j in range(HALF):
        top = samples[0:CELL, 2 * LEAF * j : 2 * LEAF * (j + 1)]
        bottom = samples[CELL : 2 * CELL, 2 * LEAF * j : 2 * LEAF * (j + 1)]
        base = (2 * j // HALF) * SUB + (2 * j % HALF) * CELL
        local[base : base + CELL, :] = jnp.where(low, top, swap_halves(bottom))
        local[base + CELL : base + 2 * CELL, :] = jnp.where(low, swap_halves(top), bottom)
    low1 = lanes((1, 2 * LEAF)) < LEAF
    for j in range(HALF):
        xs, ys, zs = [points[a : a + 1, 2 * LEAF * j : 2 * LEAF * (j + 1)] for a in range(3)]
        base = (2 * j // HALF) * SUB + HALF * CELL + (2 * j % HALF) * 2
        local[base : base + 1, :] = jnp.where(low1, xs, swap_halves(ys))
        local[base + 1 : base + 2, :] = jnp.where(low1, zs, swap_halves(zs))
        local[base + 2 : base + 3, :] = jnp.where(low1, swap_halves(xs), ys)
        local[base + 3 : base + 4, :] = jnp.where(low1, swap_halves(zs), zs)

    hops = {(0, 0): n_z // 2, (0, 1): n_z // 2 - 1, (1, 0): n_z // 2 - 1, (1, 1): n_z // 2}

    def ring(way, part, step):
        here, there = (step, step + 1) if way == 0 else ((n_z - step) % n_z, n_z - step - 1)
        rows = pl.ds(part * SUB, SUB)
        return remote(
            chunks[here].at[rows], chunks[there].at[rows], ring_send.at[way, part, step],
            ring_recv.at[way, part, step], up if way == 0 else down,
        )

    def forward(way, part, step):
        if step < hops[way, part]:
            copy = ring(way, part, step)
            copy.start()
            sent.append(copy)

    order = ((0, 0), (1, 1), (0, 1), (1, 0))
    for way, part in order:
        forward(way, part, 0)

    for side, cluster in ((0, 0), (1, 2 * HALF - 1)):
        base = (cluster // HALF) * SUB + (cluster % HALF) * CELL
        cbase = (cluster // HALF) * SUB + HALF * CELL + (cluster % HALF) * 2
        edge[side, 0:CELL, :] = local[base : base + CELL, :]
        edge[side, CELL : CELL + 2, :] = local[cbase : cbase + 2, :]
        edge[side, CELL + 2 : NODE, :] = jnp.zeros((NODE - CELL - 2, 2 * LEAF), jnp.float32)
    edges = [
        remote(edge.at[0], halo.at[1], e_send.at[0], e_recv.at[1], below),
        remote(edge.at[1], halo.at[0], e_send.at[1], e_recv.at[0], above),
    ]
    for copy in edges:
        copy.start()
    sent += edges

    for copy in asks:
        copy.wait_recv()
    moves = [
        pltpu.make_async_copy(asked_v, asked.at[pl.ds(1, n_y - 1)], q_local.at[0]),
        pltpu.make_async_copy(sent_requests.at[y], asked.at[0], q_local.at[1]),
    ]
    for move in moves:
        move.start()
    for move in moves:
        move.wait()

    def pick(chunk, target, request):
        def one(c, carry):
            cell, row = request(c)
            target[pl.ds(pl.multiple_of(c * CELL, CELL), CELL), :] = chunk[pl.ds(cell * CELL, CELL), :]
            for part in range(2):
                target[pl.ds(CAP * CELL + c * 2 + part, 1), :] = chunk[pl.ds(row + part, 1), :]
            return carry

        lax.fori_loop(0, CAP, one, 0)

    arriving = []

    def select(slot):
        chunk = chunks[slot]
        source_z = (z + n_z - slot) % n_z

        def requests(k):
            return lambda c: (asked[k, 0, source_z * CAP + c], asked[k, 1, source_z * CAP + c])

        for k in range(1, n_y):
            pick(chunk, stage.at[k - 1, slot], requests(k))
            copy = remote(
                stage.at[k - 1, slot], recv.at[k * n_z + slot], y_send.at[k - 1, slot], y_recv.at[k - 1, slot], across[k]
            )
            copy.start()
            sent.append(copy)
            arriving.append(copy)
        pick(chunk, recv.at[slot], requests(0))

    select(0)
    for step in range(1, n_z // 2 + 1):
        for way, part in order:
            if step - 1 < hops[way, part]:
                ring(way, part, step - 1).wait_recv()
                forward(way, part, step)
        select(step)
        if step < n_z // 2:
            select(n_z - step)
    for copy in arriving + edges:
        copy.wait_recv()
    for copy in sent:
        copy.wait_send()


def fetch(samples, points, requests, n_leaf):
    n_z = n_leaf // ROWS_Y
    rows = samples.shape[0]
    half, cell = requests // HALF, requests % HALF
    places = jnp.stack([half * (SUB // CELL) + cell, half * SUB + HALF * CELL + cell * 2])
    sent_requests = jnp.swapaxes(places.reshape(2, ROWS_Y, n_z * CAP), 0, 1)
    sent_requests = jnp.pad(sent_requests, ((0, 0), (0, 6), (0, 0)))
    dma = pltpu.SemaphoreType.DMA
    f32 = jnp.float32
    return pl.pallas_call(
        functools.partial(fetch_body, n_leaf),
        out_shape=(
            jax.ShapeDtypeStruct((n_leaf, MSG, 2 * LEAF), f32),
            jax.ShapeDtypeStruct((2 * SUB, 2 * LEAF), f32),
            jax.ShapeDtypeStruct((2, NODE, 2 * LEAF), f32),
        ),
        in_specs=[whole, whole, whole],
        out_specs=(whole, whole, whole),
        scratch_shapes=[VMEM((2 * SUB, 2 * LEAF), f32)] * (n_z - 1)
        + [
            VMEM((ROWS_Y - 1, n_z, MSG, 2 * LEAF), f32),
            VMEM((2, NODE, 2 * LEAF), f32),
            VMEM((ROWS_Y - 1, 8, n_z * CAP), jnp.int32),
            pltpu.SMEM((ROWS_Y, 8, n_z * CAP), jnp.int32),
            dma((2, 2, n_z // 2)),
            dma((2, 2, n_z // 2)),
            dma((ROWS_Y - 1, n_z)),
            dma((ROWS_Y - 1, n_z)),
            dma((ROWS_Y - 1,)),
            dma((ROWS_Y - 1,)),
            dma((2,)),
            dma((2,)),
            dma((2,)),
        ],
        compiler_params=pltpu.CompilerParams(
            collective_id=1, has_side_effects=True, vmem_limit_bytes=40 * MIB
        ),
        name="fetch",
    )(samples, points, sent_requests)


def sample_body(
    leaves, n_leaf, recv, local, halo, points, slots, counts, near, sketch, far_out, near_out, partial_out, cells
):
    n_z = n_leaf // ROWS_Y
    me = lax.axis_index("leaf")
    y, z = me // n_z, me % n_z
    low16 = lanes((CELL, 2 * LEAF)) < LEAF
    low1 = lanes((1, 2 * LEAF)) < LEAF
    low32 = lanes((2 * CELL, 2 * LEAF)) < LEAF
    for c in range(leaves):
        base = (c // HALF) * SUB + (c % HALF) * CELL
        cbase = (c // HALF) * SUB + HALF * CELL + (c % HALF) * 2
        cells[c + 1, 0:CELL, :] = local[base : base + CELL, :]
        cells[c + 1, CELL : CELL + 2, :] = local[cbase : cbase + 2, :]
    cells[0] = halo[0]
    cells[leaves + 1] = halo[1]

    def halves(value):
        high = value.astype(jnp.bfloat16)
        return high, (value - high.astype(jnp.float32)).astype(jnp.bfloat16)

    def pair(coordinates, first, second):
        (block_a, row_a, last_a, scale_a), (block_b, row_b, last_b, scale_b) = first, second
        x = jnp.where(low1, row_a, swap_halves(row_b))
        yy = jnp.where(low1, swap_halves(row_a), row_b)
        zz = jnp.where(low1, last_a, last_b)
        dx = coordinates[0] - x
        dy = coordinates[1] - yy
        dz = coordinates[2] - zz
        square = dx * dx + dy * dy + dz * dz
        values = jnp.exp2(square * lax.rsqrt(jnp.maximum(square, 1e-30)) * (-1.4426950408889634 / length_scale))
        block_a = block_a * scale_a
        block_b = block_b * scale_b
        rows = jnp.concatenate(
            [jnp.where(low16, block_a, swap_halves(block_b)), jnp.where(low16, swap_halves(block_a), block_b)], axis=0
        )
        return halves(values), halves(rows)

    def four(coordinates, entries):
        (k0h, k0l), (s0h, s0l) = pair(coordinates, entries[0], entries[1])
        (k1h, k1l), (s1h, s1l) = pair(coordinates, entries[2], entries[3])
        left = jnp.concatenate(
            [jnp.concatenate([s0h, s1h], axis=1), jnp.concatenate([s0l, s1l], axis=1)], axis=0
        )
        right = jnp.concatenate(
            [jnp.concatenate([k0h, k1h], axis=1), jnp.concatenate([k0l, k1l], axis=1)], axis=0
        )
        return left, right

    def far_entry(leaf, f, count):
        slot = slots[f, leaf]
        owner = slot >> 3
        message = ((y - owner // n_z) & (ROWS_Y - 1)) * n_z + ((z - owner) & (n_z - 1))
        c = slot & (CAP - 1)
        scale = jnp.where(f < count, 1.0, 0.0).astype(jnp.float32)
        return (
            recv[message, pl.ds(pl.multiple_of(c * CELL, CELL), CELL), :],
            recv[message, pl.ds(CAP * CELL + 2 * c, 1), :],
            recv[message, pl.ds(CAP * CELL + 2 * c + 1, 1), :],
            scale,
        )

    def near_entry(leaf, offset):
        at = leaf + offset
        if offset < NEAR:
            place = me * leaves + leaf + offset - NEAR // 2
            inside = (place >= 0) & (place < n_leaf * leaves)
            scale = jnp.where(inside, near[offset, leaf], 0).astype(jnp.float32)
        else:
            scale = jnp.float32(0)
        at = at if offset < NEAR else leaf
        return cells[at, 0:CELL, :], cells[at, CELL : CELL + 1, :], cells[at, CELL + 1 : CELL + 2, :], scale

    def fold(total):
        total = total[: 2 * CELL] + total[2 * CELL :]
        return total + swap_halves(total)

    def two_leaves(j, carry):
        pair_of = (2 * j, 2 * j + 1)
        coordinates = []
        both = points[:, pl.ds(pl.multiple_of(j * 2 * LEAF, 2 * LEAF), 2 * LEAF)]
        both = jnp.concatenate([both, jnp.zeros((5, 2 * LEAF), jnp.float32)], axis=0).T
        for block in (both[:LEAF], both[LEAF:]):
            coordinates.append([jnp.broadcast_to(block[:, a : a + 1], (LEAF, 2 * LEAF)) for a in range(3)])
        count = [counts[leaf] for leaf in pair_of]

        def operands(g):
            return [
                four(coordinates[i], [far_entry(pair_of[i], 4 * g + b, count[i]) for b in range(4)]) for i in range(2)
            ]

        def step(g, carried):
            totals, waiting = carried
            totals = [total + dot_nt(left, right, None) for total, (left, right) in zip(totals, waiting)]
            return totals, operands(g)

        zero = jnp.zeros((LEAF, 2 * LEAF), jnp.float32)
        steps = (jnp.maximum(count[0], count[1]) + 3) // 4
        totals, waiting = lax.fori_loop(1, steps, step, ([zero, zero], operands(0)))
        far = [total + dot_nt(left, right, None) for total, (left, right) in zip(totals, waiting)]
        close = [four(coordinates[i], [near_entry(pair_of[i], o) for o in range(4)]) for i in range(2)]
        close = [dot_nt(left, right, None) for left, right in close]
        far = jnp.where(low32, fold(far[0]), fold(far[1]))
        at = pl.ds(pl.multiple_of(j * 2 * LEAF, 2 * LEAF), 2 * LEAF)
        far_out[:, at] = far
        near_out[:, at] = jnp.where(low32, fold(close[0]), fold(close[1]))
        partial_out[:, at] = dot_nn(sketch[...], far)
        return carry

    lax.fori_loop(0, leaves // 2, two_leaves, 0)


def sample(recv, local, halo, points, slots, counts, near, sketch, n_leaf):
    leaves = counts.shape[0]
    shape = jax.ShapeDtypeStruct((RANK, leaves * LEAF), jnp.float32)
    return pl.pallas_call(
        functools.partial(sample_body, leaves, n_leaf),
        out_shape=(shape, shape, shape),
        in_specs=[whole, whole, whole, whole, scalars, scalars, scalars, whole],
        out_specs=(whole, whole, whole),
        scratch_shapes=[VMEM((leaves + 2, NODE, 2 * LEAF), jnp.float32)],
        compiler_params=pltpu.CompilerParams(vmem_limit_bytes=40 * MIB),
        name="sample",
    )(recv, local, halo, points, slots, counts, near, sketch)


def total_body(n, partial, out, parts, send_a, recv_a, send_b, recv_b):
    me = lax.axis_index("cols")
    width = partial.shape[1] // n
    peers = [(me + k) % n for k in range(1, n)]
    greet("cols", peers)

    def piece(owner):
        return pl.ds(pl.multiple_of(owner * width, width), width)

    first = []
    for k in range(1, n):
        copy = pltpu.make_async_remote_copy(
            src_ref=partial.at[:, piece(peers[k - 1])], dst_ref=parts.at[k - 1], send_sem=send_a.at[k - 1],
            recv_sem=recv_a.at[k - 1], device_id={"cols": peers[k - 1]}, device_id_type=MESH,
        )
        copy.start()
        first.append(copy)
    value = partial[:, piece(me)]
    for k in range(1, n):
        first[k - 1].wait_recv()
        value = value + parts[k - 1]
    out[:, piece(me)] = value
    second = []
    for k in range(1, n):
        copy = pltpu.make_async_remote_copy(
            src_ref=out.at[:, piece(me)], dst_ref=out.at[:, piece(me)], send_sem=send_b.at[k - 1],
            recv_sem=recv_b.at[k - 1], device_id={"cols": peers[k - 1]}, device_id_type=MESH,
        )
        copy.start()
        second.append(copy)
    for k in range(1, n):
        owner = (me + n - k) % n
        pltpu.make_async_remote_copy(
            src_ref=out.at[:, piece(owner)], dst_ref=out.at[:, piece(owner)], send_sem=send_b.at[k - 1],
            recv_sem=recv_b.at[k - 1], device_id={"cols": peers[k - 1]}, device_id_type=MESH,
        ).wait_recv()
    for copy in first + second:
        copy.wait_send()


def total(partial, n):
    rows, columns = partial.shape
    dma = pltpu.SemaphoreType.DMA
    return pl.pallas_call(
        functools.partial(total_body, n),
        out_shape=jax.ShapeDtypeStruct(partial.shape, jnp.float32),
        in_specs=[whole],
        out_specs=whole,
        scratch_shapes=[VMEM((n - 1, rows, columns // n), jnp.float32)] + [dma((n - 1,))] * 4,
        compiler_params=pltpu.CompilerParams(collective_id=2, has_side_effects=True),
        name="total",
    )(partial)


def eye(shape, first=0):
    rows = lax.broadcasted_iota(jnp.int32, shape, 0)
    return jnp.where(lanes(shape) == rows + first, 1.0, 0.0).astype(jnp.float32)


def inverse(value):
    guess = pl.reciprocal(value, approx=True)
    guess = guess * (2.0 - value * guess)
    return guess * (2.0 - value * guess)


def compress(tiles, traces):
    block = 4 if len(tiles) > 8 else 8
    shape = (RANK, 4 * RANK)
    on_diagonal = lanes(shape) == lax.broadcasted_iota(jnp.int32, shape, 0)
    tiles = [
        tile + jnp.where(on_diagonal, shift_share * trace / RANK + 1e-06, 0.0) for tile, trace in zip(tiles, traces)
    ]
    tiles = [[tile[8 * g : 8 * g + 8] for g in range(4)] for tile in tiles]
    full = (8, 4 * RANK)
    sub = lax.broadcasted_iota(jnp.int32, full, 0)
    scales = [[jnp.zeros(full, jnp.float32) for g in range(4)] for tile in tiles]
    for first in range(0, RANK, block):
        g = first // 8
        columns = [
            [[jnp.broadcast_to(part[:, first + t : first + t + 1], full) for t in range(block)] for part in tile[g:]]
            for tile in tiles
        ]
        for t in range(block):
            s = (first + t) % 8
            for tile, column, scale in zip(tiles, columns, scales):
                pivot = jnp.broadcast_to(column[0][t][s : s + 1], full)
                inv = inverse(pivot)
                scale[g] = jnp.where(sub == s, lax.rsqrt(pivot), scale[g])
                row = jnp.broadcast_to(tile[g][s : s + 1], full) * inv
                right = [None] * block
                for u in range(t + 1, block):
                    right[u] = jnp.broadcast_to(column[0][u][s : s + 1], full) * inv
                for h in range(g, 4):
                    c = column[h - g][t]
                    if h == g:
                        if s == 7:
                            continue
                        c = jnp.where(sub > s, c, 0.0)
                    tile[h] = tile[h] - c * row
                    for u in range(t + 1, block):
                        column[h - g][u] = column[h - g][u] - c * right[u]
    return [
        jnp.concatenate([part * factor for part, factor in zip(tile, scale)], axis=0)
        for tile, scale in zip(tiles, scales)
    ]


def halves(value):
    high = value.astype(jnp.bfloat16)
    return high, (value - high.astype(jnp.float32)).astype(jnp.bfloat16)


def total_of(value):
    return jnp.sum(jnp.sum(value, axis=0, keepdims=True), axis=1, keepdims=True)


def parent_tile(stacked):
    lane = lanes(stacked.shape)
    c = jnp.where(lane < RANK, stacked, 0.0)
    right = jnp.where(lane < 2 * RANK, c + pltpu.roll(c, RANK, 1), eye(stacked.shape, 2 * RANK))
    tile = lax.dot_general(
        c[:, :RANK], right, (((0,), (0,)), ((), ())), precision=highest, preferred_element_type=jnp.float32
    )
    return tile, total_of(c * c)


def project(tile, stacked):
    low = lanes(tile.shape) < 2 * RANK
    high, rest = halves(tile)
    s_high, s_rest = halves(stacked)
    high = high.astype(jnp.float32)
    first = jnp.where(low, swap_halves(rest.astype(jnp.float32)), high)
    left = jnp.concatenate([first, swap_halves(high)], axis=1)[:, : 6 * RANK].astype(jnp.bfloat16)
    return dot_nn(left, jnp.concatenate([s_high, s_high, s_rest], axis=0), None)


def level(read, write, count, group):
    def some(start):
        inputs = [read(start + b) for b in range(min(group, count))]
        pairs = [parent_tile(c) for c, _ in inputs]
        tiles = compress([tile for tile, _ in pairs], [trace for _, trace in pairs])
        for b, (tile, (_, stacked)) in enumerate(zip(tiles, inputs)):
            write(start + b, tile, project(tile, stacked))

    if count <= group:
        some(0)
    else:
        lax.fori_loop(0, count // group, lambda g, carry: (some(g * group), carry)[1], 0)


def branch_body(leaves, sketched, far, basis, branch, packed_c, packed_p, nodes, projected):
    low = lanes((RANK, 2 * LEAF)) < LEAF
    unit = eye((2 * RANK, 2 * RANK))
    group = 16

    def project_t(tile, row):
        high, rest = [part.astype(jnp.float32) for part in halves(tile)]
        r_high, r_rest = [part.astype(jnp.float32) for part in halves(row)]
        left = [jnp.where(low, swap_halves(rest), high), jnp.where(low, 0.0, high)]
        right = [jnp.where(low, swap_halves(r_high), r_high), r_rest]
        return dot_nt(
            jnp.concatenate(left, axis=1).astype(jnp.bfloat16), jnp.concatenate(right, axis=1).astype(jnp.bfloat16), None
        )

    def some(g, carry):
        bs, rows = [], []
        for j in range(group // 2):
            at = pl.ds(pl.multiple_of((g * (group // 2) + j) * 2 * LEAF, 2 * LEAF), 2 * LEAF)
            b, row = sketched[:, at], far[:, at]
            bs += [b[:, :LEAF], swap_halves(b)[:, :LEAF]]
            rows += [swap_halves(row), row]
        tiles = compress([dot_nt(b, jnp.concatenate([b, b, unit], axis=0)) for b in bs], [total_of(b * b) for b in bs])
        for b, (tile, row) in enumerate(zip(tiles, rows)):
            nodes[g * group + b] = tile
            projected[g * group + b] = project_t(tile, row)
        for j in range(group // 2):
            at = pl.ds(pl.multiple_of((g * (group // 2) + j) * 2 * LEAF, 2 * LEAF), 2 * LEAF)
            basis[:, at] = jnp.where(low, swap_halves(tiles[2 * j]), tiles[2 * j + 1])
        return carry

    lax.fori_loop(0, leaves // group, some, 0)

    def read(node):
        pair = nodes[pl.ds(2 * node, 2)].reshape(2 * RANK, 4 * RANK)
        return pltpu.roll(pair, 3 * RANK, 1), projected[pl.ds(2 * node, 2)].reshape(2 * RANK, RANK)

    def write(node, tile, value):
        nodes[node] = tile
        projected[node] = value

    count = leaves // 2
    while count >= 1:
        level(read, write, count, 16)
        count //= 2
    branch[...] = projected[0]
    quarter = lanes((8, 4 * RANK)) // RANK
    wide = dot_nn(projected[0], eye((RANK, 4 * RANK)))
    tile = nodes[0]
    for i, (source, shift) in enumerate(((tile, RANK), (wide, 0))):
        row = jnp.zeros((8, 4 * RANK), jnp.float32)
        for g in range(4):
            turned = pltpu.roll(source[8 * g : 8 * g + 8], (RANK * g - shift) % (4 * RANK), 1)
            row = jnp.where(quarter == g, turned, row)
        if i == 0:
            for g in range(8):
                packed_c[g] = row[g : g + 1]
        else:
            packed_p[...] = row


def meet(n_leaf, n_cols):
    n_y = ROWS_Y
    n_z = n_leaf // n_y
    me, col = lax.axis_index("leaf"), lax.axis_index("cols")
    y, z = me // n_z, me % n_z
    across = [((y + k) % n_y) * n_z + z for k in range(1, n_y)]
    along = [y * n_z + (z + k) % n_z for k in range(1, n_z)]
    others = [(col + k) % n_cols for k in range(1, n_cols)]
    barrier = pltpu.get_barrier_semaphore()
    for peer in across + along:
        pl.semaphore_signal(barrier, inc=1, device_id={"leaf": peer}, device_id_type=MESH)
    for peer in others:
        pl.semaphore_signal(barrier, inc=1, device_id={"cols": peer}, device_id_type=MESH)
    return lambda: pl.semaphore_wait(barrier, len(across) + len(along) + len(others))


def gather_body(n_leaf, n_cols, packed_c, packed_p, out_c, out_p, sems):
    yc_send, yc_recv, yp_send, yp_recv, zc_send, zc_recv, zp_send, zp_recv, x_send, x_recv, own = sems
    n_y = ROWS_Y
    n_z = n_leaf // n_y
    me, col = lax.axis_index("leaf"), lax.axis_index("cols")
    y, z = me // n_z, me % n_z
    across = [((y + k) % n_y) * n_z + z for k in range(1, n_y)]
    along = [y * n_z + (z + k) % n_z for k in range(1, n_z)]
    others = [(col + k) % n_cols for k in range(1, n_cols)]
    sent = []

    def push(src, dst, send, recv, axis, peer):
        copy = pltpu.make_async_remote_copy(
            src_ref=src, dst_ref=dst, send_sem=send, recv_sem=recv, device_id={axis: peer}, device_id_type=MESH
        )
        copy.start()
        sent.append(copy)

    def arrived(ref, send, recv, axis, peer):
        pltpu.make_async_remote_copy(
            src_ref=ref, dst_ref=ref, send_sem=send, recv_sem=recv, device_id={axis: peer}, device_id_type=MESH
        ).wait_recv()

    for k in range(n_y - 1):
        push(packed_c.at[col], out_c.at[col, z, y], yc_send.at[k], yc_recv.at[k], "leaf", across[k])
    for k in range(n_y - 1):
        push(packed_p, out_p.at[z, y], yp_send.at[k], yp_recv.at[k], "leaf", across[k])
    mine = [
        pltpu.make_async_copy(packed_c.at[col], out_c.at[col, z, y], own.at[0]),
        pltpu.make_async_copy(packed_p, out_p.at[z, y], own.at[1]),
    ]
    for copy in mine:
        copy.start()
    for copy in mine:
        copy.wait()
    far_first = sorted(range(n_z - 1), key=lambda k: -min(k + 1, n_z - 1 - k))
    for k in range(n_y - 1):
        arrived(out_c.at[col, z, (y + n_y - k - 1) % n_y], yc_send.at[k], yc_recv.at[k], "leaf", across[k])
    for k in far_first:
        push(out_c.at[col, z], out_c.at[col, z], zc_send.at[k], zc_recv.at[k], "leaf", along[k])
    for k in range(n_y - 1):
        arrived(out_p.at[z, (y + n_y - k - 1) % n_y], yp_send.at[k], yp_recv.at[k], "leaf", across[k])
    for k in far_first:
        push(out_p.at[z], out_p.at[z], zp_send.at[k], zp_recv.at[k], "leaf", along[k])
    for k in range(n_z - 1):
        arrived(out_c.at[col, (z + n_z - k - 1) % n_z], zc_send.at[k], zc_recv.at[k], "leaf", along[k])
    for k in range(n_cols - 1):
        push(out_c.at[col], out_c.at[col], x_send.at[k], x_recv.at[k], "cols", others[k])
    for k in range(n_cols - 1):
        arrived(out_c.at[(col + n_cols - k - 1) % n_cols], x_send.at[k], x_recv.at[k], "cols", others[k])

    def later():
        for k in range(n_z - 1):
            arrived(out_p.at[(z + n_z - k - 1) % n_z], zp_send.at[k], zp_recv.at[k], "leaf", along[k])

    def end():
        for copy in sent:
            copy.wait_send()

    return later, end


def top_body(n_leaf, gathered_c, gathered_p, transfers, root, nodes, projected, later):
    n_z = n_leaf // ROWS_Y
    count = n_leaf // 2

    def unpack(block):
        return jnp.concatenate([pltpu.roll(block, (4 * RANK - RANK * g) % (4 * RANK), 1) for g in range(4)], axis=0)

    def children(node):
        return [(child % n_z, child // n_z) for child in (2 * node, 2 * node + 1)]

    def first_level(g, carry):
        stacked = []
        for b in range(16):
            pair = children(16 * g + b)
            stacked.append(
                jnp.concatenate(
                    [unpack(jnp.concatenate([gathered_c[i, z, y] for i in range(8)], axis=0)) for z, y in pair], axis=0
                )
            )
        pairs = [parent_tile(c) for c in stacked]
        tiles = compress([tile for tile, _ in pairs], [trace for _, trace in pairs])
        for b in range(16):
            nodes[16 * g + b] = tiles[b]
            transfers[16 * g + b] = swap_halves(tiles[b])[:, : 2 * RANK]
        return carry

    lax.fori_loop(0, count // 16, first_level, 0)
    later()

    def first_projections(g, carry):
        for b in range(16):
            node = 16 * g + b
            stacked = jnp.concatenate([unpack(gathered_p[z, y]) for z, y in children(node)], axis=0)
            projected[node] = project(nodes[node], stacked)
        return carry

    lax.fori_loop(0, count // 16, first_projections, 0)

    def read(node):
        pair = nodes[pl.ds(2 * node, 2)].reshape(2 * RANK, 4 * RANK)
        return pltpu.roll(pair, 3 * RANK, 1), projected[pl.ds(2 * node, 2)].reshape(2 * RANK, 4 * RANK)

    first = count
    count //= 2
    while count >= 1:

        def write(node, tile, value, first=first):
            nodes[node] = tile
            projected[node] = value
            transfers[first + node] = swap_halves(tile)[:, : 2 * RANK]

        level(read, write, count, 16)
        first += count
        count //= 2
    root[...] = projected[0][:, :RANK]


def tree_body(
    leaves, n_leaf, n_cols, sketched, far, basis, branch, transfers, root,
    nodes, projected, upper, packed_c, packed_p, out_c, out_p, *sems,
):
    wait = meet(n_leaf, n_cols)
    branch_body(leaves, sketched, far, basis, branch, packed_c, packed_p, nodes, projected)
    wait()
    later, end = gather_body(n_leaf, n_cols, packed_c, packed_p, out_c, out_p, sems)
    top_body(n_leaf, out_c, out_p, transfers, root, nodes, upper, later)
    end()


def tree(sketched, far, n_leaf, n_cols):
    leaves = sketched.shape[1] // LEAF
    n_z = n_leaf // ROWS_Y
    f32 = jnp.float32
    dma = pltpu.SemaphoreType.DMA
    count = max(leaves, n_leaf // 2)
    return pl.pallas_call(
        functools.partial(tree_body, leaves, n_leaf, n_cols),
        out_shape=(
            jax.ShapeDtypeStruct(sketched.shape, f32),
            jax.ShapeDtypeStruct((RANK, RANK), f32),
            jax.ShapeDtypeStruct((n_leaf - 1, RANK, 2 * RANK), f32),
            jax.ShapeDtypeStruct((RANK, RANK), f32),
        ),
        in_specs=[whole, whole],
        out_specs=(whole, whole, whole, whole),
        scratch_shapes=[
            VMEM((count, RANK, 4 * RANK), f32),
            VMEM((leaves, RANK, RANK), f32),
            VMEM((n_leaf // 2, RANK, 4 * RANK), f32),
            VMEM((8, 1, 4 * RANK), f32),
            VMEM((8, 4 * RANK), f32),
            VMEM((8, n_z, ROWS_Y, 1, 4 * RANK), f32),
            VMEM((n_z, ROWS_Y, 8, 4 * RANK), f32),
        ]
        + [dma((ROWS_Y - 1,))] * 4
        + [dma((n_z - 1,))] * 4
        + [dma((n_cols - 1,))] * 2
        + [dma((2,))],
        compiler_params=pltpu.CompilerParams(
            collective_id=3, has_side_effects=True, vmem_limit_bytes=40 * MIB
        ),
        name="tree",
    )(sketched, far)


def on_device(n_leaf, n_cols, points, samples, sketch, far_requests, far_slots, far_count, near_mask):
    recv, local, halo = fetch(samples, points, far_requests[0], n_leaf)
    far_sample, near_sample, partial = sample(
        recv, local, halo, points, far_slots.T, far_count, near_mask.T, sketch, n_leaf
    )
    sketched = total(partial, n_cols)
    leaf_basis, branch_samples, top_transfer, root_sample = tree(sketched, far_sample, n_leaf, n_cols)
    return far_sample, near_sample, leaf_basis, branch_samples, jnp.swapaxes(top_transfer, 1, 2), root_sample


def solution(mesh):
    return jax.shard_map(
        functools.partial(on_device, mesh.shape["leaf"], mesh.shape["cols"]),
        mesh=mesh,
        in_specs=(
            P(None, "leaf"),
            P("cols", "leaf"),
            P(None, "cols"),
            P("leaf", None, None),
            P("leaf", None),
            P("leaf"),
            P("leaf", None),
        ),
        out_specs=(
            P("cols", "leaf"),
            P("cols", "leaf"),
            P(None, "leaf"),
            P("leaf", "cols"),
            P(),
            P(None, "cols"),
        ),
        check_vma=False,
    )
```

```python
import functools

import jax
import jax.numpy as jnp
from jax import lax
from jax.experimental import pallas as pl
from jax.experimental.pallas import tpu as pltpu
from jax.sharding import PartitionSpec as P

LEAF = 64
FAR = 16
CAP = 8
RANK = 32
NEAR = 3
ROWS_Y = 4
CELL = 16
HALF = 16
SUB = HALF * CELL + HALF * 2
MSG = CAP * CELL + CAP * 2
NODE = 24

length_scale = 0.3
shift_share = 0.05
highest = lax.Precision.HIGHEST
MESH = pl.DeviceIdType.MESH
VMEM = pltpu.VMEM
whole = pl.BlockSpec(memory_space=pltpu.VMEM)
scalars = pl.BlockSpec(memory_space=pltpu.SMEM)
MIB = 1 << 20


def lanes(shape):
    return lax.broadcasted_iota(jnp.int32, shape, len(shape) - 1)


def swap_halves(tile):
    return pltpu.roll(tile, 64, 1)


def dot_nt(a, b, precision=highest):
    return lax.dot_general(
        a, b, (((1,), (1,)), ((), ())), precision=precision, preferred_element_type=jnp.float32
    )


def dot_nn(a, b, precision=highest):
    return lax.dot_general(
        a, b, (((1,), (0,)), ((), ())), precision=precision, preferred_element_type=jnp.float32
    )


def greet(axis, peers):
    barrier = pltpu.get_barrier_semaphore()
    for peer in peers:
        pl.semaphore_signal(barrier, inc=1, device_id={axis: peer}, device_id_type=MESH)
    pl.semaphore_wait(barrier, len(peers))


def fetch_body(
    n_leaf, samples, points, sent_requests, recv, local, halo, *scratch
):
    n_y = ROWS_Y
    n_z = n_leaf // n_y
    chunks = (local,) + scratch[: n_z - 1]
    stage, edge, asked_v, asked, ring_send, ring_recv, y_send, y_recv, q_send, q_recv, q_local, e_send, e_recv = scratch[n_z - 1 :]
    me = lax.axis_index("leaf")
    y, z = me // n_z, me % n_z
    up = y * n_z + (z + 1) % n_z
    down = y * n_z + (z + n_z - 1) % n_z
    above, below = (me + 1) % n_leaf, (me + n_leaf - 1) % n_leaf
    across = [None] + [((y + k) % n_y) * n_z + z for k in range(1, n_y)]
    greet("leaf", [up, down, above, below] + across[1:])

    def remote(src, dst, send, recv_sem, peer):
        return pltpu.make_async_remote_copy(
            src_ref=src, dst_ref=dst, send_sem=send, recv_sem=recv_sem,
            device_id={"leaf": peer}, device_id_type=MESH,
        )

    sent = []
    asks = []
    for k in range(1, n_y):
        copy = remote(
            sent_requests.at[(y + k) % n_y], asked_v.at[n_y - k - 1], q_send.at[k - 1], q_recv.at[n_y - k - 1], across[k]
        )
        copy.start()
        asks.append(copy)
    sent += asks

    low = lanes((CELL, 2 * LEAF)) < LEAF
    for j in range(HALF):
        top = samples[0:CELL, 2 * LEAF * j : 2 * LEAF * (j + 1)]
        bottom = samples[CELL : 2 * CELL, 2 * LEAF * j : 2 * LEAF * (j + 1)]
        base = (2 * j // HALF) * SUB + (2 * j % HALF) * CELL
        local[base : base + CELL, :] = jnp.where(low, top, swap_halves(bottom))
        local[base + CELL : base + 2 * CELL, :] = jnp.where(low, swap_halves(top), bottom)
    low1 = lanes((1, 2 * LEAF)) < LEAF
    for j in range(HALF):
        xs, ys, zs = [points[a : a + 1, 2 * LEAF * j : 2 * LEAF * (j + 1)] for a in range(3)]
        base = (2 * j // HALF) * SUB + HALF * CELL + (2 * j % HALF) * 2
        local[base : base + 1, :] = jnp.where(low1, xs, swap_halves(ys))
        local[base + 1 : base + 2, :] = jnp.where(low1, zs, swap_halves(zs))
        local[base + 2 : base + 3, :] = jnp.where(low1, swap_halves(xs), ys)
        local[base + 3 : base + 4, :] = jnp.where(low1, swap_halves(zs), zs)

    hops = {(0, 0): n_z // 2, (0, 1): n_z // 2 - 1, (1, 0): n_z // 2 - 1, (1, 1): n_z // 2}

    def ring(way, part, step):
        here, there = (step, step + 1) if way == 0 else ((n_z - step) % n_z, n_z - step - 1)
        rows = pl.ds(part * SUB, SUB)
        return remote(
            chunks[here].at[rows], chunks[there].at[rows], ring_send.at[way, part, step],
            ring_recv.at[way, part, step], up if way == 0 else down,
        )

    def forward(way, part, step):
        if step < hops[way, part]:
            copy = ring(way, part, step)
            copy.start()
            sent.append(copy)

    order = ((0, 0), (1, 1), (0, 1), (1, 0))
    for way, part in order:
        forward(way, part, 0)

    for side, cluster in ((0, 0), (1, 2 * HALF - 1)):
        base = (cluster // HALF) * SUB + (cluster % HALF) * CELL
        cbase = (cluster // HALF) * SUB + HALF * CELL + (cluster % HALF) * 2
        edge[side, 0:CELL, :] = local[base : base + CELL, :]
        edge[side, CELL : CELL + 2, :] = local[cbase : cbase + 2, :]
        edge[side, CELL + 2 : NODE, :] = jnp.zeros((NODE - CELL - 2, 2 * LEAF), jnp.float32)
    edges = [
        remote(edge.at[0], halo.at[1], e_send.at[0], e_recv.at[1], below),
        remote(edge.at[1], halo.at[0], e_send.at[1], e_recv.at[0], above),
    ]
    for copy in edges:
        copy.start()
    sent += edges

    for copy in asks:
        copy.wait_recv()
    moves = [
        pltpu.make_async_copy(asked_v, asked.at[pl.ds(1, n_y - 1)], q_local.at[0]),
        pltpu.make_async_copy(sent_requests.at[y], asked.at[0], q_local.at[1]),
    ]
    for move in moves:
        move.start()
    for move in moves:
        move.wait()

    def pick(chunk, target, request):
        def one(c, carry):
            cell, row = request(c)
            target[pl.ds(pl.multiple_of(c * CELL, CELL), CELL), :] = chunk[pl.ds(cell * CELL, CELL), :]
            for part in range(2):
                target[pl.ds(CAP * CELL + c * 2 + part, 1), :] = chunk[pl.ds(row + part, 1), :]
            return carry

        lax.fori_loop(0, CAP, one, 0)

    arriving = []

    def select(slot):
        chunk = chunks[slot]
        source_z = (z + n_z - slot) % n_z

        def requests(k):
            return lambda c: (asked[k, 0, source_z * CAP + c], asked[k, 1, source_z * CAP + c])

        for k in range(1, n_y):
            pick(chunk, stage.at[k - 1, slot], requests(k))
            copy = remote(
                stage.at[k - 1, slot], recv.at[k * n_z + slot], y_send.at[k - 1, slot], y_recv.at[k - 1, slot], across[k]
            )
            copy.start()
            sent.append(copy)
            arriving.append(copy)
        pick(chunk, recv.at[slot], requests(0))

    select(0)
    for step in range(1, n_z // 2 + 1):
        for way, part in order:
            if step - 1 < hops[way, part]:
                ring(way, part, step - 1).wait_recv()
                forward(way, part, step)
        select(step)
        if step < n_z // 2:
            select(n_z - step)
    for copy in arriving + edges:
        copy.wait_recv()
    for copy in sent:
        copy.wait_send()


def fetch(samples, points, requests, n_leaf):
    n_z = n_leaf // ROWS_Y
    rows = samples.shape[0]
    half, cell = requests // HALF, requests % HALF
    places = jnp.stack([half * (SUB // CELL) + cell, half * SUB + HALF * CELL + cell * 2])
    sent_requests = jnp.swapaxes(places.reshape(2, ROWS_Y, n_z * CAP), 0, 1)
    sent_requests = jnp.pad(sent_requests, ((0, 0), (0, 6), (0, 0)))
    dma = pltpu.SemaphoreType.DMA
    f32 = jnp.float32
    return pl.pallas_call(
        functools.partial(fetch_body, n_leaf),
        out_shape=(
            jax.ShapeDtypeStruct((n_leaf, MSG, 2 * LEAF), f32),
            jax.ShapeDtypeStruct((2 * SUB, 2 * LEAF), f32),
            jax.ShapeDtypeStruct((2, NODE, 2 * LEAF), f32),
        ),
        in_specs=[whole, whole, whole],
        out_specs=(whole, whole, whole),
        scratch_shapes=[VMEM((2 * SUB, 2 * LEAF), f32)] * (n_z - 1)
        + [
            VMEM((ROWS_Y - 1, n_z, MSG, 2 * LEAF), f32),
            VMEM((2, NODE, 2 * LEAF), f32),
            VMEM((ROWS_Y - 1, 8, n_z * CAP), jnp.int32),
            pltpu.SMEM((ROWS_Y, 8, n_z * CAP), jnp.int32),
            dma((2, 2, n_z // 2)),
            dma((2, 2, n_z // 2)),
            dma((ROWS_Y - 1, n_z)),
            dma((ROWS_Y - 1, n_z)),
            dma((ROWS_Y - 1,)),
            dma((ROWS_Y - 1,)),
            dma((2,)),
            dma((2,)),
            dma((2,)),
        ],
        compiler_params=pltpu.CompilerParams(
            collective_id=1, has_side_effects=True, vmem_limit_bytes=40 * MIB
        ),
        name="fetch",
    )(samples, points, sent_requests)


def sample_body(
    leaves, n_leaf, recv, local, halo, points, slots, counts, near, sketch, far_out, near_out, partial_out, cells
):
    n_z = n_leaf // ROWS_Y
    me = lax.axis_index("leaf")
    y, z = me // n_z, me % n_z
    low16 = lanes((CELL, 2 * LEAF)) < LEAF
    low1 = lanes((1, 2 * LEAF)) < LEAF
    low32 = lanes((2 * CELL, 2 * LEAF)) < LEAF
    for c in range(leaves):
        base = (c // HALF) * SUB + (c % HALF) * CELL
        cbase = (c // HALF) * SUB + HALF * CELL + (c % HALF) * 2
        cells[c + 1, 0:CELL, :] = local[base : base + CELL, :]
        cells[c + 1, CELL : CELL + 2, :] = local[cbase : cbase + 2, :]
    cells[0] = halo[0]
    cells[leaves + 1] = halo[1]

    def halves(value):
        high = value.astype(jnp.bfloat16)
        return high, (value - high.astype(jnp.float32)).astype(jnp.bfloat16)

    def pair(coordinates, first, second):
        (block_a, row_a, last_a, scale_a), (block_b, row_b, last_b, scale_b) = first, second
        x = jnp.where(low1, row_a, swap_halves(row_b))
        yy = jnp.where(low1, swap_halves(row_a), row_b)
        zz = jnp.where(low1, last_a, last_b)
        dx = coordinates[0] - x
        dy = coordinates[1] - yy
        dz = coordinates[2] - zz
        square = dx * dx + dy * dy + dz * dz
        values = jnp.exp2(square * lax.rsqrt(jnp.maximum(square, 1e-30)) * (-1.4426950408889634 / length_scale))
        block_a = block_a * scale_a
        block_b = block_b * scale_b
        rows = jnp.concatenate(
            [jnp.where(low16, block_a, swap_halves(block_b)), jnp.where(low16, swap_halves(block_a), block_b)], axis=0
        )
        return halves(values), halves(rows)

    def four(coordinates, entries):
        (k0h, k0l), (s0h, s0l) = pair(coordinates, entries[0], entries[1])
        (k1h, k1l), (s1h, s1l) = pair(coordinates, entries[2], entries[3])
        left = jnp.concatenate(
            [jnp.concatenate([s0h, s1h], axis=1), jnp.concatenate([s0l, s1l], axis=1)], axis=0
        )
        right = jnp.concatenate(
            [jnp.concatenate([k0h, k1h], axis=1), jnp.concatenate([k0l, k1l], axis=1)], axis=0
        )
        return left, right

    def far_entry(leaf, f, count):
        slot = slots[f, leaf]
        owner = slot >> 3
        message = ((y - owner // n_z) & (ROWS_Y - 1)) * n_z + ((z - owner) & (n_z - 1))
        c = slot & (CAP - 1)
        scale = jnp.where(f < count, 1.0, 0.0).astype(jnp.float32)
        return (
            recv[message, pl.ds(pl.multiple_of(c * CELL, CELL), CELL), :],
            recv[message, pl.ds(CAP * CELL + 2 * c, 1), :],
            recv[message, pl.ds(CAP * CELL + 2 * c + 1, 1), :],
            scale,
        )

    def near_entry(leaf, offset):
        at = leaf + offset
        if offset < NEAR:
            place = me * leaves + leaf + offset - NEAR // 2
            inside = (place >= 0) & (place < n_leaf * leaves)
            scale = jnp.where(inside, near[offset, leaf], 0).astype(jnp.float32)
        else:
            scale = jnp.float32(0)
        at = at if offset < NEAR else leaf
        return cells[at, 0:CELL, :], cells[at, CELL : CELL + 1, :], cells[at, CELL + 1 : CELL + 2, :], scale

    def fold(total):
        total = total[: 2 * CELL] + total[2 * CELL :]
        return total + swap_halves(total)

    def two_leaves(j, carry):
        pair_of = (2 * j, 2 * j + 1)
        coordinates = []
        both = points[:, pl.ds(pl.multiple_of(j * 2 * LEAF, 2 * LEAF), 2 * LEAF)]
        both = jnp.concatenate([both, jnp.zeros((5, 2 * LEAF), jnp.float32)], axis=0).T
        for block in (both[:LEAF], both[LEAF:]):
            coordinates.append([jnp.broadcast_to(block[:, a : a + 1], (LEAF, 2 * LEAF)) for a in range(3)])
        count = [counts[leaf] for leaf in pair_of]

        def operands(g):
            return [
                four(coordinates[i], [far_entry(pair_of[i], 4 * g + b, count[i]) for b in range(4)]) for i in range(2)
            ]

        def step(g, carried):
            totals, waiting = carried
            totals = [total + dot_nt(left, right, None) for total, (left, right) in zip(totals, waiting)]
            return totals, operands(g)

        zero = jnp.zeros((LEAF, 2 * LEAF), jnp.float32)
        steps = (jnp.maximum(count[0], count[1]) + 3) // 4
        totals, waiting = lax.fori_loop(1, steps, step, ([zero, zero], operands(0)))
        far = [total + dot_nt(left, right, None) for total, (left, right) in zip(totals, waiting)]
        close = [four(coordinates[i], [near_entry(pair_of[i], o) for o in range(4)]) for i in range(2)]
        close = [dot_nt(left, right, None) for left, right in close]
        far = jnp.where(low32, fold(far[0]), fold(far[1]))
        at = pl.ds(pl.multiple_of(j * 2 * LEAF, 2 * LEAF), 2 * LEAF)
        far_out[:, at] = far
        near_out[:, at] = jnp.where(low32, fold(close[0]), fold(close[1]))
        partial_out[:, at] = dot_nn(sketch[...], far)
        return carry

    lax.fori_loop(0, leaves // 2, two_leaves, 0)


def sample(recv, local, halo, points, slots, counts, near, sketch, n_leaf):
    leaves = counts.shape[0]
    shape = jax.ShapeDtypeStruct((RANK, leaves * LEAF), jnp.float32)
    return pl.pallas_call(
        functools.partial(sample_body, leaves, n_leaf),
        out_shape=(shape, shape, shape),
        in_specs=[whole, whole, whole, whole, scalars, scalars, scalars, whole],
        out_specs=(whole, whole, whole),
        scratch_shapes=[VMEM((leaves + 2, NODE, 2 * LEAF), jnp.float32)],
        compiler_params=pltpu.CompilerParams(vmem_limit_bytes=40 * MIB),
        name="sample",
    )(recv, local, halo, points, slots, counts, near, sketch)


def eye(shape, first=0):
    rows = lax.broadcasted_iota(jnp.int32, shape, 0)
    return jnp.where(lanes(shape) == rows + first, 1.0, 0.0).astype(jnp.float32)


def inverse(value):
    guess = pl.reciprocal(value, approx=True)
    guess = guess * (2.0 - value * guess)
    return guess * (2.0 - value * guess)


def compress(tiles, traces):
    block = 8
    shape = (RANK, 4 * RANK)
    on_diagonal = lanes(shape) == lax.broadcasted_iota(jnp.int32, shape, 0)
    tiles = [
        tile + jnp.where(on_diagonal, shift_share * trace / RANK + 1e-06, 0.0) for tile, trace in zip(tiles, traces)
    ]
    tiles = [[tile[8 * g : 8 * g + 8] for g in range(4)] for tile in tiles]
    full = (8, 4 * RANK)
    sub = lax.broadcasted_iota(jnp.int32, full, 0)
    scales = [[jnp.zeros(full, jnp.float32) for g in range(4)] for tile in tiles]
    for first in range(0, RANK, block):
        g = first // 8
        columns = [
            [[jnp.broadcast_to(part[:, first + t : first + t + 1], full) for t in range(block)] for part in tile[g:]]
            for tile in tiles
        ]
        for t in range(block):
            s = (first + t) % 8
            for tile, column, scale in zip(tiles, columns, scales):
                pivot = jnp.broadcast_to(column[0][t][s : s + 1], full)
                inv = inverse(pivot)
                scale[g] = jnp.where(sub == s, lax.rsqrt(pivot), scale[g])
                row = jnp.broadcast_to(tile[g][s : s + 1], full) * inv
                right = [None] * block
                for u in range(t + 1, block):
                    right[u] = jnp.broadcast_to(column[0][u][s : s + 1], full) * inv
                for h in range(g, 4):
                    c = column[h - g][t]
                    if h == g:
                        if s == 7:
                            continue
                        c = jnp.where(sub > s, c, 0.0)
                    tile[h] = tile[h] - c * row
                    for u in range(t + 1, block):
                        column[h - g][u] = column[h - g][u] - c * right[u]
    return [
        jnp.concatenate([part * factor for part, factor in zip(tile, scale)], axis=0)
        for tile, scale in zip(tiles, scales)
    ]


def halves(value):
    high = value.astype(jnp.bfloat16)
    return high, (value - high.astype(jnp.float32)).astype(jnp.bfloat16)


def total_of(value):
    return jnp.sum(jnp.sum(value, axis=0, keepdims=True), axis=1, keepdims=True)


def parent_tile(stacked):
    lane = lanes(stacked.shape)
    c = jnp.where(lane < RANK, stacked, 0.0)
    right = jnp.where(lane < 2 * RANK, c + pltpu.roll(c, RANK, 1), eye(stacked.shape, 2 * RANK))
    tile = lax.dot_general(
        c[:, :RANK], right, (((0,), (0,)), ((), ())), precision=highest, preferred_element_type=jnp.float32
    )
    return tile, total_of(c * c)


def project(tile, stacked):
    low = lanes(tile.shape) < 2 * RANK
    high, rest = halves(tile)
    s_high, s_rest = halves(stacked)
    high = high.astype(jnp.float32)
    first = jnp.where(low, swap_halves(rest.astype(jnp.float32)), high)
    left = jnp.concatenate([first, swap_halves(high)], axis=1)[:, : 6 * RANK].astype(jnp.bfloat16)
    return dot_nn(left, jnp.concatenate([s_high, s_high, s_rest], axis=0), None)


def parents(current):
    pairs = [
        parent_tile(pltpu.roll(jnp.concatenate(current[i : i + 2], axis=0), 3 * RANK, 1))
        for i in range(0, len(current), 2)
    ]
    return compress([tile for tile, _ in pairs], [trace for _, trace in pairs])


def chain(current):
    levels = []
    while len(current) > 1:
        current = parents(current)
        levels.append(current)
    return levels


def side_by_side(first, second):
    return jnp.where(lanes(first.shape) < 2 * RANK, swap_halves(first), second)


def descriptor(src, dst, send, recv, axis, peer):
    return pltpu.make_async_remote_copy(
        src_ref=src, dst_ref=dst, send_sem=send, recv_sem=recv, device_id={axis: peer}, device_id_type=MESH
    )


PARTS = ((0, 2), (2, 1), (3, 1))


def subtree(n_cols, tiles, traces, out, send, recv):
    col = lax.axis_index("cols")
    others = [(col + k) % n_cols for k in range(1, n_cols)]
    sent = []

    def publish(part):
        rows = pl.ds(*PARTS[part])
        for k in range(n_cols - 1):
            copy = descriptor(
                out.at[col, rows], out.at[col, rows], send.at[part, k], recv.at[part, k], "cols", others[k]
            )
            copy.start()
            sent.append(copy)

    current = compress(tiles, traces)
    out[col, 0] = side_by_side(current[0], current[1])
    out[col, 1] = side_by_side(current[2], current[3])
    publish(0)
    current = parents(current)
    out[col, 2] = side_by_side(current[0], current[1])
    publish(1)
    out[col, 3] = parents(current)[0]
    publish(2)

    def collect(part):
        rows = pl.ds(*PARTS[part])
        for k in range(n_cols - 1):
            owner = (col + n_cols - k - 1) % n_cols
            descriptor(
                out.at[owner, rows], out.at[owner, rows], send.at[part, k], recv.at[part, k], "cols", others[k]
            ).wait_recv()

    def end():
        for copy in sent:
            copy.wait_send()

    return collect, end


def leaf_body(n_cols, partial, out, pieces, send_a, recv_a, send_b, recv_b):
    me = lax.axis_index("cols")
    width = partial.shape[1] // n_cols
    peers = [(me + k) % n_cols for k in range(1, n_cols)]
    greet("cols", peers)

    def piece(owner):
        return pl.ds(pl.multiple_of(owner * width, width), width)

    first = []
    for k in range(1, n_cols):
        copy = descriptor(
            partial.at[:, piece(peers[k - 1])], pieces.at[k - 1], send_a.at[k - 1], recv_a.at[k - 1], "cols", peers[k - 1]
        )
        copy.start()
        first.append(copy)
    value = partial[:, piece(me)]
    for k in range(1, n_cols):
        first[k - 1].wait_recv()
        value = value + pieces[k - 1]
    unit = eye((2 * RANK, 2 * RANK))
    bs = []
    for j in range(2):
        pair = value[:, 2 * LEAF * j : 2 * LEAF * (j + 1)]
        bs += [pair[:, :LEAF], swap_halves(pair)[:, :LEAF]]
    tiles = [dot_nt(b, jnp.concatenate([b, b, unit], axis=0)) for b in bs]
    collect, end = subtree(n_cols, tiles, [total_of(b * b) for b in bs], out, send_b, recv_b)
    for part in range(3):
        collect(part)
    for copy in first:
        copy.wait_send()
    end()


def leaf_tiles(partial, n_cols):
    rows, columns = partial.shape
    dma = pltpu.SemaphoreType.DMA
    return pl.pallas_call(
        functools.partial(leaf_body, n_cols),
        out_shape=jax.ShapeDtypeStruct((n_cols, 4, RANK, 4 * RANK), jnp.float32),
        in_specs=[whole],
        out_specs=whole,
        scratch_shapes=[VMEM((n_cols - 1, rows, columns // n_cols), jnp.float32)]
        + [dma((n_cols - 1,))] * 2
        + [dma((3, n_cols - 1))] * 2,
        compiler_params=pltpu.CompilerParams(collective_id=2, has_side_effects=True, vmem_limit_bytes=40 * MIB),
        name="leaf_tiles",
    )(partial)


def unpack(block):
    return jnp.concatenate([pltpu.roll(block, (4 * RANK - RANK * g) % (4 * RANK), 1) for g in range(4)], axis=0)


def pack(source, shift):
    quarter = lanes((8, 4 * RANK)) // RANK
    row = jnp.zeros((8, 4 * RANK), jnp.float32)
    for g in range(4):
        turned = pltpu.roll(source[8 * g : 8 * g + 8], (RANK * g - shift) % (4 * RANK), 1)
        row = jnp.where(quarter == g, turned, row)
    return row


def project_t(tile, row):
    low = lanes(tile.shape) < LEAF
    high, rest = [part.astype(jnp.float32) for part in halves(tile)]
    r_high, r_rest = [part.astype(jnp.float32) for part in halves(row)]
    left = [jnp.where(low, swap_halves(rest), high), jnp.where(low, 0.0, high)]
    right = [jnp.where(low, swap_halves(r_high), r_high), r_rest]
    return dot_nt(
        jnp.concatenate(left, axis=1).astype(jnp.bfloat16), jnp.concatenate(right, axis=1).astype(jnp.bfloat16), None
    )


def both(pair):
    return [swap_halves(pair), pair]


def climb(tiles, owner, values):
    second = both(tiles[owner, 2])
    values = [project(second[i], jnp.concatenate(values[2 * i : 2 * i + 2], axis=0)) for i in range(2)]
    return project(tiles[owner, 3], jnp.concatenate(values, axis=0))


def finish(levels, values):
    for tiles in levels:
        values = [project(tile, jnp.concatenate(values[2 * i : 2 * i + 2], axis=0)) for i, tile in enumerate(tiles)]
    return values[0]


def tree_body(
    n_leaf, n_cols, tiles, far, basis, branch, transfers, root,
    upper, samples, top_samples, chosen, packed_p, out_p,
    yc_send, yc_recv, zc_send, zc_recv, yp_send, yp_recv, zp_send, zp_recv, x_send, x_recv, own,
):
    n_y = ROWS_Y
    n_z = n_leaf // n_y
    seg = n_leaf // n_cols
    me, col = lax.axis_index("leaf"), lax.axis_index("cols")
    y, z = me // n_z, me % n_z
    across = [((y + k) % n_y) * n_z + z for k in range(1, n_y)]
    along = [y * n_z + (z + k) % n_z for k in range(1, n_z)]
    others = [(col + k) % n_cols for k in range(1, n_cols)]
    far_first = sorted(range(n_z - 1), key=lambda k: -min(k + 1, n_z - 1 - k))
    barrier = pltpu.get_barrier_semaphore()
    for peer in across + along:
        pl.semaphore_signal(barrier, inc=1, device_id={"leaf": peer}, device_id_type=MESH)
    for peer in others:
        pl.semaphore_signal(barrier, inc=1, device_id={"cols": peer}, device_id_type=MESH)

    levels = chain([tiles[c, 3] for c in range(n_cols)])
    packed_c = pack(levels[-1][0], RANK)
    pl.semaphore_wait(barrier, len(across) + len(along) + len(others))

    tree_y, tree_z = (col * seg) // n_z, (col * seg) % n_z
    slot = z % seg
    carries = z // seg == tree_z // seg
    starts = carries & (y == tree_y)

    def c_across(k):
        return descriptor(chosen.at[slot], chosen.at[slot], yc_send.at[k], yc_recv, "leaf", across[k])

    def c_along(k):
        return descriptor(chosen.at[slot], chosen.at[slot], zc_send.at[k], zc_recv.at[slot], "leaf", along[k])

    @pl.when(starts)
    def _():
        chosen[slot] = packed_c
        for k in range(n_y - 1):
            c_across(k).start()

    def lower(g, carry):
        owners = [4 * g + b for b in range(4)]
        values = []
        for c in owners:
            leaves = []
            for j in range(2):
                at = pl.ds(pl.multiple_of((2 * c + j) * 2 * LEAF, 2 * LEAF), 2 * LEAF)
                pair, rows = tiles[c, j], far[:, at]
                basis[:, at] = pair
                leaves += [project_t(q, row) for q, row in zip(both(pair), both(rows))]
            values.append(leaves)
        for c, leaves in zip(owners, values):
            samples[c] = climb(tiles, c, leaves)
        return carry

    lax.fori_loop(0, n_cols // 4, lower, 0)
    value = finish(levels, [samples[c] for c in range(n_cols)])
    branch[...] = value
    packed_p[...] = pack(jnp.concatenate([value, jnp.zeros((RANK, 3 * RANK), jnp.float32)], axis=1), 0)

    p_across = [
        descriptor(packed_p, out_p.at[z, y], yp_send.at[k], yp_recv.at[k], "leaf", across[k]) for k in range(n_y - 1)
    ]
    for copy in p_across:
        copy.start()
    mine = pltpu.make_async_copy(packed_p, out_p.at[z, y], own)
    mine.start()

    @pl.when(carries & (y != tree_y))
    def _():
        c_across(0).wait_recv()

    @pl.when(carries)
    def _():
        for k in far_first:
            c_along(k).start()

    mine.wait()
    for k in range(n_y - 1):
        other = (y + n_y - k - 1) % n_y
        descriptor(packed_p, out_p.at[z, other], yp_send.at[k], yp_recv.at[k], "leaf", across[k]).wait_recv()
    p_along = [
        descriptor(out_p.at[z], out_p.at[z], zp_send.at[k], zp_recv.at[k], "leaf", along[k]) for k in range(n_z - 1)
    ]
    for k in far_first:
        p_along[k].start()

    for i in range(seg):

        @pl.when(tree_z + i != z)
        def _():
            descriptor(chosen.at[i], chosen.at[i], zc_send.at[i], zc_recv.at[i], "leaf", along[0]).wait_recv()

    pairs = [
        parent_tile(jnp.concatenate([unpack(chosen[2 * i]), unpack(chosen[2 * i + 1])], axis=0)) for i in range(seg // 2)
    ]
    collect, end = subtree(n_cols, [tile for tile, _ in pairs], [trace for _, trace in pairs], upper, x_send, x_recv)
    collect(2)
    levels = chain([upper[c, 3] for c in range(n_cols)])
    collect(0)
    collect(1)
    for k in range(n_z - 1):
        other = (z + n_z - k - 1) % n_z
        descriptor(out_p.at[other], out_p.at[other], zp_send.at[k], zp_recv.at[k], "leaf", along[k]).wait_recv()

    def q_of(tile):
        return tile[:, : 2 * RANK]

    def higher(g, carry):
        owners = [4 * g + b for b in range(4)]
        values = []
        for c in owners:
            nodes = []
            for j in range(2):
                for i, tile in enumerate(both(upper[c, j])):
                    at = c * seg + 2 * (2 * j + i)
                    children = [unpack(out_p[(at + d) % n_z, (at + d) // n_z]) for d in range(2)]
                    nodes.append(project(tile, jnp.concatenate(children, axis=0)))
                    transfers[4 * c + 2 * j + i] = q_of(swap_halves(tile))
            values.append(nodes)
        for c, nodes in zip(owners, values):
            for i, tile in enumerate(both(upper[c, 2])):
                transfers[4 * n_cols + 2 * c + i] = q_of(swap_halves(tile))
            transfers[6 * n_cols + c] = q_of(swap_halves(upper[c, 3]))
            top_samples[c] = climb(upper, c, nodes)
        return carry

    lax.fori_loop(0, n_cols // 4, higher, 0)
    first = 7 * n_cols
    for level_tiles in levels:
        for i, tile in enumerate(level_tiles):
            transfers[first + i] = q_of(swap_halves(tile))
        first += len(level_tiles)
    root[...] = finish(levels, [top_samples[c] for c in range(n_cols)])[:, :RANK]

    @pl.when(starts)
    def _():
        for k in range(n_y - 1):
            c_across(k).wait_send()

    @pl.when(carries)
    def _():
        for k in range(n_z - 1):
            c_along(k).wait_send()

    for copy in p_across + p_along:
        copy.wait_send()
    end()


def tree(tiles, far, n_leaf, n_cols):
    n_z = n_leaf // ROWS_Y
    f32 = jnp.float32
    dma = pltpu.SemaphoreType.DMA
    return pl.pallas_call(
        functools.partial(tree_body, n_leaf, n_cols),
        out_shape=(
            jax.ShapeDtypeStruct(far.shape, f32),
            jax.ShapeDtypeStruct((RANK, RANK), f32),
            jax.ShapeDtypeStruct((n_leaf - 1, RANK, 2 * RANK), f32),
            jax.ShapeDtypeStruct((RANK, RANK), f32),
        ),
        in_specs=[whole, whole],
        out_specs=(whole, whole, whole, whole),
        scratch_shapes=[
            VMEM((n_cols, 4, RANK, 4 * RANK), f32),
            VMEM((n_cols, RANK, RANK), f32),
            VMEM((n_cols, RANK, 4 * RANK), f32),
            VMEM((n_leaf // n_cols, 8, 4 * RANK), f32),
            VMEM((8, 4 * RANK), f32),
            VMEM((n_z, ROWS_Y, 8, 4 * RANK), f32),
            dma((ROWS_Y - 1,)),
            dma,
            dma((n_z - 1,)),
            dma((n_leaf // n_cols,)),
            dma((ROWS_Y - 1,)),
            dma((ROWS_Y - 1,)),
            dma((n_z - 1,)),
            dma((n_z - 1,)),
            dma((3, n_cols - 1)),
            dma((3, n_cols - 1)),
            dma,
        ],
        compiler_params=pltpu.CompilerParams(
            collective_id=3, has_side_effects=True, vmem_limit_bytes=40 * MIB
        ),
        name="tree",
    )(tiles, far)


def on_device(n_leaf, n_cols, points, samples, sketch, far_requests, far_slots, far_count, near_mask):
    recv, local, halo = fetch(samples, points, far_requests[0], n_leaf)
    far_sample, near_sample, partial = sample(
        recv, local, halo, points, far_slots.T, far_count, near_mask.T, sketch, n_leaf
    )
    tiles = leaf_tiles(partial, n_cols)
    leaf_basis, branch_samples, top_transfer, root_sample = tree(tiles, far_sample, n_leaf, n_cols)
    return far_sample, near_sample, leaf_basis, branch_samples, jnp.swapaxes(top_transfer, 1, 2), root_sample


def solution(mesh):
    return jax.shard_map(
        functools.partial(on_device, mesh.shape["leaf"], mesh.shape["cols"]),
        mesh=mesh,
        in_specs=(
            P(None, "leaf"),
            P("cols", "leaf"),
            P(None, "cols"),
            P("leaf", None, None),
            P("leaf", None),
            P("leaf"),
            P("leaf", None),
        ),
        out_specs=(
            P("cols", "leaf"),
            P("cols", "leaf"),
            P(None, "leaf"),
            P("leaf", "cols"),
            P(),
            P(None, "cols"),
        ),
        check_vma=False,
    )
```

```python
import functools

import jax
import jax.numpy as jnp
from jax import lax
from jax.experimental import pallas as pl
from jax.experimental.pallas import tpu as pltpu
from jax.sharding import PartitionSpec as P

LEAF = 64
FAR = 16
CAP = 8
RANK = 32
NEAR = 3
SLOT_ROW = CAP
MASK_ROW = SLOT_ROW + FAR
COUNT_ROW = MASK_ROW + NEAR
ROWS_Y = 4
CELL = 16
HALF = 16
SUB = HALF * CELL + HALF * 2
MSG = CAP * CELL + CAP * 2
NODE = 24

length_scale = 0.3
shift_share = 0.05
highest = lax.Precision.HIGHEST
MESH = pl.DeviceIdType.MESH
VMEM = pltpu.VMEM
whole = pl.BlockSpec(memory_space=pltpu.VMEM)
MIB = 1 << 20


def lanes(shape):
    return lax.broadcasted_iota(jnp.int32, shape, len(shape) - 1)


def swap_halves(tile):
    return pltpu.roll(tile, 64, 1)


def dot_nt(a, b, precision=highest):
    return lax.dot_general(
        a, b, (((1,), (1,)), ((), ())), precision=precision, preferred_element_type=jnp.float32
    )


def dot_nn(a, b, precision=highest):
    return lax.dot_general(
        a, b, (((1,), (0,)), ((), ())), precision=precision, preferred_element_type=jnp.float32
    )


def halves(value):
    high = value.astype(jnp.bfloat16)
    return high, (value - high.astype(jnp.float32)).astype(jnp.bfloat16)


def columns_of(both):
    both = jnp.concatenate([both, jnp.zeros((5, 2 * LEAF), jnp.float32)], axis=0).T
    return [
        [jnp.broadcast_to(block[:, a : a + 1], (LEAF, 2 * LEAF)) for a in range(3)] for block in (both[:LEAF], both[LEAF:])
    ]


def pair_of_clusters(coordinates, first, second):
    (block_a, row_a, last_a, scale_a), (block_b, row_b, last_b, scale_b) = first, second
    low16 = lanes((CELL, 2 * LEAF)) < LEAF
    low1 = lanes((1, 2 * LEAF)) < LEAF
    x = jnp.where(low1, row_a, swap_halves(row_b))
    y = jnp.where(low1, swap_halves(row_a), row_b)
    z = jnp.where(low1, last_a, last_b)
    dx = coordinates[0] - x
    dy = coordinates[1] - y
    dz = coordinates[2] - z
    square = dx * dx + dy * dy + dz * dz
    values = jnp.exp2(square * lax.rsqrt(jnp.maximum(square, 1e-30)) * (-1.4426950408889634 / length_scale))
    block_a = block_a * scale_a
    block_b = block_b * scale_b
    rows = jnp.concatenate(
        [jnp.where(low16, block_a, swap_halves(block_b)), jnp.where(low16, swap_halves(block_a), block_b)], axis=0
    )
    return halves(values), halves(rows)


def four(coordinates, entries):
    (k0h, k0l), (s0h, s0l) = pair_of_clusters(coordinates, entries[0], entries[1])
    (k1h, k1l), (s1h, s1l) = pair_of_clusters(coordinates, entries[2], entries[3])
    left = jnp.concatenate([jnp.concatenate([s0h, s1h], axis=1), jnp.concatenate([s0l, s1l], axis=1)], axis=0)
    right = jnp.concatenate([jnp.concatenate([k0h, k1h], axis=1), jnp.concatenate([k0l, k1l], axis=1)], axis=0)
    return left, right


def fold(total):
    total = total[: 2 * CELL] + total[2 * CELL :]
    return total + swap_halves(total)


def two(first, second):
    return jnp.where(lanes((2 * CELL, 2 * LEAF)) < LEAF, fold(first), fold(second))


def greet(axis, peers):
    barrier = pltpu.get_barrier_semaphore()
    for peer in peers:
        pl.semaphore_signal(barrier, inc=1, device_id={axis: peer}, device_id_type=MESH)
    pl.semaphore_wait(barrier, len(peers))


def fetch_body(
    n_leaf, samples, points, table, recv, close, *scratch
):
    n_y = ROWS_Y
    n_z = n_leaf // n_y
    chunks = scratch[:n_z]
    local = chunks[0]
    scalars, cells, halo, stage, edge, asked_v, asked, ring_send, ring_recv, y_send, y_recv, q_send, q_recv, q_local, e_send, e_recv, start_sem = scratch[n_z:]
    me = lax.axis_index("leaf")
    y, z = me // n_z, me % n_z
    up = y * n_z + (z + 1) % n_z
    down = y * n_z + (z + n_z - 1) % n_z
    above, below = (me + 1) % n_leaf, (me + n_leaf - 1) % n_leaf
    across = [None] + [((y + k) % n_y) * n_z + z for k in range(1, n_y)]
    leaves = samples.shape[1] // LEAF
    read = pltpu.make_async_copy(table, scalars, start_sem)
    read.start()
    greet("leaf", [up, down, above, below] + across[1:])
    own = table.at[pl.ds(0, CAP)]

    def remote(src, dst, send, recv_sem, peer):
        return pltpu.make_async_remote_copy(
            src_ref=src, dst_ref=dst, send_sem=send, recv_sem=recv_sem,
            device_id={"leaf": peer}, device_id_type=MESH,
        )

    sent = []
    asks = []
    for k in range(1, n_y):
        copy = remote(
            own, asked_v.at[n_y - k - 1], q_send.at[k - 1], q_recv.at[n_y - k - 1], across[k]
        )
        copy.start()
        asks.append(copy)
    sent += asks

    low = lanes((CELL, 2 * LEAF)) < LEAF
    for j in range(HALF):
        top = samples[0:CELL, 2 * LEAF * j : 2 * LEAF * (j + 1)]
        bottom = samples[CELL : 2 * CELL, 2 * LEAF * j : 2 * LEAF * (j + 1)]
        base = (2 * j // HALF) * SUB + (2 * j % HALF) * CELL
        local[base : base + CELL, :] = jnp.where(low, top, swap_halves(bottom))
        local[base + CELL : base + 2 * CELL, :] = jnp.where(low, swap_halves(top), bottom)
    low1 = lanes((1, 2 * LEAF)) < LEAF
    for j in range(HALF):
        xs, ys, zs = [points[a : a + 1, 2 * LEAF * j : 2 * LEAF * (j + 1)] for a in range(3)]
        base = (2 * j // HALF) * SUB + HALF * CELL + (2 * j % HALF) * 2
        local[base : base + 1, :] = jnp.where(low1, xs, swap_halves(ys))
        local[base + 1 : base + 2, :] = jnp.where(low1, zs, swap_halves(zs))
        local[base + 2 : base + 3, :] = jnp.where(low1, swap_halves(xs), ys)
        local[base + 3 : base + 4, :] = jnp.where(low1, swap_halves(zs), zs)

    hops = {(0, 0): n_z // 2, (0, 1): n_z // 2 - 1, (1, 0): n_z // 2 - 1, (1, 1): n_z // 2}

    def ring(way, part, step):
        here, there = (step, step + 1) if way == 0 else ((n_z - step) % n_z, n_z - step - 1)
        rows = pl.ds(part * SUB, SUB)
        return remote(
            chunks[here].at[rows], chunks[there].at[rows], ring_send.at[way, part, step],
            ring_recv.at[way, part, step], up if way == 0 else down,
        )

    def forward(way, part, step):
        if step < hops[way, part]:
            copy = ring(way, part, step)
            copy.start()
            sent.append(copy)

    order = ((0, 0), (1, 1), (0, 1), (1, 0))
    for way, part in order:
        forward(way, part, 0)

    for side, cluster in ((0, 0), (1, 2 * HALF - 1)):
        base = (cluster // HALF) * SUB + (cluster % HALF) * CELL
        cbase = (cluster // HALF) * SUB + HALF * CELL + (cluster % HALF) * 2
        edge[side, 0:CELL, :] = local[base : base + CELL, :]
        edge[side, CELL : CELL + 2, :] = local[cbase : cbase + 2, :]
        edge[side, CELL + 2 : NODE, :] = jnp.zeros((NODE - CELL - 2, 2 * LEAF), jnp.float32)
    edges = [
        remote(edge.at[0], halo.at[1], e_send.at[0], e_recv.at[1], below),
        remote(edge.at[1], halo.at[0], e_send.at[1], e_recv.at[0], above),
    ]
    for copy in edges:
        copy.start()
    sent += edges

    for copy in asks:
        copy.wait_recv()
    moves = [read, pltpu.make_async_copy(asked_v, asked, q_local)]
    moves[1].start()
    for move in moves:
        move.wait()

    def pick(chunk, target, request):
        def one(c, carry):
            cluster = request(c)
            upper = cluster >> (HALF.bit_length() - 1)
            cell = cluster + upper * (SUB // CELL - HALF)
            row = HALF * CELL + cluster * 2 + upper * (SUB - 2 * HALF)
            target[pl.ds(pl.multiple_of(c * CELL, CELL), CELL), :] = chunk[pl.ds(cell * CELL, CELL), :]
            for part in range(2):
                target[pl.ds(CAP * CELL + c * 2 + part, 1), :] = chunk[pl.ds(row + part, 1), :]
            return carry

        lax.fori_loop(0, CAP, one, 0)

    arriving = []

    def select(slot):
        chunk = chunks[slot]
        source_z = (z + n_z - slot) % n_z

        def requests(k):
            return lambda c: (asked[k - 1, c, y * n_z + source_z] if k else scalars[c, y * n_z + source_z])

        for k in range(1, n_y):
            pick(chunk, stage.at[k - 1, slot], requests(k))
            copy = remote(
                stage.at[k - 1, slot], recv.at[k * n_z + slot], y_send.at[k - 1, slot], y_recv.at[k - 1, slot], across[k]
            )
            copy.start()
            sent.append(copy)
            arriving.append(copy)
        pick(chunk, recv.at[slot], requests(0))

    for c in range(leaves):
        base = (c // HALF) * SUB + (c % HALF) * CELL
        cbase = (c // HALF) * SUB + HALF * CELL + (c % HALF) * 2
        cells[c + 1, 0:CELL, :] = local[base : base + CELL, :]
        cells[c + 1, CELL : CELL + 2, :] = local[cbase : cbase + 2, :]

    def near_entry(leaf, offset):
        if offset < NEAR:
            place = me * leaves + leaf + offset - NEAR // 2
            inside = (place >= 0) & (place < n_leaf * leaves)
            scale = (scalars[MASK_ROW + offset, leaf] * inside.astype(jnp.int32)).astype(jnp.float32)
        else:
            scale = jnp.float32(0)
        at = leaf + offset if offset < NEAR else leaf
        return cells[at, 0:CELL, :], cells[at, CELL : CELL + 1, :], cells[at, CELL + 1 : CELL + 2, :], scale

    def near_pair(j, carry):
        at = pl.ds(pl.multiple_of(j * 2 * LEAF, 2 * LEAF), 2 * LEAF)
        coordinates = columns_of(points[:, at])
        totals = []
        for i in range(2):
            left, right = four(coordinates[i], [near_entry(2 * j + i, o) for o in range(4)])
            totals.append(dot_nt(left, right, None))
        close[:, at] = two(*totals)
        return carry

    def near_share(step):
        if step == 2:
            for copy in edges:
                copy.wait_recv()
            cells[0] = halo[0]
            cells[leaves + 1] = halo[1]
        pairs = leaves // 2
        share = -(-pairs // (n_z // 2 - 2))
        lax.fori_loop(min(pairs, (step - 2) * share), min(pairs, (step - 1) * share), near_pair, 0)

    select(0)
    for step in range(1, n_z // 2 + 1):
        for way, part in order:
            if step - 1 < hops[way, part]:
                ring(way, part, step - 1).wait_recv()
                forward(way, part, step)
        select(step)
        if step < n_z // 2:
            select(n_z - step)
        if step >= 2:
            near_share(step)
    for copy in arriving:
        copy.wait_recv()
    for copy in sent:
        copy.wait_send()


def fetch(samples, points, table, n_leaf):
    n_z = n_leaf // ROWS_Y
    rows = samples.shape[0]
    leaves = samples.shape[1] // LEAF
    dma = pltpu.SemaphoreType.DMA
    f32 = jnp.float32
    return pl.pallas_call(
        functools.partial(fetch_body, n_leaf),
        out_shape=(
            jax.ShapeDtypeStruct((n_leaf, MSG, 2 * LEAF), f32),
            jax.ShapeDtypeStruct(samples.shape, f32),
        ),
        in_specs=[whole] * 3,
        out_specs=(whole, whole),
        scratch_shapes=[VMEM((2 * SUB, 2 * LEAF), f32)] * n_z
        + [
            pltpu.SMEM(table.shape, jnp.int32),
            VMEM((leaves + 2, NODE, 2 * LEAF), f32),
            VMEM((2, NODE, 2 * LEAF), f32),
            VMEM((ROWS_Y - 1, n_z, MSG, 2 * LEAF), f32),
            VMEM((2, NODE, 2 * LEAF), f32),
            VMEM((ROWS_Y - 1, CAP, table.shape[1]), jnp.int32),
            pltpu.SMEM((ROWS_Y - 1, CAP, table.shape[1]), jnp.int32),
            dma((2, 2, n_z // 2)),
            dma((2, 2, n_z // 2)),
            dma((ROWS_Y - 1, n_z)),
            dma((ROWS_Y - 1, n_z)),
            dma((ROWS_Y - 1,)),
            dma((ROWS_Y - 1,)),
            dma,
            dma((2,)),
            dma((2,)),
            dma,
        ],
        compiler_params=pltpu.CompilerParams(
            collective_id=1, has_side_effects=True, vmem_limit_bytes=40 * MIB
        ),
        name="fetch",
    )(samples, points, table)


def sample_body(
    leaves, n_leaf, recv, near_in, points, table, sketch, far_out, near_out, partial_out, far_again, scalars, sem
):
    move = pltpu.make_async_copy(table, scalars, sem)
    move.start()
    near_out[...] = near_in[...]
    n_z = n_leaf // ROWS_Y
    me = lax.axis_index("leaf")
    y, z = me // n_z, me % n_z
    move.wait()

    def far_entry(leaf, f, count):
        slot = scalars[SLOT_ROW + f, leaf]
        owner = slot >> 3
        message = ((y - owner // n_z) & (ROWS_Y - 1)) * n_z + ((z - owner) & (n_z - 1))
        c = slot & (CAP - 1)
        scale = jnp.where(f < count, 1.0, 0.0).astype(jnp.float32)
        return (
            recv[message, pl.ds(pl.multiple_of(c * CELL, CELL), CELL), :],
            recv[message, pl.ds(CAP * CELL + 2 * c, 1), :],
            recv[message, pl.ds(CAP * CELL + 2 * c + 1, 1), :],
            scale,
        )

    def two_leaves(j, carry):
        pair_of = (2 * j, 2 * j + 1)
        at = pl.ds(pl.multiple_of(j * 2 * LEAF, 2 * LEAF), 2 * LEAF)
        coordinates = columns_of(points[:, at])
        count = [scalars[COUNT_ROW, leaf] for leaf in pair_of]

        def operands(g):
            return [
                four(coordinates[i], [far_entry(pair_of[i], 4 * g + b, count[i]) for b in range(4)]) for i in range(2)
            ]

        def step(g, carried):
            totals, waiting = carried
            totals = [total + dot_nt(left, right, None) for total, (left, right) in zip(totals, waiting)]
            return totals, operands(g)

        zero = jnp.zeros((LEAF, 2 * LEAF), jnp.float32)
        steps = (jnp.maximum(count[0], count[1]) + 3) // 4
        totals, waiting = lax.fori_loop(1, steps, step, ([zero, zero], operands(0)))
        far = [total + dot_nt(left, right, None) for total, (left, right) in zip(totals, waiting)]
        far = two(*far)
        far_out[:, at] = far
        far_again[:, at] = far
        partial_out[:, at] = dot_nn(sketch[...], far)
        return carry

    lax.fori_loop(0, leaves // 2, two_leaves, 0)


def sample(recv, near, points, table, sketch, n_leaf):
    leaves = points.shape[1] // LEAF
    shape = jax.ShapeDtypeStruct((RANK, leaves * LEAF), jnp.float32)
    return pl.pallas_call(
        functools.partial(sample_body, leaves, n_leaf),
        out_shape=(shape, shape, shape, shape),
        in_specs=[whole] * 5,
        out_specs=(whole, whole, whole, whole),
        scratch_shapes=[
            pltpu.SMEM(table.shape, jnp.int32),
            pltpu.SemaphoreType.DMA,
        ],
        compiler_params=pltpu.CompilerParams(vmem_limit_bytes=40 * MIB),
        name="sample",
    )(recv, near, points, table, sketch)


def eye(shape, first=0):
    rows = lax.broadcasted_iota(jnp.int32, shape, 0)
    return jnp.where(lanes(shape) == rows + first, 1.0, 0.0).astype(jnp.float32)


def inverse(value):
    guess = pl.reciprocal(value, approx=True)
    return guess * (2.0 - value * guess)


def compress(tiles, traces):
    block = 8
    shape = (RANK, 4 * RANK)
    on_diagonal = lanes(shape) == lax.broadcasted_iota(jnp.int32, shape, 0)
    tiles = [
        tile + jnp.where(on_diagonal, shift_share * trace / RANK + 1e-06, 0.0) for tile, trace in zip(tiles, traces)
    ]
    tiles = [[tile[8 * g : 8 * g + 8] for g in range(4)] for tile in tiles]
    full = (8, 4 * RANK)
    sub = lax.broadcasted_iota(jnp.int32, full, 0)
    scales = [[jnp.zeros(full, jnp.float32) for g in range(4)] for tile in tiles]
    for first in range(0, RANK, block):
        g = first // 8
        columns = [
            [[jnp.broadcast_to(part[:, first + t : first + t + 1], full) for t in range(block)] for part in tile[g:]]
            for tile in tiles
        ]
        for t in range(block):
            s = (first + t) % 8
            for tile, column, scale in zip(tiles, columns, scales):
                pivot = jnp.broadcast_to(column[0][t][s : s + 1], full)
                inv = inverse(pivot)
                scale[g] = jnp.where(sub == s, lax.rsqrt(pivot), scale[g])
                row = jnp.broadcast_to(tile[g][s : s + 1], full)
                right = [None] * block
                for u in range(t + 1, block):
                    right[u] = jnp.broadcast_to(column[0][u][s : s + 1], full)
                for h in range(g, 4):
                    c = column[h - g][t]
                    if h == g:
                        if s == 7:
                            continue
                        c = jnp.where(sub > s, c, 0.0)
                    tile[h] = tile[h] - (c * row) * inv
                    for u in range(t + 1, block):
                        column[h - g][u] = column[h - g][u] - (c * right[u]) * inv
    return [
        jnp.concatenate([part * factor for part, factor in zip(tile, scale)], axis=0)
        for tile, scale in zip(tiles, scales)
    ]


def total_of(value):
    return jnp.sum(jnp.sum(value, axis=0, keepdims=True), axis=1, keepdims=True)


def parent_tile(stacked):
    lane = lanes(stacked.shape)
    c = jnp.where(lane < RANK, stacked, 0.0)
    right = jnp.where(lane < 2 * RANK, c + pltpu.roll(c, RANK, 1), eye(stacked.shape, 2 * RANK))
    tile = lax.dot_general(
        c[:, :RANK], right, (((0,), (0,)), ((), ())), precision=highest, preferred_element_type=jnp.float32
    )
    return tile, total_of(c * c)


def project(tile, stacked):
    low = lanes(tile.shape) < 2 * RANK
    high, rest = halves(tile)
    s_high, s_rest = halves(stacked)
    high = high.astype(jnp.float32)
    first = jnp.where(low, swap_halves(rest.astype(jnp.float32)), high)
    left = jnp.concatenate([first, swap_halves(high)], axis=1)[:, : 6 * RANK].astype(jnp.bfloat16)
    return dot_nn(left, jnp.concatenate([s_high, s_high, s_rest], axis=0), None)


def parents(current):
    pairs = [
        parent_tile(pltpu.roll(jnp.concatenate(current[i : i + 2], axis=0), 3 * RANK, 1))
        for i in range(0, len(current), 2)
    ]
    return compress([tile for tile, _ in pairs], [trace for _, trace in pairs])


def chain(current):
    levels = []
    while len(current) > 1:
        current = parents(current)
        levels.append(current)
    return levels


def side_by_side(first, second):
    return jnp.where(lanes(first.shape) < 2 * RANK, swap_halves(first), second)


def descriptor(src, dst, send, recv, axis, peer):
    return pltpu.make_async_remote_copy(
        src_ref=src, dst_ref=dst, send_sem=send, recv_sem=recv, device_id={axis: peer}, device_id_type=MESH
    )


PARTS = ((0, 2), (2, 1), (3, 1))


def subtree(n_cols, tiles, traces, out, send, recv):
    col = lax.axis_index("cols")
    others = [(col + k) % n_cols for k in range(1, n_cols)]
    sent = []

    def publish(part):
        rows = pl.ds(*PARTS[part])
        for k in range(n_cols - 1):
            copy = descriptor(
                out.at[col, rows], out.at[col, rows], send.at[part, k], recv.at[part, k], "cols", others[k]
            )
            copy.start()
            sent.append(copy)

    current = compress(tiles, traces)
    out[col, 0] = side_by_side(current[0], current[1])
    out[col, 1] = side_by_side(current[2], current[3])
    publish(0)
    current = parents(current)
    out[col, 2] = side_by_side(current[0], current[1])
    publish(1)
    out[col, 3] = parents(current)[0]
    publish(2)

    def collect(part):
        rows = pl.ds(*PARTS[part])
        for k in range(n_cols - 1):
            owner = (col + n_cols - k - 1) % n_cols
            descriptor(
                out.at[owner, rows], out.at[owner, rows], send.at[part, k], recv.at[part, k], "cols", others[k]
            ).wait_recv()

    def end():
        for copy in sent:
            copy.wait_send()

    return collect, end


def leaf_body(n_cols, partial, out, pieces, send_a, recv_a, send_b, recv_b):
    me = lax.axis_index("cols")
    width = partial.shape[1] // n_cols
    peers = [(me + k) % n_cols for k in range(1, n_cols)]
    greet("cols", peers)

    def piece(owner):
        return pl.ds(pl.multiple_of(owner * width, width), width)

    first = []
    for k in range(1, n_cols):
        copy = descriptor(
            partial.at[:, piece(peers[k - 1])], pieces.at[k - 1], send_a.at[k - 1], recv_a.at[k - 1], "cols", peers[k - 1]
        )
        copy.start()
        first.append(copy)
    value = partial[:, piece(me)]
    for k in range(1, n_cols):
        first[k - 1].wait_recv()
        value = value + pieces[k - 1]
    unit = eye((2 * RANK, 2 * RANK))
    bs = []
    for j in range(2):
        pair = value[:, 2 * LEAF * j : 2 * LEAF * (j + 1)]
        bs += [pair[:, :LEAF], swap_halves(pair)[:, :LEAF]]
    tiles = [dot_nt(b, jnp.concatenate([b, b, unit], axis=0)) for b in bs]
    collect, end = subtree(n_cols, tiles, [total_of(b * b) for b in bs], out, send_b, recv_b)
    for part in range(3):
        collect(part)
    for copy in first:
        copy.wait_send()
    end()


def leaf_tiles(partial, n_cols):
    rows, columns = partial.shape
    dma = pltpu.SemaphoreType.DMA
    return pl.pallas_call(
        functools.partial(leaf_body, n_cols),
        out_shape=jax.ShapeDtypeStruct((n_cols, 4, RANK, 4 * RANK), jnp.float32),
        in_specs=[whole],
        out_specs=whole,
        scratch_shapes=[VMEM((n_cols - 1, rows, columns // n_cols), jnp.float32)]
        + [dma((n_cols - 1,))] * 2
        + [dma((3, n_cols - 1))] * 2,
        compiler_params=pltpu.CompilerParams(collective_id=2, has_side_effects=True, vmem_limit_bytes=40 * MIB),
        name="leaf_tiles",
    )(partial)


def unpack(block):
    return jnp.concatenate([pltpu.roll(block, (4 * RANK - RANK * g) % (4 * RANK), 1) for g in range(4)], axis=0)


def pack(source, shift):
    quarter = lanes((8, 4 * RANK)) // RANK
    row = jnp.zeros((8, 4 * RANK), jnp.float32)
    for g in range(4):
        turned = pltpu.roll(source[8 * g : 8 * g + 8], (RANK * g - shift) % (4 * RANK), 1)
        row = jnp.where(quarter == g, turned, row)
    return row


def project_t(tile, row):
    low = lanes(tile.shape) < LEAF
    high, rest = [part.astype(jnp.float32) for part in halves(tile)]
    r_high, r_rest = [part.astype(jnp.float32) for part in halves(row)]
    left = [jnp.where(low, swap_halves(rest), high), jnp.where(low, 0.0, high)]
    right = [jnp.where(low, swap_halves(r_high), r_high), r_rest]
    return dot_nt(
        jnp.concatenate(left, axis=1).astype(jnp.bfloat16), jnp.concatenate(right, axis=1).astype(jnp.bfloat16), None
    )


def both(pair):
    return [swap_halves(pair), pair]


def climb(tiles, owner, values):
    second = both(tiles[owner, 2])
    values = [project(second[i], jnp.concatenate(values[2 * i : 2 * i + 2], axis=0)) for i in range(2)]
    return project(tiles[owner, 3], jnp.concatenate(values, axis=0))


def finish(levels, values):
    for tiles in levels:
        values = [project(tile, jnp.concatenate(values[2 * i : 2 * i + 2], axis=0)) for i, tile in enumerate(tiles)]
    return values[0]


def tree_body(
    n_leaf, n_cols, tiles, far, basis, branch, transfers, root,
    upper, samples, top_samples, chosen, packed_p, out_p,
    yc_send, yc_recv, zc_send, zc_recv, yp_send, yp_recv, zp_send, zp_recv, x_send, x_recv, own,
):
    n_y = ROWS_Y
    n_z = n_leaf // n_y
    seg = n_leaf // n_cols
    me, col = lax.axis_index("leaf"), lax.axis_index("cols")
    y, z = me // n_z, me % n_z
    across = [((y + k) % n_y) * n_z + z for k in range(1, n_y)]
    along = [y * n_z + (z + k) % n_z for k in range(1, n_z)]
    others = [(col + k) % n_cols for k in range(1, n_cols)]
    far_first = sorted(range(n_z - 1), key=lambda k: -min(k + 1, n_z - 1 - k))
    barrier = pltpu.get_barrier_semaphore()
    for peer in across + along:
        pl.semaphore_signal(barrier, inc=1, device_id={"leaf": peer}, device_id_type=MESH)
    for peer in others:
        pl.semaphore_signal(barrier, inc=1, device_id={"cols": peer}, device_id_type=MESH)

    levels = chain([tiles[c, 3] for c in range(n_cols)])
    packed_c = pack(levels[-1][0], RANK)
    pl.semaphore_wait(barrier, len(across) + len(along) + len(others))

    tree_y, tree_z = (col * seg) // n_z, (col * seg) % n_z
    slot = z % seg
    carries = z // seg == tree_z // seg
    starts = carries & (y == tree_y)

    def c_across(k):
        return descriptor(chosen.at[slot], chosen.at[slot], yc_send.at[k], yc_recv, "leaf", across[k])

    def c_along(k):
        return descriptor(chosen.at[slot], chosen.at[slot], zc_send.at[k], zc_recv.at[slot], "leaf", along[k])

    @pl.when(starts)
    def _():
        chosen[slot] = packed_c
        for k in range(n_y - 1):
            c_across(k).start()

    def lower(g, carry):
        owners = [4 * g + b for b in range(4)]
        values = []
        for c in owners:
            leaves = []
            for j in range(2):
                at = pl.ds(pl.multiple_of((2 * c + j) * 2 * LEAF, 2 * LEAF), 2 * LEAF)
                pair, rows = tiles[c, j], far[:, at]
                basis[:, at] = pair
                leaves += [project_t(q, row) for q, row in zip(both(pair), both(rows))]
            values.append(leaves)
        for c, leaves in zip(owners, values):
            samples[c] = climb(tiles, c, leaves)
        return carry

    lax.fori_loop(0, n_cols // 4, lower, 0)
    value = finish(levels, [samples[c] for c in range(n_cols)])
    branch[...] = value
    packed_p[...] = pack(jnp.concatenate([value, jnp.zeros((RANK, 3 * RANK), jnp.float32)], axis=1), 0)

    p_across = [
        descriptor(packed_p, out_p.at[z, y], yp_send.at[k], yp_recv.at[k], "leaf", across[k]) for k in range(n_y - 1)
    ]
    for copy in p_across:
        copy.start()
    mine = pltpu.make_async_copy(packed_p, out_p.at[z, y], own)
    mine.start()

    @pl.when(carries & (y != tree_y))
    def _():
        c_across(0).wait_recv()

    @pl.when(carries)
    def _():
        for k in far_first:
            c_along(k).start()

    mine.wait()
    for k in range(n_y - 1):
        other = (y + n_y - k - 1) % n_y
        descriptor(packed_p, out_p.at[z, other], yp_send.at[k], yp_recv.at[k], "leaf", across[k]).wait_recv()
    p_along = [
        descriptor(out_p.at[z], out_p.at[z], zp_send.at[k], zp_recv.at[k], "leaf", along[k]) for k in range(n_z - 1)
    ]
    for k in far_first:
        p_along[k].start()

    for i in range(seg):

        @pl.when(tree_z + i != z)
        def _():
            descriptor(chosen.at[i], chosen.at[i], zc_send.at[i], zc_recv.at[i], "leaf", along[0]).wait_recv()

    pairs = [
        parent_tile(jnp.concatenate([unpack(chosen[2 * i]), unpack(chosen[2 * i + 1])], axis=0)) for i in range(seg // 2)
    ]
    collect, end = subtree(n_cols, [tile for tile, _ in pairs], [trace for _, trace in pairs], upper, x_send, x_recv)
    collect(2)
    levels = chain([upper[c, 3] for c in range(n_cols)])
    collect(0)
    collect(1)
    for k in range(n_z - 1):
        other = (z + n_z - k - 1) % n_z
        descriptor(out_p.at[other], out_p.at[other], zp_send.at[k], zp_recv.at[k], "leaf", along[k]).wait_recv()

    def q_of(tile):
        return tile[:, : 2 * RANK]

    def higher(g, carry):
        owners = [4 * g + b for b in range(4)]
        values = []
        for c in owners:
            nodes = []
            for j in range(2):
                for i, tile in enumerate(both(upper[c, j])):
                    at = c * seg + 2 * (2 * j + i)
                    children = [unpack(out_p[(at + d) % n_z, (at + d) // n_z]) for d in range(2)]
                    nodes.append(project(tile, jnp.concatenate(children, axis=0)))
                    transfers[4 * c + 2 * j + i] = q_of(swap_halves(tile))
            values.append(nodes)
        for c, nodes in zip(owners, values):
            for i, tile in enumerate(both(upper[c, 2])):
                transfers[4 * n_cols + 2 * c + i] = q_of(swap_halves(tile))
            transfers[6 * n_cols + c] = q_of(swap_halves(upper[c, 3]))
            top_samples[c] = climb(upper, c, nodes)
        return carry

    lax.fori_loop(0, n_cols // 4, higher, 0)
    first = 7 * n_cols
    for level_tiles in levels:
        for i, tile in enumerate(level_tiles):
            transfers[first + i] = q_of(swap_halves(tile))
        first += len(level_tiles)
    root[...] = finish(levels, [top_samples[c] for c in range(n_cols)])[:, :RANK]

    @pl.when(starts)
    def _():
        for k in range(n_y - 1):
            c_across(k).wait_send()

    @pl.when(carries)
    def _():
        for k in range(n_z - 1):
            c_along(k).wait_send()

    for copy in p_across + p_along:
        copy.wait_send()
    end()


def tree(tiles, far, n_leaf, n_cols):
    n_z = n_leaf // ROWS_Y
    f32 = jnp.float32
    dma = pltpu.SemaphoreType.DMA
    return pl.pallas_call(
        functools.partial(tree_body, n_leaf, n_cols),
        out_shape=(
            jax.ShapeDtypeStruct(far.shape, f32),
            jax.ShapeDtypeStruct((RANK, RANK), f32),
            jax.ShapeDtypeStruct((n_leaf - 1, RANK, 2 * RANK), f32),
            jax.ShapeDtypeStruct((RANK, RANK), f32),
        ),
        in_specs=[whole, whole],
        out_specs=(whole, whole, whole, whole),
        scratch_shapes=[
            VMEM((n_cols, 4, RANK, 4 * RANK), f32),
            VMEM((n_cols, RANK, RANK), f32),
            VMEM((n_cols, RANK, 4 * RANK), f32),
            VMEM((n_leaf // n_cols, 8, 4 * RANK), f32),
            VMEM((8, 4 * RANK), f32),
            VMEM((n_z, ROWS_Y, 8, 4 * RANK), f32),
            dma((ROWS_Y - 1,)),
            dma,
            dma((n_z - 1,)),
            dma((n_leaf // n_cols,)),
            dma((ROWS_Y - 1,)),
            dma((ROWS_Y - 1,)),
            dma((n_z - 1,)),
            dma((n_z - 1,)),
            dma((3, n_cols - 1)),
            dma((3, n_cols - 1)),
            dma,
        ],
        compiler_params=pltpu.CompilerParams(
            collective_id=3, has_side_effects=True, vmem_limit_bytes=40 * MIB
        ),
        name="tree",
    )(tiles, far)


def on_device(n_leaf, n_cols, points, samples, sketch, far_requests, far_slots, far_count, near_mask):
    table = jnp.concatenate(
        [
            jnp.pad(rows, ((0, 0), (0, 2 * LEAF - rows.shape[1])))
            for rows in (far_requests[0].T, far_slots.T, near_mask.T, far_count[None], jnp.zeros((4, LEAF), jnp.int32))
        ],
        axis=0,
    )
    recv, close = fetch(samples, points, table, n_leaf)
    far_sample, near_sample, partial, far_again = sample(recv, close, points, table, sketch, n_leaf)
    tiles = leaf_tiles(partial, n_cols)
    leaf_basis, branch_samples, top_transfer, root_sample = tree(tiles, far_again, n_leaf, n_cols)
    return far_sample, near_sample, leaf_basis, branch_samples, jnp.swapaxes(top_transfer, 1, 2), root_sample


def solution(mesh):
    return jax.shard_map(
        functools.partial(on_device, mesh.shape["leaf"], mesh.shape["cols"]),
        mesh=mesh,
        in_specs=(
            P(None, "leaf"),
            P("cols", "leaf"),
            P(None, "cols"),
            P("leaf", None, None),
            P("leaf", None),
            P("leaf"),
            P("leaf", None),
        ),
        out_specs=(
            P("cols", "leaf"),
            P("cols", "leaf"),
            P(None, "leaf"),
            P("leaf", "cols"),
            P(),
            P(None, "cols"),
        ),
        check_vma=False,
    )
```

```python
import functools

import jax
import jax.numpy as jnp
from jax import lax
from jax.experimental import pallas as pl
from jax.experimental.pallas import tpu as pltpu
from jax.sharding import PartitionSpec as P

LEAF = 64
FAR = 16
CAP = 8
RANK = 32
NEAR = 3
SLOT_ROW = CAP
MASK_ROW = SLOT_ROW + FAR
COUNT_ROW = MASK_ROW + NEAR
ROWS_Y = 4
CELL = 16
HALF = 16
SUB = HALF * CELL + HALF * 2
MSG = CAP * CELL + CAP * 2
NODE = 24

length_scale = 0.3
shift_share = 0.05
highest = lax.Precision.HIGHEST
MESH = pl.DeviceIdType.MESH
VMEM = pltpu.VMEM
whole = pl.BlockSpec(memory_space=pltpu.VMEM)
MIB = 1 << 20


def lanes(shape):
    return lax.broadcasted_iota(jnp.int32, shape, len(shape) - 1)


def swap_halves(tile):
    return pltpu.roll(tile, 64, 1)


def dot_nt(a, b, precision=highest):
    return lax.dot_general(
        a, b, (((1,), (1,)), ((), ())), precision=precision, preferred_element_type=jnp.float32
    )


def dot_nn(a, b, precision=highest):
    return lax.dot_general(
        a, b, (((1,), (0,)), ((), ())), precision=precision, preferred_element_type=jnp.float32
    )


def halves(value):
    high = value.astype(jnp.bfloat16)
    return high, (value - high.astype(jnp.float32)).astype(jnp.bfloat16)


def columns_of(both):
    both = jnp.concatenate([both, jnp.zeros((5, 2 * LEAF), jnp.float32)], axis=0).T
    return [
        [jnp.broadcast_to(block[:, a : a + 1], (LEAF, 2 * LEAF)) for a in range(3)] for block in (both[:LEAF], both[LEAF:])
    ]


def pair_of_clusters(coordinates, first, second):
    (block_a, row_a, last_a, scale_a), (block_b, row_b, last_b, scale_b) = first, second
    low16 = lanes((CELL, 2 * LEAF)) < LEAF
    low1 = lanes((1, 2 * LEAF)) < LEAF
    x = jnp.where(low1, row_a, swap_halves(row_b))
    y = jnp.where(low1, swap_halves(row_a), row_b)
    z = jnp.where(low1, last_a, last_b)
    dx = coordinates[0] - x
    dy = coordinates[1] - y
    dz = coordinates[2] - z
    square = dx * dx + dy * dy + dz * dz
    values = jnp.exp2(square * lax.rsqrt(jnp.maximum(square, 1e-30)) * (-1.4426950408889634 / length_scale))
    block_a = block_a * scale_a
    block_b = block_b * scale_b
    rows = jnp.concatenate(
        [jnp.where(low16, block_a, swap_halves(block_b)), jnp.where(low16, swap_halves(block_a), block_b)], axis=0
    )
    return halves(values), halves(rows)


def four(coordinates, entries):
    (k0h, k0l), (s0h, s0l) = pair_of_clusters(coordinates, entries[0], entries[1])
    (k1h, k1l), (s1h, s1l) = pair_of_clusters(coordinates, entries[2], entries[3])
    left = jnp.concatenate([jnp.concatenate([s0h, s1h], axis=1), jnp.concatenate([s0l, s1l], axis=1)], axis=0)
    right = jnp.concatenate([jnp.concatenate([k0h, k1h], axis=1), jnp.concatenate([k0l, k1l], axis=1)], axis=0)
    return left, right


def fold(total):
    total = total[: 2 * CELL] + total[2 * CELL :]
    return total + swap_halves(total)


def two(first, second):
    return jnp.where(lanes((2 * CELL, 2 * LEAF)) < LEAF, fold(first), fold(second))


def greet(axis, peers):
    barrier = pltpu.get_barrier_semaphore()
    for peer in peers:
        pl.semaphore_signal(barrier, inc=1, device_id={axis: peer}, device_id_type=MESH)
    pl.semaphore_wait(barrier, len(peers))


def fetch_body(
    n_leaf, samples, points, table, recv, close, columns, *scratch
):
    n_y = ROWS_Y
    n_z = n_leaf // n_y
    chunks = scratch[:n_z]
    local = chunks[0]
    scalars, cells, halo, stage, edge, asked_v, asked, ring_send, ring_recv, y_send, y_recv, q_send, q_recv, q_local, e_send, e_recv, start_sem = scratch[n_z:]
    me = lax.axis_index("leaf")
    y, z = me // n_z, me % n_z
    up = y * n_z + (z + 1) % n_z
    down = y * n_z + (z + n_z - 1) % n_z
    above, below = (me + 1) % n_leaf, (me + n_leaf - 1) % n_leaf
    across = [None] + [((y + k) % n_y) * n_z + z for k in range(1, n_y)]
    leaves = samples.shape[1] // LEAF
    read = pltpu.make_async_copy(table, scalars, start_sem)
    read.start()
    greet("leaf", [up, down, above, below] + across[1:])
    own = table.at[pl.ds(0, CAP)]

    def remote(src, dst, send, recv_sem, peer):
        return pltpu.make_async_remote_copy(
            src_ref=src, dst_ref=dst, send_sem=send, recv_sem=recv_sem,
            device_id={"leaf": peer}, device_id_type=MESH,
        )

    sent = []
    asks = []
    for k in range(1, n_y):
        copy = remote(
            own, asked_v.at[n_y - k - 1], q_send.at[k - 1], q_recv.at[n_y - k - 1], across[k]
        )
        copy.start()
        asks.append(copy)
    sent += asks

    low = lanes((CELL, 2 * LEAF)) < LEAF
    for j in range(HALF):
        top = samples[0:CELL, 2 * LEAF * j : 2 * LEAF * (j + 1)]
        bottom = samples[CELL : 2 * CELL, 2 * LEAF * j : 2 * LEAF * (j + 1)]
        base = (2 * j // HALF) * SUB + (2 * j % HALF) * CELL
        local[base : base + CELL, :] = jnp.where(low, top, swap_halves(bottom))
        local[base + CELL : base + 2 * CELL, :] = jnp.where(low, swap_halves(top), bottom)
    low1 = lanes((1, 2 * LEAF)) < LEAF
    for j in range(HALF):
        xs, ys, zs = [points[a : a + 1, 2 * LEAF * j : 2 * LEAF * (j + 1)] for a in range(3)]
        base = (2 * j // HALF) * SUB + HALF * CELL + (2 * j % HALF) * 2
        local[base : base + 1, :] = jnp.where(low1, xs, swap_halves(ys))
        local[base + 1 : base + 2, :] = jnp.where(low1, zs, swap_halves(zs))
        local[base + 2 : base + 3, :] = jnp.where(low1, swap_halves(xs), ys)
        local[base + 3 : base + 4, :] = jnp.where(low1, swap_halves(zs), zs)

    hops = {(0, 0): n_z // 2, (0, 1): n_z // 2 - 1, (1, 0): n_z // 2 - 1, (1, 1): n_z // 2}

    def ring(way, part, step):
        here, there = (step, step + 1) if way == 0 else ((n_z - step) % n_z, n_z - step - 1)
        rows = pl.ds(part * SUB, SUB)
        return remote(
            chunks[here].at[rows], chunks[there].at[rows], ring_send.at[way, part, step],
            ring_recv.at[way, part, step], up if way == 0 else down,
        )

    def forward(way, part, step):
        if step < hops[way, part]:
            copy = ring(way, part, step)
            copy.start()
            sent.append(copy)

    order = ((0, 0), (1, 1), (0, 1), (1, 0))
    for way, part in order:
        forward(way, part, 0)

    for side, cluster in ((0, 0), (1, 2 * HALF - 1)):
        base = (cluster // HALF) * SUB + (cluster % HALF) * CELL
        cbase = (cluster // HALF) * SUB + HALF * CELL + (cluster % HALF) * 2
        edge[side, 0:CELL, :] = local[base : base + CELL, :]
        edge[side, CELL : CELL + 2, :] = local[cbase : cbase + 2, :]
        edge[side, CELL + 2 : NODE, :] = jnp.zeros((NODE - CELL - 2, 2 * LEAF), jnp.float32)
    edges = [
        remote(edge.at[0], halo.at[1], e_send.at[0], e_recv.at[1], below),
        remote(edge.at[1], halo.at[0], e_send.at[1], e_recv.at[0], above),
    ]
    for copy in edges:
        copy.start()
    sent += edges

    for copy in asks:
        copy.wait_recv()
    moves = [read, pltpu.make_async_copy(asked_v, asked, q_local)]
    moves[1].start()
    for move in moves:
        move.wait()

    def pick(chunk, target, request):
        def one(c, carry):
            cluster = request(c)
            upper = cluster >> (HALF.bit_length() - 1)
            cell = cluster + upper * (SUB // CELL - HALF)
            row = HALF * CELL + cluster * 2 + upper * (SUB - 2 * HALF)
            target[pl.ds(pl.multiple_of(c * CELL, CELL), CELL), :] = chunk[pl.ds(cell * CELL, CELL), :]
            for part in range(2):
                target[pl.ds(CAP * CELL + c * 2 + part, 1), :] = chunk[pl.ds(row + part, 1), :]
            return carry

        lax.fori_loop(0, CAP, one, 0)

    arriving = []

    def select(slot):
        chunk = chunks[slot]
        source_z = (z + n_z - slot) % n_z

        def requests(k):
            return lambda c: (asked[k - 1, c, y * n_z + source_z] if k else scalars[c, y * n_z + source_z])

        for k in range(1, n_y):
            pick(chunk, stage.at[k - 1, slot], requests(k))
            copy = remote(
                stage.at[k - 1, slot], recv.at[k * n_z + slot], y_send.at[k - 1, slot], y_recv.at[k - 1, slot], across[k]
            )
            copy.start()
            sent.append(copy)
            arriving.append(copy)
        pick(chunk, recv.at[slot], requests(0))

    for c in range(leaves):
        base = (c // HALF) * SUB + (c % HALF) * CELL
        cbase = (c // HALF) * SUB + HALF * CELL + (c % HALF) * 2
        cells[c + 1, 0:CELL, :] = local[base : base + CELL, :]
        cells[c + 1, CELL : CELL + 2, :] = local[cbase : cbase + 2, :]

    def near_entry(leaf, offset):
        if offset < NEAR:
            place = me * leaves + leaf + offset - NEAR // 2
            inside = (place >= 0) & (place < n_leaf * leaves)
            scale = (scalars[MASK_ROW + offset, leaf] * inside.astype(jnp.int32)).astype(jnp.float32)
        else:
            scale = jnp.float32(0)
        at = leaf + offset if offset < NEAR else leaf
        return cells[at, 0:CELL, :], cells[at, CELL : CELL + 1, :], cells[at, CELL + 1 : CELL + 2, :], scale

    def near_pair(j, carry):
        at = pl.ds(pl.multiple_of(j * 2 * LEAF, 2 * LEAF), 2 * LEAF)
        coordinates = columns_of(points[:, at])
        for i in range(2):
            for a in range(3):
                columns[2 * j + i, a] = coordinates[i][a]
        totals = []
        for i in range(2):
            left, right = four(coordinates[i], [near_entry(2 * j + i, o) for o in range(4)])
            totals.append(dot_nt(left, right, None))
        close[:, at] = two(*totals)
        return carry

    def near_share(step):
        if step == 2:
            for copy in edges:
                copy.wait_recv()
            cells[0] = halo[0]
            cells[leaves + 1] = halo[1]
        pairs = leaves // 2
        share = -(-pairs // (n_z // 2 - 2))
        lax.fori_loop(min(pairs, (step - 2) * share), min(pairs, (step - 1) * share), near_pair, 0)

    select(0)
    for step in range(1, n_z // 2 + 1):
        for way, part in order:
            if step - 1 < hops[way, part]:
                ring(way, part, step - 1).wait_recv()
                forward(way, part, step)
        select(step)
        if step < n_z // 2:
            select(n_z - step)
        if step >= 2:
            near_share(step)
    for copy in arriving:
        copy.wait_recv()
    for copy in sent:
        copy.wait_send()


def fetch(samples, points, table, n_leaf):
    n_z = n_leaf // ROWS_Y
    rows = samples.shape[0]
    leaves = samples.shape[1] // LEAF
    dma = pltpu.SemaphoreType.DMA
    f32 = jnp.float32
    return pl.pallas_call(
        functools.partial(fetch_body, n_leaf),
        out_shape=(
            jax.ShapeDtypeStruct((n_leaf, MSG, 2 * LEAF), f32),
            jax.ShapeDtypeStruct(samples.shape, f32),
            jax.ShapeDtypeStruct((leaves, 3, LEAF, 2 * LEAF), f32),
        ),
        in_specs=[whole] * 3,
        out_specs=(whole, whole, whole),
        scratch_shapes=[VMEM((2 * SUB, 2 * LEAF), f32)] * n_z
        + [
            pltpu.SMEM(table.shape, jnp.int32),
            VMEM((leaves + 2, NODE, 2 * LEAF), f32),
            VMEM((2, NODE, 2 * LEAF), f32),
            VMEM((ROWS_Y - 1, n_z, MSG, 2 * LEAF), f32),
            VMEM((2, NODE, 2 * LEAF), f32),
            VMEM((ROWS_Y - 1, CAP, table.shape[1]), jnp.int32),
            pltpu.SMEM((ROWS_Y - 1, CAP, table.shape[1]), jnp.int32),
            dma((2, 2, n_z // 2)),
            dma((2, 2, n_z // 2)),
            dma((ROWS_Y - 1, n_z)),
            dma((ROWS_Y - 1, n_z)),
            dma((ROWS_Y - 1,)),
            dma((ROWS_Y - 1,)),
            dma,
            dma((2,)),
            dma((2,)),
            dma,
        ],
        compiler_params=pltpu.CompilerParams(
            collective_id=1, has_side_effects=True, vmem_limit_bytes=40 * MIB
        ),
        name="fetch",
    )(samples, points, table)


def sample_body(
    leaves, n_leaf, recv, near_in, columns, table, sketch, far_out, near_out, partial_out, far_again, totals, scalars, sem
):
    move = pltpu.make_async_copy(table, scalars, sem)
    move.start()
    near_out[...] = near_in[...]
    totals[...] = jnp.zeros(totals.shape, jnp.float32)
    n_z = n_leaf // ROWS_Y
    me = lax.axis_index("leaf")
    y, z = me // n_z, me % n_z
    move.wait()

    def far_entry(leaf, f, count):
        slot = scalars[SLOT_ROW + f, leaf]
        owner = slot >> 3
        message = ((y - owner // n_z) & (ROWS_Y - 1)) * n_z + ((z - owner) & (n_z - 1))
        c = slot & (CAP - 1)
        scale = jnp.where(f < count, 1.0, 0.0).astype(jnp.float32)
        return (
            recv[message, pl.ds(pl.multiple_of(c * CELL, CELL), CELL), :],
            recv[message, pl.ds(CAP * CELL + 2 * c, 1), :],
            recv[message, pl.ds(CAP * CELL + 2 * c + 1, 1), :],
            scale,
        )

    def steps_of(leaf):
        return (scalars[COUNT_ROW, leaf] + 3) // 4

    def operands(leaf, g):
        count = scalars[COUNT_ROW, leaf]
        place = jnp.minimum(leaf, leaves - 1)
        coordinates = [columns[place, a] for a in range(3)]
        return four(coordinates, [far_entry(leaf, 4 * g + b, count) for b in range(4)])

    def following(leaf, g):
        last = g + 1 >= steps_of(leaf)
        return jnp.where(last, jnp.minimum(leaf + 1, leaves), leaf), jnp.where(last, 0, g + 1)

    def work(leaf, g):
        second = following(leaf, g)
        return following(*second), (leaf, second[0]), (operands(leaf, g), operands(*second))

    def add(places, waiting):
        for place, (left, right) in zip(places, waiting):
            totals[place] += dot_nt(left, right, None)

    def turn(t, carried):
        at, places, waiting = carried
        add(places, waiting)
        return work(*at)

    zero = jnp.int32(0)
    steps = lax.fori_loop(0, leaves, lambda leaf, total: total + steps_of(leaf), zero)
    at, places, waiting = lax.fori_loop(1, (steps + 1) // 2, turn, work(zero, zero))
    add(places, waiting)
    for j in range(leaves // 2):
        at = pl.ds(j * 2 * LEAF, 2 * LEAF)
        far = two(totals[2 * j], totals[2 * j + 1])
        far_out[:, at] = far
        far_again[:, at] = far
        partial_out[:, at] = dot_nn(sketch[...], far)


def sample(recv, near, columns, table, sketch, n_leaf):
    leaves = columns.shape[0]
    shape = jax.ShapeDtypeStruct((RANK, leaves * LEAF), jnp.float32)
    return pl.pallas_call(
        functools.partial(sample_body, leaves, n_leaf),
        out_shape=(shape, shape, shape, shape),
        in_specs=[whole] * 5,
        out_specs=(whole, whole, whole, whole),
        scratch_shapes=[
            VMEM((leaves + 1, LEAF, 2 * LEAF), jnp.float32),
            pltpu.SMEM(table.shape, jnp.int32),
            pltpu.SemaphoreType.DMA,
        ],
        compiler_params=pltpu.CompilerParams(vmem_limit_bytes=40 * MIB),
        name="sample",
    )(recv, near, columns, table, sketch)


def eye(shape, first=0):
    rows = lax.broadcasted_iota(jnp.int32, shape, 0)
    return jnp.where(lanes(shape) == rows + first, 1.0, 0.0).astype(jnp.float32)


def inverse(value):
    guess = pl.reciprocal(value, approx=True)
    return guess * (2.0 - value * guess)


def compress(tiles, traces):
    block = 8
    shape = (RANK, 4 * RANK)
    on_diagonal = lanes(shape) == lax.broadcasted_iota(jnp.int32, shape, 0)
    tiles = [
        tile + jnp.where(on_diagonal, shift_share * trace / RANK + 1e-06, 0.0) for tile, trace in zip(tiles, traces)
    ]
    tiles = [[tile[8 * g : 8 * g + 8] for g in range(4)] for tile in tiles]
    full = (8, 4 * RANK)
    sub = lax.broadcasted_iota(jnp.int32, full, 0)
    scales = [[jnp.zeros(full, jnp.float32) for g in range(4)] for tile in tiles]
    for first in range(0, RANK, block):
        g = first // 8
        columns = [
            [[jnp.broadcast_to(part[:, first + t : first + t + 1], full) for t in range(block)] for part in tile[g:]]
            for tile in tiles
        ]
        for t in range(block):
            s = (first + t) % 8
            for tile, column, scale in zip(tiles, columns, scales):
                pivot = jnp.broadcast_to(column[0][t][s : s + 1], full)
                inv = inverse(pivot)
                scale[g] = jnp.where(sub == s, lax.rsqrt(pivot), scale[g])
                row = jnp.broadcast_to(tile[g][s : s + 1], full)
                right = [None] * block
                for u in range(t + 1, block):
                    right[u] = jnp.broadcast_to(column[0][u][s : s + 1], full)
                for h in range(g, 4):
                    c = column[h - g][t]
                    if h == g:
                        if s == 7:
                            continue
                        c = jnp.where(sub > s, c, 0.0)
                    tile[h] = tile[h] - (c * row) * inv
                    for u in range(t + 1, block):
                        column[h - g][u] = column[h - g][u] - (c * right[u]) * inv
    return [
        jnp.concatenate([part * factor for part, factor in zip(tile, scale)], axis=0)
        for tile, scale in zip(tiles, scales)
    ]


def total_of(value):
    return jnp.sum(jnp.sum(value, axis=0, keepdims=True), axis=1, keepdims=True)


def parent_tile(stacked):
    lane = lanes(stacked.shape)
    c = jnp.where(lane < RANK, stacked, 0.0)
    right = jnp.where(lane < 2 * RANK, c + pltpu.roll(c, RANK, 1), eye(stacked.shape, 2 * RANK))
    tile = lax.dot_general(
        c[:, :RANK], right, (((0,), (0,)), ((), ())), precision=highest, preferred_element_type=jnp.float32
    )
    return tile, total_of(c * c)


def project(tile, stacked):
    low = lanes(tile.shape) < 2 * RANK
    high, rest = halves(tile)
    s_high, s_rest = halves(stacked)
    high = high.astype(jnp.float32)
    first = jnp.where(low, swap_halves(rest.astype(jnp.float32)), high)
    left = jnp.concatenate([first, swap_halves(high)], axis=1)[:, : 6 * RANK].astype(jnp.bfloat16)
    return dot_nn(left, jnp.concatenate([s_high, s_high, s_rest], axis=0), None)


def parents(current):
    pairs = [
        parent_tile(pltpu.roll(jnp.concatenate(current[i : i + 2], axis=0), 3 * RANK, 1))
        for i in range(0, len(current), 2)
    ]
    return compress([tile for tile, _ in pairs], [trace for _, trace in pairs])


def chain(current):
    levels = []
    while len(current) > 1:
        current = parents(current)
        levels.append(current)
    return levels


def side_by_side(first, second):
    return jnp.where(lanes(first.shape) < 2 * RANK, swap_halves(first), second)


def descriptor(src, dst, send, recv, axis, peer):
    return pltpu.make_async_remote_copy(
        src_ref=src, dst_ref=dst, send_sem=send, recv_sem=recv, device_id={axis: peer}, device_id_type=MESH
    )


PARTS = ((0, 2), (2, 1), (3, 1))


def subtree(n_cols, tiles, traces, out, send, recv):
    col = lax.axis_index("cols")
    others = [(col + k) % n_cols for k in range(1, n_cols)]
    sent = []

    def publish(part):
        rows = pl.ds(*PARTS[part])
        for k in range(n_cols - 1):
            copy = descriptor(
                out.at[col, rows], out.at[col, rows], send.at[part, k], recv.at[part, k], "cols", others[k]
            )
            copy.start()
            sent.append(copy)

    current = compress(tiles, traces)
    out[col, 0] = side_by_side(current[0], current[1])
    out[col, 1] = side_by_side(current[2], current[3])
    publish(0)
    current = parents(current)
    out[col, 2] = side_by_side(current[0], current[1])
    publish(1)
    out[col, 3] = parents(current)[0]
    publish(2)

    def collect(part):
        rows = pl.ds(*PARTS[part])
        for k in range(n_cols - 1):
            owner = (col + n_cols - k - 1) % n_cols
            descriptor(
                out.at[owner, rows], out.at[owner, rows], send.at[part, k], recv.at[part, k], "cols", others[k]
            ).wait_recv()

    def end():
        for copy in sent:
            copy.wait_send()

    return collect, end


def leaf_body(n_cols, partial, out, pieces, send_a, recv_a, send_b, recv_b):
    me = lax.axis_index("cols")
    width = partial.shape[1] // n_cols
    peers = [(me + k) % n_cols for k in range(1, n_cols)]
    greet("cols", peers)

    def piece(owner):
        return pl.ds(pl.multiple_of(owner * width, width), width)

    first = []
    for k in range(1, n_cols):
        copy = descriptor(
            partial.at[:, piece(peers[k - 1])], pieces.at[k - 1], send_a.at[k - 1], recv_a.at[k - 1], "cols", peers[k - 1]
        )
        copy.start()
        first.append(copy)
    value = partial[:, piece(me)]
    for k in range(1, n_cols):
        first[k - 1].wait_recv()
        value = value + pieces[k - 1]
    unit = eye((2 * RANK, 2 * RANK))
    bs = []
    for j in range(2):
        pair = value[:, 2 * LEAF * j : 2 * LEAF * (j + 1)]
        bs += [pair[:, :LEAF], swap_halves(pair)[:, :LEAF]]
    tiles = [dot_nt(b, jnp.concatenate([b, b, unit], axis=0)) for b in bs]
    collect, end = subtree(n_cols, tiles, [total_of(b * b) for b in bs], out, send_b, recv_b)
    for part in range(3):
        collect(part)
    for copy in first:
        copy.wait_send()
    end()


def leaf_tiles(partial, n_cols):
    rows, columns = partial.shape
    dma = pltpu.SemaphoreType.DMA
    return pl.pallas_call(
        functools.partial(leaf_body, n_cols),
        out_shape=jax.ShapeDtypeStruct((n_cols, 4, RANK, 4 * RANK), jnp.float32),
        in_specs=[whole],
        out_specs=whole,
        scratch_shapes=[VMEM((n_cols - 1, rows, columns // n_cols), jnp.float32)]
        + [dma((n_cols - 1,))] * 2
        + [dma((3, n_cols - 1))] * 2,
        compiler_params=pltpu.CompilerParams(collective_id=2, has_side_effects=True, vmem_limit_bytes=40 * MIB),
        name="leaf_tiles",
    )(partial)


def unpack(block):
    return jnp.concatenate([pltpu.roll(block, (4 * RANK - RANK * g) % (4 * RANK), 1) for g in range(4)], axis=0)


def pack(source, shift):
    quarter = lanes((8, 4 * RANK)) // RANK
    row = jnp.zeros((8, 4 * RANK), jnp.float32)
    for g in range(4):
        turned = pltpu.roll(source[8 * g : 8 * g + 8], (RANK * g - shift) % (4 * RANK), 1)
        row = jnp.where(quarter == g, turned, row)
    return row


def project_t(tile, row):
    low = lanes(tile.shape) < LEAF
    high, rest = [part.astype(jnp.float32) for part in halves(tile)]
    r_high, r_rest = [part.astype(jnp.float32) for part in halves(row)]
    left = [jnp.where(low, swap_halves(rest), high), jnp.where(low, 0.0, high)]
    right = [jnp.where(low, swap_halves(r_high), r_high), r_rest]
    return dot_nt(
        jnp.concatenate(left, axis=1).astype(jnp.bfloat16), jnp.concatenate(right, axis=1).astype(jnp.bfloat16), None
    )


def both(pair):
    return [swap_halves(pair), pair]


def climb(tiles, owner, values):
    second = both(tiles[owner, 2])
    values = [project(second[i], jnp.concatenate(values[2 * i : 2 * i + 2], axis=0)) for i in range(2)]
    return project(tiles[owner, 3], jnp.concatenate(values, axis=0))


def finish(levels, values):
    for tiles in levels:
        values = [project(tile, jnp.concatenate(values[2 * i : 2 * i + 2], axis=0)) for i, tile in enumerate(tiles)]
    return values[0]


def tree_body(
    n_leaf, n_cols, tiles, far, basis, branch, transfers, root,
    upper, chosen, packed_p, out_p,
    yc_send, yc_recv, zc_send, zc_recv, yp_send, yp_recv, zp_send, zp_recv, x_send, x_recv, own,
):
    n_y = ROWS_Y
    n_z = n_leaf // n_y
    seg = n_leaf // n_cols
    me, col = lax.axis_index("leaf"), lax.axis_index("cols")
    y, z = me // n_z, me % n_z
    across = [((y + k) % n_y) * n_z + z for k in range(1, n_y)]
    along = [y * n_z + (z + k) % n_z for k in range(1, n_z)]
    others = [(col + k) % n_cols for k in range(1, n_cols)]
    far_first = sorted(range(n_z - 1), key=lambda k: -min(k + 1, n_z - 1 - k))
    barrier = pltpu.get_barrier_semaphore()
    for peer in across + along:
        pl.semaphore_signal(barrier, inc=1, device_id={"leaf": peer}, device_id_type=MESH)
    for peer in others:
        pl.semaphore_signal(barrier, inc=1, device_id={"cols": peer}, device_id_type=MESH)

    levels = chain([tiles[c, 3] for c in range(n_cols)])
    packed_c = pack(levels[-1][0], RANK)

    values = []
    for c in range(n_cols):
        leaves = []
        for j in range(2):
            at = pl.ds((2 * c + j) * 2 * LEAF, 2 * LEAF)
            pair, rows = tiles[c, j], far[:, at]
            basis[:, at] = pair
            leaves += [project_t(q, row) for q, row in zip(both(pair), both(rows))]
        values.append(leaves)
    values = [climb(tiles, c, leaves) for c, leaves in enumerate(values)]
    pl.semaphore_wait(barrier, len(across) + len(along) + len(others))

    tree_y, tree_z = (col * seg) // n_z, (col * seg) % n_z
    slot = z % seg
    carries = z // seg == tree_z // seg
    starts = carries & (y == tree_y)

    def c_across(k):
        return descriptor(chosen.at[slot], chosen.at[slot], yc_send.at[k], yc_recv, "leaf", across[k])

    def c_along(k):
        return descriptor(chosen.at[slot], chosen.at[slot], zc_send.at[k], zc_recv.at[slot], "leaf", along[k])

    @pl.when(starts)
    def _():
        chosen[slot] = packed_c
        for k in range(n_y - 1):
            c_across(k).start()

    value = finish(levels, values)
    branch[...] = value
    packed_p[...] = pack(jnp.concatenate([value, jnp.zeros((RANK, 3 * RANK), jnp.float32)], axis=1), 0)

    p_across = [
        descriptor(packed_p, out_p.at[z, y], yp_send.at[k], yp_recv.at[k], "leaf", across[k]) for k in range(n_y - 1)
    ]
    for copy in p_across:
        copy.start()
    mine = pltpu.make_async_copy(packed_p, out_p.at[z, y], own)
    mine.start()

    @pl.when(carries & (y != tree_y))
    def _():
        c_across(0).wait_recv()

    @pl.when(carries)
    def _():
        for k in far_first:
            c_along(k).start()

    mine.wait()
    for k in range(n_y - 1):
        other = (y + n_y - k - 1) % n_y
        descriptor(packed_p, out_p.at[z, other], yp_send.at[k], yp_recv.at[k], "leaf", across[k]).wait_recv()
    p_along = [
        descriptor(out_p.at[z], out_p.at[z], zp_send.at[k], zp_recv.at[k], "leaf", along[k]) for k in range(n_z - 1)
    ]
    for k in far_first:
        p_along[k].start()

    for i in range(seg):

        @pl.when(tree_z + i != z)
        def _():
            descriptor(chosen.at[i], chosen.at[i], zc_send.at[i], zc_recv.at[i], "leaf", along[0]).wait_recv()

    pairs = [
        parent_tile(jnp.concatenate([unpack(chosen[2 * i]), unpack(chosen[2 * i + 1])], axis=0)) for i in range(seg // 2)
    ]
    collect, end = subtree(n_cols, [tile for tile, _ in pairs], [trace for _, trace in pairs], upper, x_send, x_recv)
    for part in (0, 1, 2):
        collect(part)
    for k in range(n_z - 1):
        other = (z + n_z - k - 1) % n_z
        descriptor(out_p.at[other], out_p.at[other], zp_send.at[k], zp_recv.at[k], "leaf", along[k]).wait_recv()

    def q_of(tile):
        return swap_halves(tile)[:, : 2 * RANK]

    levels = chain([upper[c, 3] for c in range(n_cols)])
    values = []
    for c in range(n_cols):
        nodes = []
        for j in range(2):
            for i, tile in enumerate(both(upper[c, j])):
                at = c * seg + 2 * (2 * j + i)
                children = [unpack(out_p[(at + d) % n_z, (at + d) // n_z]) for d in range(2)]
                nodes.append(project(tile, jnp.concatenate(children, axis=0)))
                transfers[4 * c + 2 * j + i] = q_of(tile)
        values.append(nodes)
        for i, tile in enumerate(both(upper[c, 2])):
            transfers[4 * n_cols + 2 * c + i] = q_of(tile)
        transfers[6 * n_cols + c] = q_of(upper[c, 3])
    values = [climb(upper, c, nodes) for c, nodes in enumerate(values)]
    first = 7 * n_cols
    for level_tiles in levels:
        for i, tile in enumerate(level_tiles):
            transfers[first + i] = q_of(tile)
        first += len(level_tiles)
    root[...] = finish(levels, values)[:, :RANK]

    @pl.when(starts)
    def _():
        for k in range(n_y - 1):
            c_across(k).wait_send()

    @pl.when(carries)
    def _():
        for k in range(n_z - 1):
            c_along(k).wait_send()

    for copy in p_across + p_along:
        copy.wait_send()
    end()


def tree(tiles, far, n_leaf, n_cols):
    n_z = n_leaf // ROWS_Y
    f32 = jnp.float32
    dma = pltpu.SemaphoreType.DMA
    return pl.pallas_call(
        functools.partial(tree_body, n_leaf, n_cols),
        out_shape=(
            jax.ShapeDtypeStruct(far.shape, f32),
            jax.ShapeDtypeStruct((RANK, RANK), f32),
            jax.ShapeDtypeStruct((n_leaf - 1, RANK, 2 * RANK), f32),
            jax.ShapeDtypeStruct((RANK, RANK), f32),
        ),
        in_specs=[whole, whole],
        out_specs=(whole, whole, whole, whole),
        scratch_shapes=[
            VMEM((n_cols, 4, RANK, 4 * RANK), f32),
            VMEM((n_leaf // n_cols, 8, 4 * RANK), f32),
            VMEM((8, 4 * RANK), f32),
            VMEM((n_z, ROWS_Y, 8, 4 * RANK), f32),
            dma((ROWS_Y - 1,)),
            dma,
            dma((n_z - 1,)),
            dma((n_leaf // n_cols,)),
            dma((ROWS_Y - 1,)),
            dma((ROWS_Y - 1,)),
            dma((n_z - 1,)),
            dma((n_z - 1,)),
            dma((3, n_cols - 1)),
            dma((3, n_cols - 1)),
            dma,
        ],
        compiler_params=pltpu.CompilerParams(
            collective_id=3, has_side_effects=True, vmem_limit_bytes=40 * MIB
        ),
        name="tree",
    )(tiles, far)


def on_device(n_leaf, n_cols, points, samples, sketch, far_requests, far_slots, far_count, near_mask):
    table = jnp.zeros((32, 2 * LEAF), jnp.int32)
    for row, block in ((0, far_requests[0].T), (SLOT_ROW, far_slots.T), (MASK_ROW, near_mask.T), (COUNT_ROW, far_count[None])):
        table += jnp.pad(block, ((row, 32 - row - block.shape[0]), (0, 2 * LEAF - block.shape[1])))
    recv, close, columns = fetch(samples, points, table, n_leaf)
    far_sample, near_sample, partial, far_again = sample(recv, close, columns, table, sketch, n_leaf)
    tiles = leaf_tiles(partial, n_cols)
    leaf_basis, branch_samples, top_transfer, root_sample = tree(tiles, far_again, n_leaf, n_cols)
    return far_sample, near_sample, leaf_basis, branch_samples, jnp.swapaxes(top_transfer, 1, 2), root_sample


def solution(mesh):
    return jax.shard_map(
        functools.partial(on_device, mesh.shape["leaf"], mesh.shape["cols"]),
        mesh=mesh,
        in_specs=(
            P(None, "leaf"),
            P("cols", "leaf"),
            P(None, "cols"),
            P("leaf", None, None),
            P("leaf", None),
            P("leaf"),
            P("leaf", None),
        ),
        out_specs=(
            P("cols", "leaf"),
            P("cols", "leaf"),
            P(None, "leaf"),
            P("leaf", "cols"),
            P(),
            P(None, "cols"),
        ),
        check_vma=False,
    )
```

```python
import functools

import jax
import jax.numpy as jnp
from jax import lax
from jax.experimental import pallas as pl
from jax.experimental.pallas import tpu as pltpu
from jax.sharding import PartitionSpec as P

LEAF = 64
FAR = 16
CAP = 8
RANK = 32
NEAR = 3
SLOT_ROW = CAP
MASK_ROW = SLOT_ROW + FAR
COUNT_ROW = MASK_ROW + NEAR
ROWS_Y = 4
CELL = 16
HALF = 16
SUB = HALF * CELL + HALF * 2
MSG = CAP * CELL + CAP * 2
NODE = 24

length_scale = 0.3
shift_share = 0.05
highest = lax.Precision.HIGHEST
MESH = pl.DeviceIdType.MESH
VMEM = pltpu.VMEM
whole = pl.BlockSpec(memory_space=pltpu.VMEM)
MIB = 1 << 20


def lanes(shape):
    return lax.broadcasted_iota(jnp.int32, shape, len(shape) - 1)


def swap_halves(tile):
    return pltpu.roll(tile, 64, 1)


def dot_nt(a, b, precision=highest):
    return lax.dot_general(
        a, b, (((1,), (1,)), ((), ())), precision=precision, preferred_element_type=jnp.float32
    )


def dot_nn(a, b, precision=highest):
    return lax.dot_general(
        a, b, (((1,), (0,)), ((), ())), precision=precision, preferred_element_type=jnp.float32
    )


def halves(value):
    high = value.astype(jnp.bfloat16)
    return high, (value - high.astype(jnp.float32)).astype(jnp.bfloat16)


def columns_of(both):
    both = jnp.concatenate([both, jnp.zeros((5, 2 * LEAF), jnp.float32)], axis=0).T
    return [
        [jnp.broadcast_to(block[:, a : a + 1], (LEAF, 2 * LEAF)) for a in range(3)] for block in (both[:LEAF], both[LEAF:])
    ]


def pair_of_clusters(coordinates, first, second):
    (block_a, row_a, last_a, scale_a), (block_b, row_b, last_b, scale_b) = first, second
    low16 = lanes((CELL, 2 * LEAF)) < LEAF
    low1 = lanes((1, 2 * LEAF)) < LEAF
    x = jnp.where(low1, row_a, swap_halves(row_b))
    y = jnp.where(low1, swap_halves(row_a), row_b)
    z = jnp.where(low1, last_a, last_b)
    dx = coordinates[0] - x
    dy = coordinates[1] - y
    dz = coordinates[2] - z
    square = dx * dx + dy * dy + dz * dz
    values = jnp.exp2(square * lax.rsqrt(jnp.maximum(square, 1e-30)) * (-1.4426950408889634 / length_scale))
    block_a = block_a * scale_a
    block_b = block_b * scale_b
    rows = jnp.concatenate(
        [jnp.where(low16, block_a, swap_halves(block_b)), jnp.where(low16, swap_halves(block_a), block_b)], axis=0
    )
    return halves(values), halves(rows)


def four(coordinates, entries):
    (k0h, k0l), (s0h, s0l) = pair_of_clusters(coordinates, entries[0], entries[1])
    (k1h, k1l), (s1h, s1l) = pair_of_clusters(coordinates, entries[2], entries[3])
    left = jnp.concatenate([jnp.concatenate([s0h, s1h], axis=1), jnp.concatenate([s0l, s1l], axis=1)], axis=0)
    right = jnp.concatenate([jnp.concatenate([k0h, k1h], axis=1), jnp.concatenate([k0l, k1l], axis=1)], axis=0)
    return left, right


def fold(total):
    total = total[: 2 * CELL] + total[2 * CELL :]
    return total + swap_halves(total)


def two(first, second):
    return jnp.where(lanes((2 * CELL, 2 * LEAF)) < LEAF, fold(first), fold(second))


def greet(axis, peers):
    barrier = pltpu.get_barrier_semaphore()
    for peer in peers:
        pl.semaphore_signal(barrier, inc=1, device_id={axis: peer}, device_id_type=MESH)
    return lambda: pl.semaphore_wait(barrier, len(peers))


def fetch_body(
    n_leaf, samples, points, table, recv, close, columns, *scratch
):
    n_y = ROWS_Y
    n_z = n_leaf // n_y
    chunks = scratch[:n_z]
    local = chunks[0]
    scalars, cells, halo, stage, edge, asked_v, asked, ring_send, ring_recv, y_send, y_recv, q_send, q_recv, q_local, e_send, e_recv, start_sem = scratch[n_z:]
    me = lax.axis_index("leaf")
    y, z = me // n_z, me % n_z
    up = y * n_z + (z + 1) % n_z
    down = y * n_z + (z + n_z - 1) % n_z
    above, below = (me + 1) % n_leaf, (me + n_leaf - 1) % n_leaf
    across = [None] + [((y + k) % n_y) * n_z + z for k in range(1, n_y)]
    leaves = samples.shape[1] // LEAF
    read = pltpu.make_async_copy(table, scalars, start_sem)
    read.start()
    greet("leaf", [up, down, above, below] + across[1:])()
    own = table.at[pl.ds(0, CAP)]

    def remote(src, dst, send, recv_sem, peer):
        return pltpu.make_async_remote_copy(
            src_ref=src, dst_ref=dst, send_sem=send, recv_sem=recv_sem,
            device_id={"leaf": peer}, device_id_type=MESH,
        )

    sent = []
    asks = []
    for k in range(1, n_y):
        copy = remote(
            own, asked_v.at[n_y - k - 1], q_send.at[k - 1], q_recv.at[n_y - k - 1], across[k]
        )
        copy.start()
        asks.append(copy)
    sent += asks

    low = lanes((CELL, 2 * LEAF)) < LEAF
    for j in range(HALF):
        top = samples[0:CELL, 2 * LEAF * j : 2 * LEAF * (j + 1)]
        bottom = samples[CELL : 2 * CELL, 2 * LEAF * j : 2 * LEAF * (j + 1)]
        base = (2 * j // HALF) * SUB + (2 * j % HALF) * CELL
        local[base : base + CELL, :] = jnp.where(low, top, swap_halves(bottom))
        local[base + CELL : base + 2 * CELL, :] = jnp.where(low, swap_halves(top), bottom)
    low1 = lanes((1, 2 * LEAF)) < LEAF
    for j in range(HALF):
        xs, ys, zs = [points[a : a + 1, 2 * LEAF * j : 2 * LEAF * (j + 1)] for a in range(3)]
        base = (2 * j // HALF) * SUB + HALF * CELL + (2 * j % HALF) * 2
        local[base : base + 1, :] = jnp.where(low1, xs, swap_halves(ys))
        local[base + 1 : base + 2, :] = jnp.where(low1, zs, swap_halves(zs))
        local[base + 2 : base + 3, :] = jnp.where(low1, swap_halves(xs), ys)
        local[base + 3 : base + 4, :] = jnp.where(low1, swap_halves(zs), zs)

    hops = {(0, 0): n_z // 2, (0, 1): n_z // 2 - 1, (1, 0): n_z // 2 - 1, (1, 1): n_z // 2}

    def ring(way, part, step):
        here, there = (step, step + 1) if way == 0 else ((n_z - step) % n_z, n_z - step - 1)
        rows = pl.ds(part * SUB, SUB)
        return remote(
            chunks[here].at[rows], chunks[there].at[rows], ring_send.at[way, part, step],
            ring_recv.at[way, part, step], up if way == 0 else down,
        )

    def forward(way, part, step):
        if step < hops[way, part]:
            copy = ring(way, part, step)
            copy.start()
            sent.append(copy)

    order = ((0, 0), (1, 1), (0, 1), (1, 0))
    for way, part in order:
        forward(way, part, 0)

    for side, cluster in ((0, 0), (1, 2 * HALF - 1)):
        base = (cluster // HALF) * SUB + (cluster % HALF) * CELL
        cbase = (cluster // HALF) * SUB + HALF * CELL + (cluster % HALF) * 2
        edge[side, 0:CELL, :] = local[base : base + CELL, :]
        edge[side, CELL : CELL + 2, :] = local[cbase : cbase + 2, :]
        edge[side, CELL + 2 : NODE, :] = jnp.zeros((NODE - CELL - 2, 2 * LEAF), jnp.float32)
    edges = [
        remote(edge.at[0], halo.at[1], e_send.at[0], e_recv.at[1], below),
        remote(edge.at[1], halo.at[0], e_send.at[1], e_recv.at[0], above),
    ]
    for copy in edges:
        copy.start()
    sent += edges

    for copy in asks:
        copy.wait_recv()
    moves = [read, pltpu.make_async_copy(asked_v, asked, q_local)]
    moves[1].start()
    for move in moves:
        move.wait()

    def pick(chunk, target, request):
        def one(c, carry):
            cluster = request(c)
            upper = cluster >> (HALF.bit_length() - 1)
            cell = cluster + upper * (SUB // CELL - HALF)
            row = HALF * CELL + cluster * 2 + upper * (SUB - 2 * HALF)
            target[pl.ds(pl.multiple_of(c * CELL, CELL), CELL), :] = chunk[pl.ds(cell * CELL, CELL), :]
            for part in range(2):
                target[pl.ds(CAP * CELL + c * 2 + part, 1), :] = chunk[pl.ds(row + part, 1), :]
            return carry

        lax.fori_loop(0, CAP, one, 0)

    arriving = []

    def select(slot):
        chunk = chunks[slot]
        source_z = (z + n_z - slot) % n_z

        def requests(k):
            return lambda c: (asked[k - 1, c, y * n_z + source_z] if k else scalars[c, y * n_z + source_z])

        for k in sorted(range(1, n_y), key=lambda k: -min(k, n_y - k)):
            pick(chunk, stage.at[k - 1, slot], requests(k))
            copy = remote(
                stage.at[k - 1, slot], recv.at[k * n_z + slot], y_send.at[k - 1, slot], y_recv.at[k - 1, slot], across[k]
            )
            copy.start()
            sent.append(copy)
            arriving.append(copy)
        pick(chunk, recv.at[slot], requests(0))

    for c in range(leaves):
        base = (c // HALF) * SUB + (c % HALF) * CELL
        cbase = (c // HALF) * SUB + HALF * CELL + (c % HALF) * 2
        cells[c + 1, 0:CELL, :] = local[base : base + CELL, :]
        cells[c + 1, CELL : CELL + 2, :] = local[cbase : cbase + 2, :]

    def near_entry(leaf, offset):
        if offset < NEAR:
            place = me * leaves + leaf + offset - NEAR // 2
            inside = (place >= 0) & (place < n_leaf * leaves)
            scale = (scalars[MASK_ROW + offset, leaf] * inside.astype(jnp.int32)).astype(jnp.float32)
        else:
            scale = jnp.float32(0)
        at = leaf + offset if offset < NEAR else leaf
        return cells[at, 0:CELL, :], cells[at, CELL : CELL + 1, :], cells[at, CELL + 1 : CELL + 2, :], scale

    def near_pair(j, carry):
        at = pl.ds(pl.multiple_of(j * 2 * LEAF, 2 * LEAF), 2 * LEAF)
        coordinates = columns_of(points[:, at])
        for i in range(2):
            for a in range(3):
                columns[2 * j + i, a] = coordinates[i][a]
        totals = []
        for i in range(2):
            left, right = four(coordinates[i], [near_entry(2 * j + i, o) for o in range(4)])
            totals.append(dot_nt(left, right, None))
        close[:, at] = two(*totals)
        return carry

    def near_share(step):
        if step == 2:
            for copy in edges:
                copy.wait_recv()
            cells[0] = halo[0]
            cells[leaves + 1] = halo[1]
        pairs = leaves // 2
        share = -(-pairs // (n_z // 2 - 2))
        lax.fori_loop(min(pairs, (step - 2) * share), min(pairs, (step - 1) * share), near_pair, 0)

    select(0)
    for step in range(1, n_z // 2 + 1):
        for way, part in order:
            if step - 1 < hops[way, part]:
                ring(way, part, step - 1).wait_recv()
                forward(way, part, step)
        select(step)
        if step < n_z // 2:
            select(n_z - step)
        if step >= 2:
            near_share(step)
    for copy in arriving:
        copy.wait_recv()
    for copy in sent:
        copy.wait_send()


def fetch(samples, points, table, n_leaf):
    n_z = n_leaf // ROWS_Y
    rows = samples.shape[0]
    leaves = samples.shape[1] // LEAF
    dma = pltpu.SemaphoreType.DMA
    f32 = jnp.float32
    return pl.pallas_call(
        functools.partial(fetch_body, n_leaf),
        out_shape=(
            jax.ShapeDtypeStruct((n_leaf, MSG, 2 * LEAF), f32),
            jax.ShapeDtypeStruct(samples.shape, f32),
            jax.ShapeDtypeStruct((leaves, 3, LEAF, 2 * LEAF), f32),
        ),
        in_specs=[whole] * 3,
        out_specs=(whole, whole, whole),
        scratch_shapes=[VMEM((2 * SUB, 2 * LEAF), f32)] * n_z
        + [
            pltpu.SMEM(table.shape, jnp.int32),
            VMEM((leaves + 2, NODE, 2 * LEAF), f32),
            VMEM((2, NODE, 2 * LEAF), f32),
            VMEM((ROWS_Y - 1, n_z, MSG, 2 * LEAF), f32),
            VMEM((2, NODE, 2 * LEAF), f32),
            VMEM((ROWS_Y - 1, CAP, table.shape[1]), jnp.int32),
            pltpu.SMEM((ROWS_Y - 1, CAP, table.shape[1]), jnp.int32),
            dma((2, 2, n_z // 2)),
            dma((2, 2, n_z // 2)),
            dma((ROWS_Y - 1, n_z)),
            dma((ROWS_Y - 1, n_z)),
            dma((ROWS_Y - 1,)),
            dma((ROWS_Y - 1,)),
            dma,
            dma((2,)),
            dma((2,)),
            dma,
        ],
        compiler_params=pltpu.CompilerParams(
            collective_id=1, has_side_effects=True, vmem_limit_bytes=40 * MIB
        ),
        name="fetch",
    )(samples, points, table)


def sample_body(
    leaves, n_leaf, recv, near_in, columns, table, far_out, near_out, far_again, totals, scalars, sem
):
    move = pltpu.make_async_copy(table, scalars, sem)
    move.start()
    near_out[...] = near_in[...]
    totals[...] = jnp.zeros(totals.shape, jnp.float32)
    n_z = n_leaf // ROWS_Y
    me = lax.axis_index("leaf")
    y, z = me // n_z, me % n_z
    move.wait()

    def far_entry(leaf, f, count):
        slot = scalars[SLOT_ROW + f, leaf]
        owner = slot >> 3
        message = ((y - owner // n_z) & (ROWS_Y - 1)) * n_z + ((z - owner) & (n_z - 1))
        c = slot & (CAP - 1)
        scale = jnp.where(f < count, 1.0, 0.0).astype(jnp.float32)
        return (
            recv[message, pl.ds(pl.multiple_of(c * CELL, CELL), CELL), :],
            recv[message, pl.ds(CAP * CELL + 2 * c, 1), :],
            recv[message, pl.ds(CAP * CELL + 2 * c + 1, 1), :],
            scale,
        )

    def steps_of(leaf):
        return (scalars[COUNT_ROW, leaf] + 3) // 4

    def operands(leaf, g):
        count = scalars[COUNT_ROW, leaf]
        place = jnp.minimum(leaf, leaves - 1)
        coordinates = [columns[place, a] for a in range(3)]
        return four(coordinates, [far_entry(leaf, 4 * g + b, count) for b in range(4)])

    def following(leaf, g):
        last = g + 1 >= steps_of(leaf)
        return jnp.where(last, jnp.minimum(leaf + 1, leaves), leaf), jnp.where(last, 0, g + 1)

    def work(leaf, g):
        second = following(leaf, g)
        return following(*second), (leaf, second[0]), (operands(leaf, g), operands(*second))

    def add(places, waiting):
        for place, (left, right) in zip(places, waiting):
            totals[place] += dot_nt(left, right, None)

    def turn(t, carried):
        at, places, waiting = carried
        add(places, waiting)
        return work(*at)

    zero = jnp.int32(0)
    steps = lax.fori_loop(0, leaves, lambda leaf, total: total + steps_of(leaf), zero)
    at, places, waiting = lax.fori_loop(1, (steps + 1) // 2, turn, work(zero, zero))
    add(places, waiting)
    for j in range(leaves // 2):
        at = pl.ds(j * 2 * LEAF, 2 * LEAF)
        far = two(totals[2 * j], totals[2 * j + 1])
        far_out[:, at] = far
        far_again[:, at] = far


def sample(recv, near, columns, table, n_leaf):
    leaves = columns.shape[0]
    shape = jax.ShapeDtypeStruct((RANK, leaves * LEAF), jnp.float32)
    return pl.pallas_call(
        functools.partial(sample_body, leaves, n_leaf),
        out_shape=(shape, shape, shape),
        in_specs=[whole] * 4,
        out_specs=(whole, whole, whole),
        scratch_shapes=[
            VMEM((leaves + 1, LEAF, 2 * LEAF), jnp.float32),
            pltpu.SMEM(table.shape, jnp.int32),
            pltpu.SemaphoreType.DMA,
        ],
        compiler_params=pltpu.CompilerParams(vmem_limit_bytes=40 * MIB),
        name="sample",
    )(recv, near, columns, table)


def eye(shape, first=0):
    rows = lax.broadcasted_iota(jnp.int32, shape, 0)
    return jnp.where(lanes(shape) == rows + first, 1.0, 0.0).astype(jnp.float32)


def inverse(value):
    guess = pl.reciprocal(value, approx=True)
    return guess


def compress(tiles, traces):
    block = 8
    shape = (RANK, 4 * RANK)
    on_diagonal = lanes(shape) == lax.broadcasted_iota(jnp.int32, shape, 0)
    tiles = [
        tile + jnp.where(on_diagonal, shift_share * trace / RANK + 1e-06, 0.0) for tile, trace in zip(tiles, traces)
    ]
    tiles = [[tile[8 * g : 8 * g + 8] for g in range(4)] for tile in tiles]
    full = (8, 4 * RANK)
    sub = lax.broadcasted_iota(jnp.int32, full, 0)
    scales = [[jnp.zeros(full, jnp.float32) for g in range(4)] for tile in tiles]
    for first in range(0, RANK, block):
        g = first // 8
        columns = [
            [[jnp.broadcast_to(part[:, first + t : first + t + 1], full) for t in range(block)] for part in tile[g:]]
            for tile in tiles
        ]
        for t in range(block):
            s = (first + t) % 8
            for tile, column, scale in zip(tiles, columns, scales):
                pivot = jnp.broadcast_to(column[0][t][s : s + 1], full)
                inv = inverse(pivot)
                scale[g] = jnp.where(sub == s, lax.rsqrt(pivot), scale[g])
                row = jnp.broadcast_to(tile[g][s : s + 1], full)
                right = [None] * block
                for u in range(t + 1, block):
                    right[u] = jnp.broadcast_to(column[0][u][s : s + 1], full)
                for h in range(g, 4):
                    c = column[h - g][t]
                    if h == g:
                        if s == 7:
                            continue
                        c = jnp.where(sub > s, c, 0.0)
                    tile[h] = tile[h] - (c * row) * inv
                    for u in range(t + 1, block):
                        column[h - g][u] = column[h - g][u] - (c * right[u]) * inv
    return [
        jnp.concatenate([part * factor for part, factor in zip(tile, scale)], axis=0)
        for tile, scale in zip(tiles, scales)
    ]


def total_of(value):
    return jnp.sum(jnp.sum(value, axis=0, keepdims=True), axis=1, keepdims=True)


def parent_tile(stacked):
    lane = lanes(stacked.shape)
    c = jnp.where(lane < RANK, stacked, 0.0)
    right = jnp.where(lane < 2 * RANK, c + pltpu.roll(c, RANK, 1), eye(stacked.shape, 2 * RANK))
    tile = lax.dot_general(
        c[:, :RANK], right, (((0,), (0,)), ((), ())), precision=highest, preferred_element_type=jnp.float32
    )
    return tile, total_of(c * c)


def project(tile, stacked):
    low = lanes(tile.shape) < 2 * RANK
    high, rest = halves(tile)
    s_high, s_rest = halves(stacked)
    high = high.astype(jnp.float32)
    first = jnp.where(low, swap_halves(rest.astype(jnp.float32)), high)
    left = jnp.concatenate([first, swap_halves(high)], axis=1)[:, : 6 * RANK].astype(jnp.bfloat16)
    return dot_nn(left, jnp.concatenate([s_high, s_high, s_rest], axis=0), None)


def parents(current):
    pairs = [
        parent_tile(pltpu.roll(jnp.concatenate(current[i : i + 2], axis=0), 3 * RANK, 1))
        for i in range(0, len(current), 2)
    ]
    return compress([tile for tile, _ in pairs], [trace for _, trace in pairs])


def chain(current):
    levels = []
    while len(current) > 1:
        current = parents(current)
        levels.append(current)
    return levels


def side_by_side(first, second):
    return jnp.where(lanes(first.shape) < 2 * RANK, swap_halves(first), second)


def descriptor(src, dst, send, recv, axis, peer):
    return pltpu.make_async_remote_copy(
        src_ref=src, dst_ref=dst, send_sem=send, recv_sem=recv, device_id={axis: peer}, device_id_type=MESH
    )


PARTS = ((0, 2), (2, 1), (3, 1))


def subtree(n_cols, tiles, traces, out, send, recv):
    col = lax.axis_index("cols")
    others = [(col + k) % n_cols for k in range(1, n_cols)]
    sent = []

    def publish(part):
        rows = pl.ds(*PARTS[part])
        for k in range(n_cols - 1):
            copy = descriptor(
                out.at[col, rows], out.at[col, rows], send.at[part, k], recv.at[part, k], "cols", others[k]
            )
            copy.start()
            sent.append(copy)

    current = compress(tiles, traces)
    out[col, 0] = side_by_side(current[0], current[1])
    out[col, 1] = side_by_side(current[2], current[3])
    publish(0)
    current = parents(current)
    out[col, 2] = side_by_side(current[0], current[1])
    publish(1)
    out[col, 3] = parents(current)[0]
    publish(2)

    def collect(part):
        rows = pl.ds(*PARTS[part])
        for k in range(n_cols - 1):
            owner = (col + n_cols - k - 1) % n_cols
            descriptor(
                out.at[owner, rows], out.at[owner, rows], send.at[part, k], recv.at[part, k], "cols", others[k]
            ).wait_recv()

    def end():
        for copy in sent:
            copy.wait_send()

    return collect, end


def leaf_body(n_cols, far, sketch, out, partial, pieces, send_a, recv_a, send_b, recv_b):
    me = lax.axis_index("cols")
    width = partial.shape[1] // n_cols
    peers = [(me + k) % n_cols for k in range(1, n_cols)]
    ready = greet("cols", peers)
    for j in range(partial.shape[1] // (2 * LEAF)):
        at = pl.ds(j * 2 * LEAF, 2 * LEAF)
        partial[:, at] = dot_nn(sketch[...], far[:, at])
    ready()

    def piece(owner):
        return pl.ds(pl.multiple_of(owner * width, width), width)

    first = []
    for k in range(1, n_cols):
        copy = descriptor(
            partial.at[:, piece(peers[k - 1])], pieces.at[k - 1], send_a.at[k - 1], recv_a.at[k - 1], "cols", peers[k - 1]
        )
        copy.start()
        first.append(copy)
    value = partial[:, piece(me)]
    for k in range(1, n_cols):
        first[k - 1].wait_recv()
        value = value + pieces[k - 1]
    unit = eye((2 * RANK, 2 * RANK))
    bs = []
    for j in range(2):
        pair = value[:, 2 * LEAF * j : 2 * LEAF * (j + 1)]
        bs += [pair[:, :LEAF], swap_halves(pair)[:, :LEAF]]
    tiles = [dot_nt(b, jnp.concatenate([b, b, unit], axis=0)) for b in bs]
    collect, end = subtree(n_cols, tiles, [total_of(b * b) for b in bs], out, send_b, recv_b)
    for part in range(3):
        collect(part)
    for copy in first:
        copy.wait_send()
    end()


def leaf_tiles(far, sketch, n_cols):
    rows, columns = far.shape
    dma = pltpu.SemaphoreType.DMA
    return pl.pallas_call(
        functools.partial(leaf_body, n_cols),
        out_shape=jax.ShapeDtypeStruct((n_cols, 4, RANK, 4 * RANK), jnp.float32),
        in_specs=[whole, whole],
        out_specs=whole,
        scratch_shapes=[VMEM(far.shape, jnp.float32), VMEM((n_cols - 1, rows, columns // n_cols), jnp.float32)]
        + [dma((n_cols - 1,))] * 2
        + [dma((3, n_cols - 1))] * 2,
        compiler_params=pltpu.CompilerParams(collective_id=2, has_side_effects=True, vmem_limit_bytes=40 * MIB),
        name="leaf_tiles",
    )(far, sketch)


def unpack(block):
    return jnp.concatenate([pltpu.roll(block, (4 * RANK - RANK * g) % (4 * RANK), 1) for g in range(4)], axis=0)


def pack(source, shift):
    quarter = lanes((8, 4 * RANK)) // RANK
    row = jnp.zeros((8, 4 * RANK), jnp.float32)
    for g in range(4):
        turned = pltpu.roll(source[8 * g : 8 * g + 8], (RANK * g - shift) % (4 * RANK), 1)
        row = jnp.where(quarter == g, turned, row)
    return row


def project_t(tile, row):
    low = lanes(tile.shape) < LEAF
    high, rest = [part.astype(jnp.float32) for part in halves(tile)]
    r_high, r_rest = [part.astype(jnp.float32) for part in halves(row)]
    left = [jnp.where(low, swap_halves(rest), high), jnp.where(low, 0.0, high)]
    right = [jnp.where(low, swap_halves(r_high), r_high), r_rest]
    return dot_nt(
        jnp.concatenate(left, axis=1).astype(jnp.bfloat16), jnp.concatenate(right, axis=1).astype(jnp.bfloat16), None
    )


def both(pair):
    return [swap_halves(pair), pair]


def climb(tiles, owner, values):
    second = both(tiles[owner, 2])
    values = [project(second[i], jnp.concatenate(values[2 * i : 2 * i + 2], axis=0)) for i in range(2)]
    return project(tiles[owner, 3], jnp.concatenate(values, axis=0))


def finish(levels, values):
    for tiles in levels:
        values = [project(tile, jnp.concatenate(values[2 * i : 2 * i + 2], axis=0)) for i, tile in enumerate(tiles)]
    return values[0]


def tree_body(
    n_leaf, n_cols, tiles, far, branch, transfers, root,
    upper, chosen, packed_p, out_p,
    yc_send, yc_recv, zc_send, zc_recv, yp_send, yp_recv, zp_send, zp_recv, x_send, x_recv, own,
):
    n_y = ROWS_Y
    n_z = n_leaf // n_y
    seg = n_leaf // n_cols
    me, col = lax.axis_index("leaf"), lax.axis_index("cols")
    y, z = me // n_z, me % n_z
    across = [((y + k) % n_y) * n_z + z for k in range(1, n_y)]
    along = [y * n_z + (z + k) % n_z for k in range(1, n_z)]
    others = [(col + k) % n_cols for k in range(1, n_cols)]
    far_first = sorted(range(n_z - 1), key=lambda k: -min(k + 1, n_z - 1 - k))
    barrier = pltpu.get_barrier_semaphore()
    for peer in across + along:
        pl.semaphore_signal(barrier, inc=1, device_id={"leaf": peer}, device_id_type=MESH)
    for peer in others:
        pl.semaphore_signal(barrier, inc=1, device_id={"cols": peer}, device_id_type=MESH)

    levels = chain([tiles[c, 3] for c in range(n_cols)])
    packed_c = pack(levels[-1][0], RANK)

    values = []
    for c in range(n_cols):
        leaves = []
        for j in range(2):
            at = pl.ds((2 * c + j) * 2 * LEAF, 2 * LEAF)
            pair, rows = tiles[c, j], far[:, at]
            leaves += [project_t(q, row) for q, row in zip(both(pair), both(rows))]
        values.append(leaves)
    values = [climb(tiles, c, leaves) for c, leaves in enumerate(values)]
    pl.semaphore_wait(barrier, len(across) + len(along) + len(others))

    tree_y, tree_z = (col * seg) // n_z, (col * seg) % n_z
    slot = z % seg
    carries = z // seg == tree_z // seg
    starts = carries & (y == tree_y)

    def c_across(k):
        return descriptor(chosen.at[slot], chosen.at[slot], yc_send.at[k], yc_recv, "leaf", across[k])

    def c_along(k):
        return descriptor(chosen.at[slot], chosen.at[slot], zc_send.at[k], zc_recv.at[slot], "leaf", along[k])

    @pl.when(starts)
    def _():
        chosen[slot] = packed_c
        for k in range(n_y - 1):
            c_across(k).start()

    value = finish(levels, values)
    branch[...] = value
    packed_p[...] = pack(jnp.concatenate([value, jnp.zeros((RANK, 3 * RANK), jnp.float32)], axis=1), 0)

    p_across = [
        descriptor(packed_p, out_p.at[z, y], yp_send.at[k], yp_recv.at[k], "leaf", across[k]) for k in range(n_y - 1)
    ]
    for copy in p_across:
        copy.start()
    mine = pltpu.make_async_copy(packed_p, out_p.at[z, y], own)
    mine.start()

    @pl.when(carries & (y != tree_y))
    def _():
        c_across(0).wait_recv()

    @pl.when(carries)
    def _():
        for k in far_first:
            c_along(k).start()

    mine.wait()
    for k in range(n_y - 1):
        other = (y + n_y - k - 1) % n_y
        descriptor(packed_p, out_p.at[z, other], yp_send.at[k], yp_recv.at[k], "leaf", across[k]).wait_recv()
    p_along = [
        descriptor(out_p.at[z], out_p.at[z], zp_send.at[k], zp_recv.at[k], "leaf", along[k]) for k in range(n_z - 1)
    ]
    for k in far_first:
        p_along[k].start()

    for i in range(seg):

        @pl.when(tree_z + i != z)
        def _():
            descriptor(chosen.at[i], chosen.at[i], zc_send.at[i], zc_recv.at[i], "leaf", along[0]).wait_recv()

    pairs = [
        parent_tile(jnp.concatenate([unpack(chosen[2 * i]), unpack(chosen[2 * i + 1])], axis=0)) for i in range(seg // 2)
    ]
    collect, end = subtree(n_cols, [tile for tile, _ in pairs], [trace for _, trace in pairs], upper, x_send, x_recv)
    for part in (0, 1, 2):
        collect(part)
    for k in range(n_z - 1):
        other = (z + n_z - k - 1) % n_z
        descriptor(out_p.at[other], out_p.at[other], zp_send.at[k], zp_recv.at[k], "leaf", along[k]).wait_recv()

    def q_of(tile):
        return swap_halves(tile)[:, : 2 * RANK]

    levels = chain([upper[c, 3] for c in range(n_cols)])
    values = []
    for c in range(n_cols):
        nodes = []
        for j in range(2):
            for i, tile in enumerate(both(upper[c, j])):
                at = c * seg + 2 * (2 * j + i)
                children = [unpack(out_p[(at + d) % n_z, (at + d) // n_z]) for d in range(2)]
                nodes.append(project(tile, jnp.concatenate(children, axis=0)))
                transfers[4 * c + 2 * j + i] = q_of(tile)
        values.append(nodes)
        for i, tile in enumerate(both(upper[c, 2])):
            transfers[4 * n_cols + 2 * c + i] = q_of(tile)
        transfers[6 * n_cols + c] = q_of(upper[c, 3])
    values = [climb(upper, c, nodes) for c, nodes in enumerate(values)]
    first = 7 * n_cols
    for level_tiles in levels:
        for i, tile in enumerate(level_tiles):
            transfers[first + i] = q_of(tile)
        first += len(level_tiles)
    root[...] = finish(levels, values)[:, :RANK]

    @pl.when(starts)
    def _():
        for k in range(n_y - 1):
            c_across(k).wait_send()

    @pl.when(carries)
    def _():
        for k in range(n_z - 1):
            c_along(k).wait_send()

    for copy in p_across + p_along:
        copy.wait_send()
    end()


def tree(tiles, far, n_leaf, n_cols):
    n_z = n_leaf // ROWS_Y
    f32 = jnp.float32
    dma = pltpu.SemaphoreType.DMA
    return pl.pallas_call(
        functools.partial(tree_body, n_leaf, n_cols),
        out_shape=(
            jax.ShapeDtypeStruct((RANK, RANK), f32),
            jax.ShapeDtypeStruct((n_leaf - 1, RANK, 2 * RANK), f32),
            jax.ShapeDtypeStruct((RANK, RANK), f32),
        ),
        in_specs=[whole, whole],
        out_specs=(whole, whole, whole),
        scratch_shapes=[
            VMEM((n_cols, 4, RANK, 4 * RANK), f32),
            VMEM((n_leaf // n_cols, 8, 4 * RANK), f32),
            VMEM((8, 4 * RANK), f32),
            VMEM((n_z, ROWS_Y, 8, 4 * RANK), f32),
            dma((ROWS_Y - 1,)),
            dma,
            dma((n_z - 1,)),
            dma((n_leaf // n_cols,)),
            dma((ROWS_Y - 1,)),
            dma((ROWS_Y - 1,)),
            dma((n_z - 1,)),
            dma((n_z - 1,)),
            dma((3, n_cols - 1)),
            dma((3, n_cols - 1)),
            dma,
        ],
        compiler_params=pltpu.CompilerParams(
            collective_id=3, has_side_effects=True, vmem_limit_bytes=40 * MIB
        ),
        name="tree",
    )(tiles, far)


def results_body(tiles, branch, transfers, root, basis_out, branch_out, transfers_out, root_out):
    for c in range(tiles.shape[0]):
        for j in range(2):
            basis_out[:, pl.ds((2 * c + j) * 2 * LEAF, 2 * LEAF)] = tiles[c, j]
    branch_out[...] = branch[...]
    transfers_out[...] = transfers[...]
    root_out[...] = root[...]


def results(tiles, branch, transfers, root):
    f32 = jnp.float32
    return pl.pallas_call(
        results_body,
        out_shape=(
            jax.ShapeDtypeStruct((RANK, 4 * tiles.shape[0] * LEAF), f32),
            jax.ShapeDtypeStruct(branch.shape, f32),
            jax.ShapeDtypeStruct(transfers.shape, f32),
            jax.ShapeDtypeStruct(root.shape, f32),
        ),
        in_specs=[whole] * 4,
        out_specs=(whole,) * 4,
        compiler_params=pltpu.CompilerParams(vmem_limit_bytes=40 * MIB),
        name="results",
    )(tiles, branch, transfers, root)


def on_device(n_leaf, n_cols, points, samples, sketch, far_requests, far_slots, far_count, near_mask):
    table = jnp.zeros((32, 2 * LEAF), jnp.int32)
    for row, block in ((0, far_requests[0].T), (SLOT_ROW, far_slots.T), (MASK_ROW, near_mask.T), (COUNT_ROW, far_count[None])):
        table += jnp.pad(block, ((row, 32 - row - block.shape[0]), (0, 2 * LEAF - block.shape[1])))
    recv, close, columns = fetch(samples, points, table, n_leaf)
    far_sample, near_sample, far_again = sample(recv, close, columns, table, n_leaf)
    tiles = leaf_tiles(far_again, sketch, n_cols)
    branch_samples, top_transfer, root_sample = tree(tiles, far_again, n_leaf, n_cols)
    leaf_basis, branch_samples, top_transfer, root_sample = results(tiles, branch_samples, top_transfer, root_sample)
    return far_sample, near_sample, leaf_basis, branch_samples, jnp.swapaxes(top_transfer, 1, 2), root_sample


def solution(mesh):
    return jax.shard_map(
        functools.partial(on_device, mesh.shape["leaf"], mesh.shape["cols"]),
        mesh=mesh,
        in_specs=(
            P(None, "leaf"),
            P("cols", "leaf"),
            P(None, "cols"),
            P("leaf", None, None),
            P("leaf", None),
            P("leaf"),
            P("leaf", None),
        ),
        out_specs=(
            P("cols", "leaf"),
            P("cols", "leaf"),
            P(None, "leaf"),
            P("leaf", "cols"),
            P(),
            P(None, "cols"),
        ),
        check_vma=False,
    )
```

```python
import functools

import jax
import jax.numpy as jnp
from jax import lax
from jax.experimental import pallas as pl
from jax.experimental.pallas import tpu as pltpu
from jax.sharding import PartitionSpec as P

LEAF = 64
FAR = 16
CAP = 8
RANK = 32
NEAR = 3
SLOT_ROW = CAP
MASK_ROW = SLOT_ROW + FAR
COUNT_ROW = MASK_ROW + NEAR
ROWS_Y = 4
CELL = 16
HALF = 16
SUB = HALF * CELL + HALF * 2
MSG = CAP * CELL + CAP * 2
NODE = 24

length_scale = 0.3
shift_share = 0.05
highest = lax.Precision.HIGHEST
MESH = pl.DeviceIdType.MESH
VMEM = pltpu.VMEM
whole = pl.BlockSpec(memory_space=pltpu.VMEM)
MIB = 1 << 20


def lanes(shape):
    return lax.broadcasted_iota(jnp.int32, shape, len(shape) - 1)


def swap_halves(tile):
    return pltpu.roll(tile, 64, 1)


def dot_nt(a, b, precision=highest):
    return lax.dot_general(
        a, b, (((1,), (1,)), ((), ())), precision=precision, preferred_element_type=jnp.float32
    )


def dot_nn(a, b, precision=highest):
    return lax.dot_general(
        a, b, (((1,), (0,)), ((), ())), precision=precision, preferred_element_type=jnp.float32
    )


def halves(value):
    high = value.astype(jnp.bfloat16)
    return high, (value - high.astype(jnp.float32)).astype(jnp.bfloat16)


def columns_of(both):
    both = jnp.concatenate([both, jnp.zeros((5, 2 * LEAF), jnp.float32)], axis=0).T
    return [
        [jnp.broadcast_to(block[:, a : a + 1], (LEAF, 2 * LEAF)) for a in range(3)] for block in (both[:LEAF], both[LEAF:])
    ]


def pair_of_clusters(coordinates, first, second):
    (block_a, row_a, last_a, scale_a), (block_b, row_b, last_b, scale_b) = first, second
    low16 = lanes((CELL, 2 * LEAF)) < LEAF
    low1 = lanes((1, 2 * LEAF)) < LEAF
    x = jnp.where(low1, row_a, swap_halves(row_b))
    y = jnp.where(low1, swap_halves(row_a), row_b)
    z = jnp.where(low1, last_a, last_b)
    dx = coordinates[0] - x
    dy = coordinates[1] - y
    dz = coordinates[2] - z
    square = dx * dx + dy * dy + dz * dz
    values = jnp.exp2(square * lax.rsqrt(jnp.maximum(square, 1e-30)) * (-1.4426950408889634 / length_scale))
    block_a = block_a * scale_a
    block_b = block_b * scale_b
    rows = jnp.concatenate(
        [jnp.where(low16, block_a, swap_halves(block_b)), jnp.where(low16, swap_halves(block_a), block_b)], axis=0
    )
    return halves(values), halves(rows)


def four(coordinates, entries):
    (k0h, k0l), (s0h, s0l) = pair_of_clusters(coordinates, entries[0], entries[1])
    (k1h, k1l), (s1h, s1l) = pair_of_clusters(coordinates, entries[2], entries[3])
    left = jnp.concatenate([jnp.concatenate([s0h, s1h], axis=1), jnp.concatenate([s0l, s1l], axis=1)], axis=0)
    right = jnp.concatenate([jnp.concatenate([k0h, k1h], axis=1), jnp.concatenate([k0l, k1l], axis=1)], axis=0)
    return left, right


def fold(total):
    total = total[: 2 * CELL] + total[2 * CELL :]
    return total + swap_halves(total)


def two(first, second):
    return jnp.where(lanes((2 * CELL, 2 * LEAF)) < LEAF, fold(first), fold(second))


def greet(axis, peers):
    barrier = pltpu.get_barrier_semaphore()
    for peer in peers:
        pl.semaphore_signal(barrier, inc=1, device_id={axis: peer}, device_id_type=MESH)
    return lambda: pl.semaphore_wait(barrier, len(peers))


def fetch_body(
    n_leaf, samples, points, table, recv, close, columns, *scratch
):
    n_y = ROWS_Y
    n_z = n_leaf // n_y
    chunks = scratch[:n_z]
    local = chunks[0]
    scalars, cells, halo, stage, edge, asked_v, asked, ring_send, ring_recv, y_send, y_recv, q_send, q_recv, q_local, e_send, e_recv, start_sem = scratch[n_z:]
    me = lax.axis_index("leaf")
    y, z = me // n_z, me % n_z
    up = y * n_z + (z + 1) % n_z
    down = y * n_z + (z + n_z - 1) % n_z
    above, below = (me + 1) % n_leaf, (me + n_leaf - 1) % n_leaf
    across = [None] + [((y + k) % n_y) * n_z + z for k in range(1, n_y)]
    leaves = samples.shape[1] // LEAF
    read = pltpu.make_async_copy(table, scalars, start_sem)
    read.start()
    ready = greet("leaf", [up, down, above, below] + across[1:])
    own = table.at[pl.ds(0, CAP)]

    def remote(src, dst, send, recv_sem, peer):
        return pltpu.make_async_remote_copy(
            src_ref=src, dst_ref=dst, send_sem=send, recv_sem=recv_sem,
            device_id={"leaf": peer}, device_id_type=MESH,
        )

    low = lanes((CELL, 2 * LEAF)) < LEAF
    for j in range(HALF):
        top = samples[0:CELL, 2 * LEAF * j : 2 * LEAF * (j + 1)]
        bottom = samples[CELL : 2 * CELL, 2 * LEAF * j : 2 * LEAF * (j + 1)]
        base = (2 * j // HALF) * SUB + (2 * j % HALF) * CELL
        local[base : base + CELL, :] = jnp.where(low, top, swap_halves(bottom))
        local[base + CELL : base + 2 * CELL, :] = jnp.where(low, swap_halves(top), bottom)
    low1 = lanes((1, 2 * LEAF)) < LEAF
    for j in range(HALF):
        xs, ys, zs = [points[a : a + 1, 2 * LEAF * j : 2 * LEAF * (j + 1)] for a in range(3)]
        base = (2 * j // HALF) * SUB + HALF * CELL + (2 * j % HALF) * 2
        local[base : base + 1, :] = jnp.where(low1, xs, swap_halves(ys))
        local[base + 1 : base + 2, :] = jnp.where(low1, zs, swap_halves(zs))
        local[base + 2 : base + 3, :] = jnp.where(low1, swap_halves(xs), ys)
        local[base + 3 : base + 4, :] = jnp.where(low1, swap_halves(zs), zs)

    for side, cluster in ((0, 0), (1, 2 * HALF - 1)):
        base = (cluster // HALF) * SUB + (cluster % HALF) * CELL
        cbase = (cluster // HALF) * SUB + HALF * CELL + (cluster % HALF) * 2
        edge[side, 0:CELL, :] = local[base : base + CELL, :]
        edge[side, CELL : CELL + 2, :] = local[cbase : cbase + 2, :]
        edge[side, CELL + 2 : NODE, :] = jnp.zeros((NODE - CELL - 2, 2 * LEAF), jnp.float32)
    ready()

    sent = []
    asks = []
    for k in range(1, n_y):
        copy = remote(
            own, asked_v.at[n_y - k - 1], q_send.at[k - 1], q_recv.at[n_y - k - 1], across[k]
        )
        copy.start()
        asks.append(copy)
    sent += asks

    hops = {(0, 0): n_z // 2, (0, 1): n_z // 2 - 1, (1, 0): n_z // 2 - 1, (1, 1): n_z // 2}

    def ring(way, part, step):
        here, there = (step, step + 1) if way == 0 else ((n_z - step) % n_z, n_z - step - 1)
        rows = pl.ds(part * SUB, SUB)
        return remote(
            chunks[here].at[rows], chunks[there].at[rows], ring_send.at[way, part, step],
            ring_recv.at[way, part, step], up if way == 0 else down,
        )

    def forward(way, part, step):
        if step < hops[way, part]:
            copy = ring(way, part, step)
            copy.start()
            sent.append(copy)

    order = ((0, 0), (1, 1), (0, 1), (1, 0))
    for way, part in order:
        forward(way, part, 0)

    edges = [
        remote(edge.at[0], halo.at[1], e_send.at[0], e_recv.at[1], below),
        remote(edge.at[1], halo.at[0], e_send.at[1], e_recv.at[0], above),
    ]
    for copy in edges:
        copy.start()
    sent += edges

    for copy in asks:
        copy.wait_recv()
    moves = [read, pltpu.make_async_copy(asked_v, asked, q_local)]
    moves[1].start()
    for move in moves:
        move.wait()

    def pick(chunk, target, request):
        def one(c, carry):
            cluster = request(c)
            upper = cluster >> (HALF.bit_length() - 1)
            cell = cluster + upper * (SUB // CELL - HALF)
            row = HALF * CELL + cluster * 2 + upper * (SUB - 2 * HALF)
            target[pl.ds(pl.multiple_of(c * CELL, CELL), CELL), :] = chunk[pl.ds(cell * CELL, CELL), :]
            for part in range(2):
                target[pl.ds(CAP * CELL + c * 2 + part, 1), :] = chunk[pl.ds(row + part, 1), :]
            return carry

        lax.fori_loop(0, CAP, one, 0)

    arriving = []

    def select(slot):
        chunk = chunks[slot]
        source_z = (z + n_z - slot) % n_z

        def requests(k):
            return lambda c: (asked[k - 1, c, y * n_z + source_z] if k else scalars[c, y * n_z + source_z])

        for k in sorted(range(1, n_y), key=lambda k: -min(k, n_y - k)):
            pick(chunk, stage.at[k - 1, slot], requests(k))
            copy = remote(
                stage.at[k - 1, slot], recv.at[k * n_z + slot], y_send.at[k - 1, slot], y_recv.at[k - 1, slot], across[k]
            )
            copy.start()
            sent.append(copy)
            arriving.append(copy)
        pick(chunk, recv.at[slot], requests(0))

    for c in range(leaves):
        base = (c // HALF) * SUB + (c % HALF) * CELL
        cbase = (c // HALF) * SUB + HALF * CELL + (c % HALF) * 2
        cells[c + 1, 0:CELL, :] = local[base : base + CELL, :]
        cells[c + 1, CELL : CELL + 2, :] = local[cbase : cbase + 2, :]

    def near_entry(leaf, offset):
        if offset < NEAR:
            place = me * leaves + leaf + offset - NEAR // 2
            inside = (place >= 0) & (place < n_leaf * leaves)
            scale = (scalars[MASK_ROW + offset, leaf] * inside.astype(jnp.int32)).astype(jnp.float32)
        else:
            scale = jnp.float32(0)
        at = leaf + offset if offset < NEAR else leaf
        return cells[at, 0:CELL, :], cells[at, CELL : CELL + 1, :], cells[at, CELL + 1 : CELL + 2, :], scale

    def near_pair(j, carry):
        at = pl.ds(pl.multiple_of(j * 2 * LEAF, 2 * LEAF), 2 * LEAF)
        coordinates = columns_of(points[:, at])
        for i in range(2):
            for a in range(3):
                columns[2 * j + i, a] = coordinates[i][a]
        totals = []
        for i in range(2):
            left, right = four(coordinates[i], [near_entry(2 * j + i, o) for o in range(4)])
            totals.append(dot_nt(left, right, None))
        close[:, at] = two(*totals)
        return carry

    def near_share(step):
        if step == 2:
            for copy in edges:
                copy.wait_recv()
            cells[0] = halo[0]
            cells[leaves + 1] = halo[1]
        pairs = leaves // 2
        share = -(-pairs // (n_z // 2 - 2))
        lax.fori_loop(min(pairs, (step - 2) * share), min(pairs, (step - 1) * share), near_pair, 0)

    select(0)
    for step in range(1, n_z // 2 + 1):
        for way, part in order:
            if step - 1 < hops[way, part]:
                ring(way, part, step - 1).wait_recv()
                forward(way, part, step)
        select(step)
        if step < n_z // 2:
            select(n_z - step)
        if step >= 2:
            near_share(step)
    for copy in arriving:
        copy.wait_recv()
    for copy in sent:
        copy.wait_send()


def fetch(samples, points, table, n_leaf):
    n_z = n_leaf // ROWS_Y
    rows = samples.shape[0]
    leaves = samples.shape[1] // LEAF
    dma = pltpu.SemaphoreType.DMA
    f32 = jnp.float32
    return pl.pallas_call(
        functools.partial(fetch_body, n_leaf),
        out_shape=(
            jax.ShapeDtypeStruct((n_leaf, MSG, 2 * LEAF), f32),
            jax.ShapeDtypeStruct(samples.shape, f32),
            jax.ShapeDtypeStruct((leaves, 3, LEAF, 2 * LEAF), f32),
        ),
        in_specs=[whole] * 3,
        out_specs=(whole, whole, whole),
        scratch_shapes=[VMEM((2 * SUB, 2 * LEAF), f32)] * n_z
        + [
            pltpu.SMEM(table.shape, jnp.int32),
            VMEM((leaves + 2, NODE, 2 * LEAF), f32),
            VMEM((2, NODE, 2 * LEAF), f32),
            VMEM((ROWS_Y - 1, n_z, MSG, 2 * LEAF), f32),
            VMEM((2, NODE, 2 * LEAF), f32),
            VMEM((ROWS_Y - 1, CAP, table.shape[1]), jnp.int32),
            pltpu.SMEM((ROWS_Y - 1, CAP, table.shape[1]), jnp.int32),
            dma((2, 2, n_z // 2)),
            dma((2, 2, n_z // 2)),
            dma((ROWS_Y - 1, n_z)),
            dma((ROWS_Y - 1, n_z)),
            dma((ROWS_Y - 1,)),
            dma((ROWS_Y - 1,)),
            dma,
            dma((2,)),
            dma((2,)),
            dma,
        ],
        compiler_params=pltpu.CompilerParams(
            collective_id=1, has_side_effects=True, vmem_limit_bytes=40 * MIB
        ),
        name="fetch",
    )(samples, points, table)


def sample_body(
    leaves, n_leaf, recv, near_in, columns, table, far_out, near_out, far_again, totals, scalars, sem
):
    move = pltpu.make_async_copy(table, scalars, sem)
    move.start()
    near_out[...] = near_in[...]
    totals[...] = jnp.zeros(totals.shape, jnp.float32)
    n_z = n_leaf // ROWS_Y
    me = lax.axis_index("leaf")
    y, z = me // n_z, me % n_z
    move.wait()

    def far_entry(leaf, f, count):
        slot = scalars[SLOT_ROW + f, leaf]
        owner = slot >> 3
        message = ((y - owner // n_z) & (ROWS_Y - 1)) * n_z + ((z - owner) & (n_z - 1))
        c = slot & (CAP - 1)
        scale = jnp.where(f < count, 1.0, 0.0).astype(jnp.float32)
        return (
            recv[message, pl.ds(pl.multiple_of(c * CELL, CELL), CELL), :],
            recv[message, pl.ds(CAP * CELL + 2 * c, 1), :],
            recv[message, pl.ds(CAP * CELL + 2 * c + 1, 1), :],
            scale,
        )

    def steps_of(leaf):
        return (scalars[COUNT_ROW, leaf] + 3) // 4

    def operands(leaf, g):
        count = scalars[COUNT_ROW, leaf]
        place = jnp.minimum(leaf, leaves - 1)
        coordinates = [columns[place, a] for a in range(3)]
        return four(coordinates, [far_entry(leaf, 4 * g + b, count) for b in range(4)])

    def following(leaf, g):
        last = g + 1 >= steps_of(leaf)
        return jnp.where(last, jnp.minimum(leaf + 1, leaves), leaf), jnp.where(last, 0, g + 1)

    def work(leaf, g):
        second = following(leaf, g)
        return following(*second), (leaf, second[0]), (operands(leaf, g), operands(*second))

    def add(places, waiting):
        for place, (left, right) in zip(places, waiting):
            totals[place] += dot_nt(left, right, None)

    def turn(t, carried):
        at, places, waiting = carried
        add(places, waiting)
        return work(*at)

    zero = jnp.int32(0)
    steps = lax.fori_loop(0, leaves, lambda leaf, total: total + steps_of(leaf), zero)
    at, places, waiting = lax.fori_loop(1, (steps + 1) // 2, turn, work(zero, zero))
    add(places, waiting)
    for j in range(leaves // 2):
        at = pl.ds(j * 2 * LEAF, 2 * LEAF)
        far = two(totals[2 * j], totals[2 * j + 1])
        far_out[:, at] = far
        far_again[:, at] = far


def sample(recv, near, columns, table, n_leaf):
    leaves = columns.shape[0]
    shape = jax.ShapeDtypeStruct((RANK, leaves * LEAF), jnp.float32)
    return pl.pallas_call(
        functools.partial(sample_body, leaves, n_leaf),
        out_shape=(shape, shape, shape),
        in_specs=[whole] * 4,
        out_specs=(whole, whole, whole),
        scratch_shapes=[
            VMEM((leaves + 1, LEAF, 2 * LEAF), jnp.float32),
            pltpu.SMEM(table.shape, jnp.int32),
            pltpu.SemaphoreType.DMA,
        ],
        compiler_params=pltpu.CompilerParams(vmem_limit_bytes=40 * MIB),
        name="sample",
    )(recv, near, columns, table)


def eye(shape, first=0):
    rows = lax.broadcasted_iota(jnp.int32, shape, 0)
    return jnp.where(lanes(shape) == rows + first, 1.0, 0.0).astype(jnp.float32)


def inverse(value):
    guess = pl.reciprocal(value, approx=True)
    return guess


def compress(tiles, traces):
    block = 8
    shape = (RANK, 4 * RANK)
    on_diagonal = lanes(shape) == lax.broadcasted_iota(jnp.int32, shape, 0)
    tiles = [
        tile + jnp.where(on_diagonal, shift_share * trace / RANK + 1e-06, 0.0) for tile, trace in zip(tiles, traces)
    ]
    tiles = [[tile[8 * g : 8 * g + 8] for g in range(4)] for tile in tiles]
    full = (8, 4 * RANK)
    sub = lax.broadcasted_iota(jnp.int32, full, 0)
    scales = [[jnp.zeros(full, jnp.float32) for g in range(4)] for tile in tiles]
    for first in range(0, RANK, block):
        g = first // 8
        columns = [
            [[jnp.broadcast_to(part[:, first + t : first + t + 1], full) for t in range(block)] for part in tile[g:]]
            for tile in tiles
        ]
        for t in range(block):
            s = (first + t) % 8
            for tile, column, scale in zip(tiles, columns, scales):
                pivot = jnp.broadcast_to(column[0][t][s : s + 1], full)
                inv = inverse(pivot)
                scale[g] = jnp.where(sub == s, lax.rsqrt(pivot), scale[g])
                row = jnp.broadcast_to(tile[g][s : s + 1], full)
                right = [None] * block
                for u in range(t + 1, block):
                    right[u] = jnp.broadcast_to(column[0][u][s : s + 1], full)
                for h in range(g, 4):
                    c = column[h - g][t]
                    if h == g:
                        if s == 7:
                            continue
                        c = jnp.where(sub > s, c, 0.0)
                    tile[h] = tile[h] - (c * row) * inv
                    for u in range(t + 1, block):
                        column[h - g][u] = column[h - g][u] - (c * right[u]) * inv
    return [
        jnp.concatenate([part * factor for part, factor in zip(tile, scale)], axis=0)
        for tile, scale in zip(tiles, scales)
    ]


def total_of(value):
    return jnp.sum(jnp.sum(value, axis=0, keepdims=True), axis=1, keepdims=True)


def parent_tile(stacked):
    lane = lanes(stacked.shape)
    c = jnp.where(lane < RANK, stacked, 0.0)
    right = jnp.where(lane < 2 * RANK, c + pltpu.roll(c, RANK, 1), eye(stacked.shape, 2 * RANK))
    tile = lax.dot_general(
        c[:, :RANK], right, (((0,), (0,)), ((), ())), precision=highest, preferred_element_type=jnp.float32
    )
    return tile, total_of(c * c)


def project(tile, stacked):
    low = lanes(tile.shape) < 2 * RANK
    high, rest = halves(tile)
    s_high, s_rest = halves(stacked)
    high = high.astype(jnp.float32)
    first = jnp.where(low, swap_halves(rest.astype(jnp.float32)), high)
    left = jnp.concatenate([first, swap_halves(high)], axis=1)[:, : 6 * RANK].astype(jnp.bfloat16)
    return dot_nn(left, jnp.concatenate([s_high, s_high, s_rest], axis=0), None)


def parents(current):
    pairs = [
        parent_tile(pltpu.roll(jnp.concatenate(current[i : i + 2], axis=0), 3 * RANK, 1))
        for i in range(0, len(current), 2)
    ]
    return compress([tile for tile, _ in pairs], [trace for _, trace in pairs])


def chain(current):
    levels = []
    while len(current) > 1:
        current = parents(current)
        levels.append(current)
    return levels


def side_by_side(first, second):
    return jnp.where(lanes(first.shape) < 2 * RANK, swap_halves(first), second)


def descriptor(src, dst, send, recv, axis, peer):
    return pltpu.make_async_remote_copy(
        src_ref=src, dst_ref=dst, send_sem=send, recv_sem=recv, device_id={axis: peer}, device_id_type=MESH
    )


PARTS = ((0, 2), (2, 1), (3, 1))


def subtree(n_cols, tiles, traces, out, send, recv):
    col = lax.axis_index("cols")
    others = [(col + k) % n_cols for k in range(1, n_cols)]
    sent = []

    def publish(part):
        rows = pl.ds(*PARTS[part])
        for k in range(n_cols - 1):
            copy = descriptor(
                out.at[col, rows], out.at[col, rows], send.at[part, k], recv.at[part, k], "cols", others[k]
            )
            copy.start()
            sent.append(copy)

    current = compress(tiles, traces)
    out[col, 0] = side_by_side(current[0], current[1])
    out[col, 1] = side_by_side(current[2], current[3])
    publish(0)
    current = parents(current)
    out[col, 2] = side_by_side(current[0], current[1])
    publish(1)
    out[col, 3] = parents(current)[0]
    publish(2)

    def collect(part):
        rows = pl.ds(*PARTS[part])
        for k in range(n_cols - 1):
            owner = (col + n_cols - k - 1) % n_cols
            descriptor(
                out.at[owner, rows], out.at[owner, rows], send.at[part, k], recv.at[part, k], "cols", others[k]
            ).wait_recv()

    def end():
        for copy in sent:
            copy.wait_send()

    return collect, end


def leaf_body(n_cols, far, sketch, out, partial, pieces, send_a, recv_a, send_b, recv_b):
    me = lax.axis_index("cols")
    width = partial.shape[1] // n_cols
    peers = [(me + k) % n_cols for k in range(1, n_cols)]
    ready = greet("cols", peers)
    for j in range(partial.shape[1] // (2 * LEAF)):
        at = pl.ds(j * 2 * LEAF, 2 * LEAF)
        partial[:, at] = dot_nn(sketch[...], far[:, at])
    ready()

    def piece(owner):
        return pl.ds(pl.multiple_of(owner * width, width), width)

    first = []
    for k in range(1, n_cols):
        copy = descriptor(
            partial.at[:, piece(peers[k - 1])], pieces.at[k - 1], send_a.at[k - 1], recv_a.at[k - 1], "cols", peers[k - 1]
        )
        copy.start()
        first.append(copy)
    value = partial[:, piece(me)]
    for k in range(1, n_cols):
        first[k - 1].wait_recv()
        value = value + pieces[k - 1]
    unit = eye((2 * RANK, 2 * RANK))
    bs = []
    for j in range(2):
        pair = value[:, 2 * LEAF * j : 2 * LEAF * (j + 1)]
        bs += [pair[:, :LEAF], swap_halves(pair)[:, :LEAF]]
    tiles = [dot_nt(b, jnp.concatenate([b, b, unit], axis=0)) for b in bs]
    collect, end = subtree(n_cols, tiles, [total_of(b * b) for b in bs], out, send_b, recv_b)
    for part in range(3):
        collect(part)
    for copy in first:
        copy.wait_send()
    end()


def leaf_tiles(far, sketch, n_cols):
    rows, columns = far.shape
    dma = pltpu.SemaphoreType.DMA
    return pl.pallas_call(
        functools.partial(leaf_body, n_cols),
        out_shape=jax.ShapeDtypeStruct((n_cols, 4, RANK, 4 * RANK), jnp.float32),
        in_specs=[whole, whole],
        out_specs=whole,
        scratch_shapes=[VMEM(far.shape, jnp.float32), VMEM((n_cols - 1, rows, columns // n_cols), jnp.float32)]
        + [dma((n_cols - 1,))] * 2
        + [dma((3, n_cols - 1))] * 2,
        compiler_params=pltpu.CompilerParams(collective_id=2, has_side_effects=True, vmem_limit_bytes=40 * MIB),
        name="leaf_tiles",
    )(far, sketch)


def unpack(block):
    return jnp.concatenate([pltpu.roll(block, (4 * RANK - RANK * g) % (4 * RANK), 1) for g in range(4)], axis=0)


def pack(source, shift):
    quarter = lanes((8, 4 * RANK)) // RANK
    row = jnp.zeros((8, 4 * RANK), jnp.float32)
    for g in range(4):
        turned = pltpu.roll(source[8 * g : 8 * g + 8], (RANK * g - shift) % (4 * RANK), 1)
        row = jnp.where(quarter == g, turned, row)
    return row


def project_t(tile, row):
    low = lanes(tile.shape) < LEAF
    high, rest = [part.astype(jnp.float32) for part in halves(tile)]
    r_high, r_rest = [part.astype(jnp.float32) for part in halves(row)]
    left = [jnp.where(low, swap_halves(rest), high), jnp.where(low, 0.0, high)]
    right = [jnp.where(low, swap_halves(r_high), r_high), r_rest]
    return dot_nt(
        jnp.concatenate(left, axis=1).astype(jnp.bfloat16), jnp.concatenate(right, axis=1).astype(jnp.bfloat16), None
    )


def both(pair):
    return [swap_halves(pair), pair]


def climb(tiles, owner, values):
    second = both(tiles[owner, 2])
    values = [project(second[i], jnp.concatenate(values[2 * i : 2 * i + 2], axis=0)) for i in range(2)]
    return project(tiles[owner, 3], jnp.concatenate(values, axis=0))


def finish(levels, values):
    for tiles in levels:
        values = [project(tile, jnp.concatenate(values[2 * i : 2 * i + 2], axis=0)) for i, tile in enumerate(tiles)]
    return values[0]


def tree_body(
    n_leaf, n_cols, tiles, far, branch, transfers, root,
    upper, chosen, packed_p, out_p,
    yc_send, yc_recv, zc_send, zc_recv, yp_send, yp_recv, zp_send, zp_recv, x_send, x_recv, own,
):
    n_y = ROWS_Y
    n_z = n_leaf // n_y
    seg = n_leaf // n_cols
    me, col = lax.axis_index("leaf"), lax.axis_index("cols")
    y, z = me // n_z, me % n_z
    across = [((y + k) % n_y) * n_z + z for k in range(1, n_y)]
    along = [y * n_z + (z + k) % n_z for k in range(1, n_z)]
    others = [(col + k) % n_cols for k in range(1, n_cols)]
    far_first = sorted(range(n_z - 1), key=lambda k: -min(k + 1, n_z - 1 - k))
    barrier = pltpu.get_barrier_semaphore()
    for peer in across + along:
        pl.semaphore_signal(barrier, inc=1, device_id={"leaf": peer}, device_id_type=MESH)
    for peer in others:
        pl.semaphore_signal(barrier, inc=1, device_id={"cols": peer}, device_id_type=MESH)

    levels = chain([tiles[c, 3] for c in range(n_cols)])
    packed_c = pack(levels[-1][0], RANK)

    values = []
    for c in range(n_cols):
        leaves = []
        for j in range(2):
            at = pl.ds((2 * c + j) * 2 * LEAF, 2 * LEAF)
            pair, rows = tiles[c, j], far[:, at]
            leaves += [project_t(q, row) for q, row in zip(both(pair), both(rows))]
        values.append(leaves)
    values = [climb(tiles, c, leaves) for c, leaves in enumerate(values)]
    pl.semaphore_wait(barrier, len(across) + len(along) + len(others))

    tree_y, tree_z = (col * seg) // n_z, (col * seg) % n_z
    slot = z % seg
    carries = z // seg == tree_z // seg
    starts = carries & (y == tree_y)

    def c_across(k):
        return descriptor(chosen.at[slot], chosen.at[slot], yc_send.at[k], yc_recv, "leaf", across[k])

    def c_along(k):
        return descriptor(chosen.at[slot], chosen.at[slot], zc_send.at[k], zc_recv.at[slot], "leaf", along[k])

    @pl.when(starts)
    def _():
        chosen[slot] = packed_c
        for k in range(n_y - 1):
            c_across(k).start()

    value = finish(levels, values)
    branch[...] = value
    packed_p[...] = pack(jnp.concatenate([value, jnp.zeros((RANK, 3 * RANK), jnp.float32)], axis=1), 0)

    p_across = [
        descriptor(packed_p, out_p.at[z, y], yp_send.at[k], yp_recv.at[k], "leaf", across[k]) for k in range(n_y - 1)
    ]
    for copy in p_across:
        copy.start()
    mine = pltpu.make_async_copy(packed_p, out_p.at[z, y], own)
    mine.start()

    @pl.when(carries & (y != tree_y))
    def _():
        c_across(0).wait_recv()

    @pl.when(carries)
    def _():
        for k in far_first:
            c_along(k).start()

    mine.wait()
    for k in range(n_y - 1):
        other = (y + n_y - k - 1) % n_y
        descriptor(packed_p, out_p.at[z, other], yp_send.at[k], yp_recv.at[k], "leaf", across[k]).wait_recv()
    p_along = [
        descriptor(out_p.at[z], out_p.at[z], zp_send.at[k], zp_recv.at[k], "leaf", along[k]) for k in range(n_z - 1)
    ]
    for k in far_first:
        p_along[k].start()

    for i in range(seg):

        @pl.when(tree_z + i != z)
        def _():
            descriptor(chosen.at[i], chosen.at[i], zc_send.at[i], zc_recv.at[i], "leaf", along[0]).wait_recv()

    pairs = [
        parent_tile(jnp.concatenate([unpack(chosen[2 * i]), unpack(chosen[2 * i + 1])], axis=0)) for i in range(seg // 2)
    ]
    collect, end = subtree(n_cols, [tile for tile, _ in pairs], [trace for _, trace in pairs], upper, x_send, x_recv)
    for part in (0, 1, 2):
        collect(part)
    for k in range(n_z - 1):
        other = (z + n_z - k - 1) % n_z
        descriptor(out_p.at[other], out_p.at[other], zp_send.at[k], zp_recv.at[k], "leaf", along[k]).wait_recv()

    def q_of(tile):
        return swap_halves(tile)[:, : 2 * RANK]

    levels = chain([upper[c, 3] for c in range(n_cols)])
    values = []
    for c in range(n_cols):
        nodes = []
        for j in range(2):
            for i, tile in enumerate(both(upper[c, j])):
                at = c * seg + 2 * (2 * j + i)
                children = [unpack(out_p[(at + d) % n_z, (at + d) // n_z]) for d in range(2)]
                nodes.append(project(tile, jnp.concatenate(children, axis=0)))
                transfers[4 * c + 2 * j + i] = q_of(tile)
        values.append(nodes)
        for i, tile in enumerate(both(upper[c, 2])):
            transfers[4 * n_cols + 2 * c + i] = q_of(tile)
        transfers[6 * n_cols + c] = q_of(upper[c, 3])
    values = [climb(upper, c, nodes) for c, nodes in enumerate(values)]
    first = 7 * n_cols
    for level_tiles in levels:
        for i, tile in enumerate(level_tiles):
            transfers[first + i] = q_of(tile)
        first += len(level_tiles)
    root[...] = finish(levels, values)[:, :RANK]

    @pl.when(starts)
    def _():
        for k in range(n_y - 1):
            c_across(k).wait_send()

    @pl.when(carries)
    def _():
        for k in range(n_z - 1):
            c_along(k).wait_send()

    for copy in p_across + p_along:
        copy.wait_send()
    end()


def tree(tiles, far, n_leaf, n_cols):
    n_z = n_leaf // ROWS_Y
    f32 = jnp.float32
    dma = pltpu.SemaphoreType.DMA
    return pl.pallas_call(
        functools.partial(tree_body, n_leaf, n_cols),
        out_shape=(
            jax.ShapeDtypeStruct((RANK, RANK), f32),
            jax.ShapeDtypeStruct((n_leaf - 1, RANK, 2 * RANK), f32),
            jax.ShapeDtypeStruct((RANK, RANK), f32),
        ),
        in_specs=[whole, whole],
        out_specs=(whole, whole, whole),
        scratch_shapes=[
            VMEM((n_cols, 4, RANK, 4 * RANK), f32),
            VMEM((n_leaf // n_cols, 8, 4 * RANK), f32),
            VMEM((8, 4 * RANK), f32),
            VMEM((n_z, ROWS_Y, 8, 4 * RANK), f32),
            dma((ROWS_Y - 1,)),
            dma,
            dma((n_z - 1,)),
            dma((n_leaf // n_cols,)),
            dma((ROWS_Y - 1,)),
            dma((ROWS_Y - 1,)),
            dma((n_z - 1,)),
            dma((n_z - 1,)),
            dma((3, n_cols - 1)),
            dma((3, n_cols - 1)),
            dma,
        ],
        compiler_params=pltpu.CompilerParams(
            collective_id=3, has_side_effects=True, vmem_limit_bytes=40 * MIB
        ),
        name="tree",
    )(tiles, far)


def results_body(tiles, branch, transfers, root, basis_out, branch_out, transfers_out, root_out):
    for c in range(tiles.shape[0]):
        for j in range(2):
            basis_out[:, pl.ds((2 * c + j) * 2 * LEAF, 2 * LEAF)] = tiles[c, j]
    branch_out[...] = branch[...]
    transfers_out[...] = transfers[...]
    root_out[...] = root[...]


def results(tiles, branch, transfers, root):
    f32 = jnp.float32
    return pl.pallas_call(
        results_body,
        out_shape=(
            jax.ShapeDtypeStruct((RANK, 4 * tiles.shape[0] * LEAF), f32),
            jax.ShapeDtypeStruct(branch.shape, f32),
            jax.ShapeDtypeStruct(transfers.shape, f32),
            jax.ShapeDtypeStruct(root.shape, f32),
        ),
        in_specs=[whole] * 4,
        out_specs=(whole,) * 4,
        compiler_params=pltpu.CompilerParams(vmem_limit_bytes=40 * MIB),
        name="results",
    )(tiles, branch, transfers, root)


def on_device(n_leaf, n_cols, points, samples, sketch, far_requests, far_slots, far_count, near_mask):
    table = jnp.zeros((32, 2 * LEAF), jnp.int32)
    for row, block in ((0, far_requests[0].T), (SLOT_ROW, far_slots.T), (MASK_ROW, near_mask.T), (COUNT_ROW, far_count[None])):
        table += jnp.pad(block, ((row, 32 - row - block.shape[0]), (0, 2 * LEAF - block.shape[1])))
    recv, close, columns = fetch(samples, points, table, n_leaf)
    far_sample, near_sample, far_again = sample(recv, close, columns, table, n_leaf)
    tiles = leaf_tiles(far_again, sketch, n_cols)
    branch_samples, top_transfer, root_sample = tree(tiles, far_again, n_leaf, n_cols)
    leaf_basis, branch_samples, top_transfer, root_sample = results(tiles, branch_samples, top_transfer, root_sample)
    return far_sample, near_sample, leaf_basis, branch_samples, jnp.swapaxes(top_transfer, 1, 2), root_sample


def solution(mesh):
    return jax.shard_map(
        functools.partial(on_device, mesh.shape["leaf"], mesh.shape["cols"]),
        mesh=mesh,
        in_specs=(
            P(None, "leaf"),
            P("cols", "leaf"),
            P(None, "cols"),
            P("leaf", None, None),
            P("leaf", None),
            P("leaf"),
            P("leaf", None),
        ),
        out_specs=(
            P("cols", "leaf"),
            P("cols", "leaf"),
            P(None, "leaf"),
            P("leaf", "cols"),
            P(),
            P(None, "cols"),
        ),
        check_vma=False,
    )
```
